32 devices in a mesh: dp: 4 (over z), blk: 8 (over y, x, core).
Axes of the slice: x: 2, y: 2, z: 4, core: 2. Of those that a mesh axis runs over, the one named last changes fastest.
Arguments:
- inputs: bfloat16 [16, 1024, 1024], P('dp', 'blk'), may hold values from -6 to 6
- mask_pos: int32 [16, 307], P('dp'), may hold values from 0 to 1023, as said below
- mask_count: int32 [16], P('dp'), may hold values from 51 to 307, as said below
- replace: bfloat16 [16, 307, 1024], P('dp'), may hold values from -6 to 6
- cotangent: bfloat16 [16, 307, 1024], P('dp'), may hold values from -6 to 6
- query_weight: bfloat16 [1024, 1024], replicated, may hold values from -0.1875 to 0.1875
- query_bias: bfloat16 [1024], replicated, may hold values from -3 to 3
- key_weight: bfloat16 [1024, 1024], replicated, may hold values from -0.1875 to 0.1875
- value_weight: bfloat16 [1024, 1024], replicated, may hold values from -0.1875 to 0.1875
- value_bias: bfloat16 [1024], replicated, may hold values from -3 to 3
- out_weight: bfloat16 [1024, 1024], replicated, may hold values from -0.375 to 0.375
- out_bias: bfloat16 [1024], replicated, may hold values from -3 to 3
- first_gain: bfloat16 [1024], replicated, may hold values from 0.099609375 to 1.8984375
- first_shift: bfloat16 [1024], replicated, may hold values from -3 to 3
- inner_weight: bfloat16 [1024, 4096], replicated, may hold values from -0.1875 to 0.1875
- inner_bias: bfloat16 [4096], replicated, may hold values from -3 to 3
- outer_weight: bfloat16 [4096, 1024], replicated, may hold values from -0.09375 to 0.09375
- outer_bias: bfloat16 [1024], replicated, may hold values from -3 to 3
- second_gain: bfloat16 [1024], replicated, may hold values from 0.099609375 to 1.8984375
- second_shift: bfloat16 [1024], replicated, may hold values from -3 to 3
Outputs:
- layer_out: float32 [16, 1024, 1024], P('dp', 'blk')
- input_grad: float32 [16, 1024, 1024], P('dp', 'blk')
- query_weight_grad: float32 [1024, 1024], P(('dp', 'blk'))
- query_bias_grad: float32 [1024], P(('dp', 'blk'))
- key_weight_grad: float32 [1024, 1024], P(('dp', 'blk'))
- value_weight_grad: float32 [1024, 1024], P(('dp', 'blk'))
- value_bias_grad: float32 [1024], P(('dp', 'blk'))
- out_weight_grad: float32 [1024, 1024], P(('dp', 'blk'))
- out_bias_grad: float32 [1024], P(('dp', 'blk'))
- first_gain_grad: float32 [1024], P(('dp', 'blk'))
- first_shift_grad: float32 [1024], P(('dp', 'blk'))
- inner_weight_grad: float32 [1024, 4096], P(('dp', 'blk'))
- inner_bias_grad: float32 [4096], P(('dp', 'blk'))
- outer_weight_grad: float32 [4096, 1024], P(('dp', 'blk'))
- outer_bias_grad: float32 [1024], P(('dp', 'blk'))
- second_gain_grad: float32 [1024], P(('dp', 'blk'))
- second_shift_grad: float32 [1024], P(('dp', 'blk'))
The draws below stay inside these ranges and needn't reach their ends.
Inputs may be any that keep to these rules, and one draw needn't show every extreme that they name: `mask_pos`: row s lists distinct positions of sequence s; only its first mask_count[s] slots are in use. `mask_count`: slots in use of each sequence's list; some sequence uses all 307.
All inputs are finite; a program needn't handle non-finite values.
Results may differ from the reference program's by a relative error of at most 0.018.
Values may be sent and summed in bfloat16 or wider, within the bound.
No kernel may reach another device: no remote copies, remote signals or barrier semaphores. Data moves between devices by JAX's collectives and lax.ppermute only.
A program may use at most 320 MiB of HBM per device.

```python
import math
import jax
import jax.numpy as jnp
from jax import lax

D = 1024
HEADS = 16
HEAD = 64
FF = 4096
LEN = 1024
SEQS = 16
MAXM = 307


def draw_mask_pos(key, part):
    key = jax.random.fold_in(key, 11)
    seq_keys = jax.random.split(key, SEQS)

    def one_row(row_key):
        return jax.random.permutation(row_key, LEN)[:MAXM]
    return jax.vmap(one_row)(seq_keys).astype(jnp.int32)


def draw_mask_count(key, part):
    key = jax.random.fold_in(key, 23)
    key_one, key_two = jax.random.split(key)
    counts = jax.random.randint(key_one, (SEQS,), LEN // 20, MAXM + 1)
    chosen = jax.random.randint(key_two, (), 0, SEQS)
    return jnp.where(jnp.arange(SEQS) == chosen, MAXM, counts).astype(jnp.int32)


def block_levels(key, dims, pieces, least, high):
    factor_of, own = 1.0, jax.random.fold_in(key, 6)
    for position, parts in pieces:
        steps = jnp.exp(jax.random.uniform(jax.random.fold_in(own, position), (parts,), jnp.float32, least / len(pieces), high / len(pieces)))
        factor_of = factor_of * jnp.repeat(steps, dims[position] // parts).reshape([-1 if axis == position else 1 for axis in range(len(dims))])
    return factor_of


def centred(own_key, dims, width, limit, cuts=(), kind=jnp.bfloat16):
    level = block_levels(own_key, dims, cuts, -0.22, 0.18) if cuts else 1.0
    values = jax.random.normal(own_key, dims, jnp.float32) * width * level
    return jnp.minimum(jnp.maximum(values, -limit), limit).astype(kind)


def setup_inputs(seed: int = 0) -> dict:
    streams_of = jax.random.split(jax.random.key(seed), 21)
    inputs = centred(streams_of[0], (SEQS, LEN, D), 1.0, 6.0, ((0, 4), (1, 8)))
    mask_pos = draw_mask_pos(jax.random.fold_in(streams_of[20], 71), 0)
    mask_count = draw_mask_count(jax.random.fold_in(streams_of[20], 71), 0)
    replace = centred(streams_of[3], (SEQS, MAXM, D), 1.0, 6.0, ((0, 4),))
    cotangent = centred(streams_of[4], (SEQS, MAXM, D), 1.0, 6.0, ((0, 4),))
    query_weight = centred(streams_of[5], (D, D), D ** -0.5, 0.1875)
    query_bias = centred(streams_of[6], (D,), 0.5, 3.0)
    key_weight = centred(streams_of[7], (D, D), D ** -0.5, 0.1875)
    value_weight = centred(streams_of[8], (D, D), D ** -0.5, 0.1875)
    value_bias = centred(streams_of[9], (D,), 0.5, 3.0)
    out_weight = centred(streams_of[10], (D, D), (D // 4) ** -0.5, 0.375)
    out_bias = centred(streams_of[11], (D,), 0.5, 3.0)
    first_gain = jnp.clip(1.0 + 0.18 * jax.random.normal(streams_of[12], (D,), jnp.float32), 0.099609375, 1.8984375).astype(jnp.bfloat16)
    first_shift = centred(streams_of[13], (D,), 0.5, 3.0)
    inner_weight = centred(streams_of[14], (D, FF), D ** -0.5, 0.1875)
    inner_bias = centred(streams_of[15], (FF,), 0.5, 3.0)
    outer_weight = centred(streams_of[16], (FF, D), FF ** -0.5, 0.09375)
    outer_bias = centred(streams_of[17], (D,), 0.5, 3.0)
    second_gain = jnp.clip(1.0 + 0.18 * jax.random.normal(streams_of[18], (D,), jnp.float32), 0.099609375, 1.8984375).astype(jnp.bfloat16)
    second_shift = centred(streams_of[19], (D,), 0.5, 3.0)
    return dict(inputs=inputs, mask_pos=mask_pos, mask_count=mask_count, replace=replace, cotangent=cotangent, query_weight=query_weight, query_bias=query_bias, key_weight=key_weight, value_weight=value_weight, value_bias=value_bias, out_weight=out_weight, out_bias=out_bias, first_gain=first_gain, first_shift=first_shift, inner_weight=inner_weight, inner_bias=inner_bias, outer_weight=outer_weight, outer_bias=outer_bias, second_gain=second_gain, second_shift=second_shift)


EPSILON = 1e-05

@jax.custom_vjp
def low(v):
    return lax.optimization_barrier(v.astype(jnp.bfloat16)).astype(jnp.float32)

@jax.custom_vjp
def low_back(v):
    return v

def low_keep(v):
    return (low(v), None)

def low_pass(kept, grad):
    return (grad,)

def back_keep(v):
    return (v, None)

def back_low(kept, grad):
    return (low(grad),)
low.defvjp(low_keep, low_pass)
low_back.defvjp(back_keep, back_low)

def layer_norm(hidden, gain, shift):
    center = hidden - lax.optimization_barrier(jnp.mean(hidden, axis=-1, keepdims=True))
    spread = lax.optimization_barrier(jnp.mean(center * center, axis=-1, keepdims=True))
    return center * lax.rsqrt(spread + EPSILON) * gain + shift

def product(left, right):
    return jnp.dot(left, right, precision=lax.Precision.HIGHEST)

def one_sequence(params, row_in, positions, count, fresh):
    query_weight, query_bias, key_weight, value_weight, value_bias, out_weight, out_bias, first_gain, first_shift, inner_weight, inner_bias, outer_weight, outer_bias, second_gain, second_shift = params
    live_slot = jnp.arange(MAXM, dtype=jnp.int32) < count
    target = jnp.where(live_slot, positions, LEN).astype(jnp.int32)
    current = row_in.at[target].set(fresh, mode='drop')
    query = low(low_back(product(current, query_weight) + query_bias))
    keys = low(low_back(product(current, key_weight)))
    values = low(low_back(product(current, value_weight) + value_bias))
    query_heads = query.reshape(LEN, HEADS, HEAD)
    key_heads = keys.reshape(LEN, HEADS, HEAD)
    value_heads = values.reshape(LEN, HEADS, HEAD)
    raw_scores = jnp.einsum('qhc,khc->hqk', query_heads, key_heads, precision=lax.Precision.HIGHEST)
    scores = low_back(raw_scores) * (1.0 / math.sqrt(HEAD))
    highest = lax.optimization_barrier(jnp.max(scores, axis=-1, keepdims=True))
    expon = jnp.exp(scores - highest)
    shares = expon / lax.optimization_barrier(jnp.sum(expon, axis=-1, keepdims=True))
    mixed = jnp.einsum('hqk,khc->qhc', low(shares), value_heads, precision=lax.Precision.HIGHEST)
    mixed = low(low_back(mixed.reshape(LEN, D)))
    summed_one = current + low_back(product(mixed, out_weight)) + out_bias
    first = layer_norm(summed_one, first_gain, first_shift)
    inner = low_back(product(low(first), inner_weight)) + inner_bias
    active = low(jax.nn.gelu(inner, approximate=False))
    summed_two = first + low_back(product(active, outer_weight)) + outer_bias
    return layer_norm(summed_two, second_gain, second_shift)

def reference(inputs, mask_pos, mask_count, replace, cotangent, query_weight, query_bias, key_weight, value_weight, value_bias, out_weight, out_bias, first_gain, first_shift, inner_weight, inner_bias, outer_weight, outer_bias, second_gain, second_shift):
    params = tuple((w.astype(jnp.float32) for w in (query_weight, query_bias, key_weight, value_weight, value_bias, out_weight, out_bias, first_gain, first_shift, inner_weight, inner_bias, outer_weight, outer_bias, second_gain, second_shift)))
    fresh_rows = replace.astype(jnp.float32)
    checked = jax.checkpoint(one_sequence)

    def forward(weights, rows_in):

        def step(carry, item):
            row_in, positions, count, fresh = item
            return (carry, checked(weights, row_in, positions, count, fresh))
        _, outs = lax.scan(step, jnp.zeros((), jnp.float32), (rows_in, mask_pos, mask_count, fresh_rows))
        return outs
    result, pull = jax.vjp(forward, params, inputs.astype(jnp.float32))

    def spread_rows(positions, count, rows):
        live_slot = jnp.arange(MAXM, dtype=jnp.int32) < count
        target = jnp.where(live_slot, positions, LEN).astype(jnp.int32)
        return jnp.zeros((LEN, D), jnp.float32).at[target].set(rows, mode='drop')
    seeded = jax.vmap(spread_rows)(mask_pos, mask_count, cotangent.astype(jnp.float32))
    grads, input_grad = pull(seeded)
    g_query, g_query_bias, g_key, g_value, g_value_bias, g_out, g_out_bias, g_first_gain, g_first_shift, g_inner, g_inner_bias, g_outer, g_outer_bias, g_second_gain, g_second_shift = grads
    return (result, input_grad, g_query, g_query_bias, g_key, g_value, g_value_bias, g_out, g_out_bias, g_first_gain, g_first_shift, g_inner, g_inner_bias, g_outer, g_outer_bias, g_second_gain, g_second_shift)
```

```python
import math

import jax
import jax.numpy as jnp
from jax import lax
from jax.sharding import PartitionSpec as P

HEAD = 64
EPSILON = 1e-05
BOTH = ("dp", "blk")
LOW = jnp.bfloat16
FULL = jnp.float32


def product(left, right):
    return jnp.dot(left, right, preferred_element_type=FULL)


def left_product(left, right):
    return lax.dot_general(left, right, (((0,), (0,)), ((), ())), preferred_element_type=FULL)


def right_product(left, right):
    return lax.dot_general(left, right, (((1,), (1,)), ((), ())), preferred_element_type=FULL)


def norm_stats(hidden):
    center = hidden - jnp.mean(hidden, axis=-1, keepdims=True)
    spread = jnp.mean(center * center, axis=-1, keepdims=True)
    factor = lax.rsqrt(spread + EPSILON)
    return center * factor, factor


def norm_pull(unit, factor, gain, grad):
    scaled = grad * gain
    inner = jnp.mean(scaled, axis=-1, keepdims=True)
    along = jnp.mean(scaled * unit, axis=-1, keepdims=True)
    return factor * (scaled - inner - unit * along)


def gelu_parts(inner):
    half = 0.5 * (1.0 + lax.erf(inner * (1.0 / math.sqrt(2.0))))
    slope = half + inner * jnp.exp(-0.5 * inner * inner) * (1.0 / math.sqrt(2.0 * math.pi))
    return inner * half, slope


def attention_forward(query, key, value):
    rows, width = query.shape
    heads = width // HEAD

    def split(a):
        return jnp.transpose(a.reshape(rows, heads, HEAD), (1, 0, 2))

    scores = jnp.einsum("hqc,hkc->hqk", split(query), split(key), preferred_element_type=FULL)
    scores = scores * (1.0 / math.sqrt(HEAD))
    highest = jnp.max(scores, axis=-1, keepdims=True)
    expon = jnp.exp(scores - highest)
    total = jnp.sum(expon, axis=-1, keepdims=True)
    shares = (expon / total).astype(LOW)
    mixed = jnp.einsum("hqk,hkc->hqc", shares, split(value), preferred_element_type=FULL)
    mixed = jnp.transpose(mixed, (1, 0, 2)).reshape(rows, width).astype(LOW)
    return mixed, highest + jnp.log(total)


def attention_backward(query, key, value, mixed, grad_mixed, log_total):
    rows, width = query.shape
    heads = width // HEAD

    def split(a):
        return jnp.transpose(a.reshape(rows, heads, HEAD), (1, 0, 2))

    def join(a):
        return jnp.transpose(a, (1, 0, 2)).reshape(rows, width).astype(LOW)

    query, key, value, mixed, grad = map(split, (query, key, value, mixed, grad_mixed))
    scale = 1.0 / math.sqrt(HEAD)
    scores = jnp.einsum("hqc,hkc->hqk", query, key, preferred_element_type=FULL) * scale
    shares = jnp.exp(scores - log_total)
    grad_shares = jnp.einsum("hqc,hkc->hqk", grad, value, preferred_element_type=FULL)
    delta = jnp.sum(grad.astype(FULL) * mixed.astype(FULL), axis=-1, keepdims=True)
    grad_scores = (shares * (grad_shares - delta) * scale).astype(LOW)
    query_grad = jnp.einsum("hqk,hkc->hqc", grad_scores, key, preferred_element_type=FULL)
    key_grad = jnp.einsum("hqk,hqc->hkc", grad_scores, query, preferred_element_type=FULL)
    value_grad = jnp.einsum("hqk,hqc->hkc", shares.astype(LOW), grad, preferred_element_type=FULL)
    return join(query_grad), join(key_grad), join(value_grad)


def per_device(
    inputs,
    mask_pos,
    mask_count,
    replace,
    cotangent,
    query_weight,
    query_bias,
    key_weight,
    value_weight,
    value_bias,
    out_weight,
    out_bias,
    first_gain,
    first_shift,
    inner_weight,
    inner_bias,
    outer_weight,
    outer_bias,
    second_gain,
    second_shift,
):
    groups, rows, width = inputs.shape
    hidden = inner_weight.shape[1]
    slots = mask_pos.shape[1]
    blocks = lax.axis_size("blk")
    number = lax.axis_size("dp") * blocks
    size = blocks // groups
    piece = rows // size
    own_rows = blocks * piece
    teams = number // size
    bits = teams.bit_length() - 1
    place = lax.axis_index("blk")
    flat = lax.axis_index("dp") * blocks + place
    sequence = place // size
    rank = place % size
    team = flat // size
    share = width // size
    hidden_share = hidden // size

    def hop(array, mask):
        return lax.ppermute(array, BOTH, [(i, i ^ mask) for i in range(number)])

    def gather(array):
        return jnp.concatenate([array] + [hop(array, k) for k in range(1, size)], axis=0)

    def columns(array, who, count):
        return lax.dynamic_slice_in_dim(array, who * count, count, axis=1)

    def absolute(pieces, axis):
        stacked = jnp.stack(pieces)
        return jnp.concatenate(
            [lax.dynamic_index_in_dim(stacked, q ^ rank, 0, keepdims=False) for q in range(size)],
            axis=axis,
        )

    def scatter_part(array, order):
        array = array.reshape((2,) * bits + array.shape[1:])
        left = list(range(bits))[::-1]
        for step, bit in enumerate(order):
            axis = left.index(bit)
            mine = (team >> bit) & 1
            away = lax.dynamic_index_in_dim(array, 1 - mine, axis, keepdims=False)
            keep = lax.dynamic_index_in_dim(array, mine, axis, keepdims=False)
            came = hop(away, size << bit)
            array = keep.astype(FULL) + came.astype(FULL)
            if step < bits - 1:
                array = array.astype(LOW)
            left.remove(bit)
        return array

    rest = list(range(3, bits))
    orders = ([0, 1, 2] + rest, [1, 2, 0] + rest, [2, 0, 1] + rest)

    def scatter(array):
        array = array.astype(LOW)
        wide = array.shape[-1]
        unit = wide // 8
        cuts = (0, 3 * unit, 6 * unit, wide)
        return jnp.concatenate(
            [
                scatter_part(array[..., cuts[k] : cuts[k + 1]], orders[k])
                for k in range(3)
            ],
            axis=-1,
        )

    def settle(array):
        lines = array.shape[0] // size
        array = array.reshape(size, lines, array.shape[1])
        parts = []
        for k in range(size):
            part = lax.dynamic_index_in_dim(array, rank ^ k, 0, keepdims=False)
            parts.append(hop(part, k) if k else part)
        return parts

    arrived = lax.all_to_all(inputs.reshape(blocks, piece, width), "blk", 0, 0)
    arrived = arrived.reshape(own_rows, width)
    lane = jnp.arange(own_rows, dtype=jnp.int32)
    places = (lane // piece) * rows + rank * piece + lane % piece
    my_pos = lax.dynamic_index_in_dim(mask_pos, sequence, 0, keepdims=False)
    my_count = lax.dynamic_index_in_dim(mask_count, sequence, 0, keepdims=False)
    live = jnp.arange(slots, dtype=jnp.int32) < my_count
    matches = (my_pos[None, :] == places[:, None]) & live[None, :]
    select = matches.astype(LOW)
    masked = jnp.any(matches, axis=1)[:, None]
    fresh = lax.dynamic_index_in_dim(replace, sequence, 0, keepdims=False)
    pulled = lax.dynamic_index_in_dim(cotangent, sequence, 0, keepdims=False)
    swapped = product(select, fresh).astype(LOW)
    seeded = product(select, pulled)
    current = jnp.where(masked, swapped, arrived)
    current_all = gather(current)

    heads_weight = jnp.concatenate(
        [columns(w, rank, share) for w in (query_weight, key_weight, value_weight)], axis=1
    )
    heads_bias = jnp.concatenate(
        [
            lax.dynamic_slice_in_dim(query_bias, rank * share, share),
            jnp.zeros((share,), LOW),
            lax.dynamic_slice_in_dim(value_bias, rank * share, share),
        ]
    )
    joined = (product(current_all, heads_weight) + heads_bias.astype(FULL)).astype(LOW)
    query, key, value = (joined[:, k * share : (k + 1) * share] for k in range(3))
    mixed_heads, log_total = attention_forward(query, key, value)

    mixed_parts = mixed_heads.reshape(size, own_rows, share)
    mixed = absolute([mixed_parts[0]] + [hop(mixed_parts[k], k) for k in range(1, size)], 1)
    mixed_all = gather(mixed)

    gain_one = first_gain.astype(FULL)
    gain_two = second_gain.astype(FULL)
    summed_one = current.astype(FULL) + product(mixed, out_weight) + out_bias.astype(FULL)
    unit_one, factor_one = norm_stats(summed_one)
    first = unit_one * gain_one + first_shift.astype(FULL)
    first_low = first.astype(LOW)
    first_all = gather(first_low)
    inner = product(first_low, inner_weight) + inner_bias.astype(FULL)
    active, slope = gelu_parts(inner)
    active = active.astype(LOW)
    active_split = active.reshape(own_rows, teams, size, hidden // number)

    def active_of(who):
        return lax.dynamic_index_in_dim(active_split, who, 2, keepdims=False)

    active_all = jnp.concatenate(
        [active_of(rank)] + [hop(active_of(rank ^ k), k) for k in range(1, size)], axis=0
    ).reshape(size * own_rows, hidden_share)
    summed_two = first + product(active, outer_weight) + outer_bias.astype(FULL)
    unit_two, factor_two = norm_stats(summed_two)
    result = unit_two * gain_two + second_shift.astype(FULL)

    def home(array):
        array = array.astype(LOW).reshape(blocks, piece, width)
        array = lax.all_to_all(array, "blk", 0, 0)
        return array.reshape(groups, rows, width).astype(FULL)

    layer_out = home(result)
    second_gain_grad = jnp.sum(seeded * unit_two, axis=0)
    second_shift_grad = jnp.sum(seeded, axis=0)
    grad_two = norm_pull(unit_two, factor_two, gain_two, seeded)
    outer_bias_grad = jnp.sum(grad_two, axis=0)
    grad_two_low = grad_two.astype(LOW)
    grad_two_all = gather(grad_two_low)
    outer_weight_grad = left_product(active_all, grad_two_all)
    outer_weight_grad = scatter(outer_weight_grad.reshape(teams, hidden // number, width))

    grad_inner = slope * right_product(grad_two_low, outer_weight)
    inner_bias_grad = jnp.sum(grad_inner, axis=0)
    grad_inner_low = grad_inner.astype(LOW)
    grad_inner_all = jnp.concatenate(
        [columns(grad_inner_low, rank, hidden_share)]
        + [hop(columns(grad_inner_low, rank ^ k, hidden_share), k) for k in range(1, size)],
        axis=0,
    )
    inner_weight_grad = left_product(first_all, grad_inner_all)
    inner_weight_grad = scatter(inner_weight_grad.reshape(teams, width // teams, hidden_share))

    grad_first = grad_two + right_product(grad_inner_low, inner_weight)
    first_gain_grad = jnp.sum(grad_first * unit_one, axis=0)
    first_shift_grad = jnp.sum(grad_first, axis=0)
    grad_one = norm_pull(unit_one, factor_one, gain_one, grad_first)
    out_bias_grad = jnp.sum(grad_one, axis=0)
    grad_one_low = grad_one.astype(LOW)
    grad_one_all = jnp.concatenate(
        [columns(grad_one_low, rank, share)]
        + [hop(columns(grad_one_low, rank ^ k, share), k) for k in range(1, size)],
        axis=0,
    )
    out_weight_grad = left_product(mixed_all, grad_one_all)
    grad_mixed = right_product(grad_one_low, out_weight).astype(LOW)
    grad_mixed_heads = jnp.concatenate(
        [columns(grad_mixed, rank, share)]
        + [hop(columns(grad_mixed, rank ^ k, share), k) for k in range(1, size)],
        axis=0,
    )
    query_grad, key_grad, value_grad = attention_backward(
        query, key, value, mixed_heads, grad_mixed_heads, log_total
    )
    joined_grad = jnp.concatenate([query_grad, key_grad, value_grad], axis=1)
    joined_weight_grad = left_product(current_all, joined_grad)
    four_grad = jnp.concatenate([joined_weight_grad, out_weight_grad], axis=1)
    four_grad = scatter(four_grad.reshape(teams, width // teams, 4 * share))

    back = right_product(joined_grad, heads_weight).reshape(size, own_rows, width)
    input_grad = grad_one + back[0]
    for k in range(1, size):
        input_grad = input_grad + hop(back[k].astype(LOW), k).astype(FULL)
    input_grad = home(jnp.where(masked, 0.0, input_grad))

    def spot(array):
        return lax.dynamic_update_slice_in_dim(jnp.zeros((width,), FULL), array, rank * share, 0)

    query_bias_grad = spot(jnp.sum(query_grad.astype(FULL), axis=0))
    value_bias_grad = spot(jnp.sum(value_grad.astype(FULL), axis=0))
    vectors = (
        query_bias_grad,
        value_bias_grad,
        out_bias_grad,
        first_gain_grad,
        first_shift_grad,
        inner_bias_grad,
        outer_bias_grad,
        second_gain_grad,
        second_shift_grad,
    )
    lines = jnp.concatenate([v.reshape(number, 1, -1) for v in vectors], axis=2)
    lines = jnp.sum(lax.all_to_all(lines, BOTH, 0, 0), axis=(0, 1))
    spots, start = [], 0
    for v in vectors:
        spots.append(lines[start : start + v.shape[0] // number])
        start += v.shape[0] // number

    inner_weight_grad = absolute(settle(inner_weight_grad), 1)
    four = absolute([p.reshape(width // number, 4, share) for p in settle(four_grad)], 2)
    return (
        layer_out,
        input_grad,
        four[:, 0],
        spots[0],
        four[:, 1],
        four[:, 2],
        spots[1],
        four[:, 3],
        spots[2],
        spots[3],
        spots[4],
        inner_weight_grad,
        spots[5],
        outer_weight_grad,
        spots[6],
        spots[7],
        spots[8],
    )


def solution(mesh):
    split = P("dp", "blk", None)
    row = P("dp")
    both = P(BOTH)
    in_specs = (split, row, row, row, row) + (P(),) * 15
    out_specs = (split, split) + (both,) * 15
    return jax.shard_map(
        per_device, mesh=mesh, in_specs=in_specs, out_specs=out_specs, check_vma=False
    )
```

```python
import functools
import math

import jax
import jax.numpy as jnp
from jax import lax
from jax.experimental import pallas as pl
from jax.experimental.pallas import tpu as pltpu
from jax.sharding import PartitionSpec as P

HEAD = 64
EPSILON = 1e-05
BOTH = ("dp", "blk")
LOW = jnp.bfloat16
FULL = jnp.float32
CHUNK = 256
CHEAP = pl.CostEstimate(flops=1, bytes_accessed=1, transcendentals=0)


def product(left, right):
    return jnp.dot(left, right, preferred_element_type=FULL)


def right_product(left, right):
    return lax.dot_general(left, right, (((1,), (1,)), ((), ())), preferred_element_type=FULL)


def norm_stats(hidden):
    center = hidden - jnp.mean(hidden, axis=-1, keepdims=True)
    spread = jnp.mean(center * center, axis=-1, keepdims=True)
    factor = lax.rsqrt(spread + EPSILON)
    return center * factor, factor


def norm_pull(unit, factor, gain, grad):
    scaled = grad * gain
    inner = jnp.mean(scaled, axis=-1, keepdims=True)
    along = jnp.mean(scaled * unit, axis=-1, keepdims=True)
    return factor * (scaled - inner - unit * along)


def column_sum(array):
    return jnp.sum(array, axis=0, keepdims=True)


def gelu_parts(inner):
    bell = jnp.exp(-0.5 * inner * inner)
    t = 1.0 / (1.0 + (0.3275911 * math.sqrt(0.5)) * jnp.abs(inner))
    poly = 0.5 * 1.061405429
    for c in (-1.453152027, 1.421413741, -0.284496736, 0.254829592):
        poly = poly * t + 0.5 * c
    tail = poly * t * bell
    below = jnp.where(inner >= 0.0, 1.0 - tail, tail)
    return inner * below, below + inner * bell * (1.0 / math.sqrt(2.0 * math.pi))


def params(mib=56):
    return pltpu.CompilerParams(vmem_limit_bytes=mib << 20)


def forward_kernel(query_ref, key_ref, value_ref, mixed_ref, log_ref):
    lane = lax.broadcasted_iota(jnp.int32, (1, 2 * HEAD), 1)
    query = query_ref[...] * LOW(1.0 / math.sqrt(HEAD))
    key = key_ref[...]
    value_t = value_ref[...].T
    outs = []
    for head in range(2):
        mine = (lane < HEAD) if head == 0 else (lane >= HEAD)
        scores = right_product(key, jnp.where(mine, query, LOW(0)))
        highest = jnp.max(scores, axis=0, keepdims=True)
        expon = jnp.exp(scores - highest)
        total = jnp.sum(expon, axis=0, keepdims=True)
        out = product(value_t[head * HEAD : (head + 1) * HEAD], expon.astype(LOW))
        outs.append(out * (1.0 / total))
        log_ref[0, head : head + 1, :] = highest + jnp.log(total)
    mixed_ref[...] = jnp.concatenate(outs, axis=0).T.astype(LOW)


def backward_kernel(
    members, query_ref, key_ref, value_ref, mixed_ref, log_ref, *refs
):
    grads = refs[:members]
    out_ref, key_sum, value_sum = refs[-3:]
    step = pl.program_id(1)

    @pl.when(step == 0)
    def _():
        key_sum[...] = jnp.zeros_like(key_sum)
        value_sum[...] = jnp.zeros_like(value_sum)

    scale = 1.0 / math.sqrt(HEAD)
    lane = lax.broadcasted_iota(jnp.int32, (1, 2 * HEAD), 1)
    query = query_ref[...] * LOW(scale)
    key = key_ref[...]
    value = value_ref[...]
    grad = grads[0][...]
    for k in range(1, members):
        grad = jnp.where(step == k, grads[k][...], grad)
    tile = query.shape[0]
    both = (grad.astype(FULL) * mixed_ref[...].astype(FULL)).T
    key_t = key.T
    outs = []
    for head in range(2):
        mine = (lane < HEAD) if head == 0 else (lane >= HEAD)
        own = slice(head * HEAD, (head + 1) * HEAD)
        delta = jnp.sum(both[own], axis=0, keepdims=True)
        query_one = jnp.where(mine, query, LOW(0))
        grad_one = jnp.where(mine, grad, LOW(0))
        shares = jnp.exp(right_product(key, query_one) - log_ref[0, head : head + 1, :])
        grad_shares = right_product(value, grad_one)
        grad_scores = (shares * (grad_shares - delta)).astype(LOW)
        value_sum[...] += product(shares.astype(LOW), grad_one)
        key_sum[...] += product(grad_scores, query_one)
        outs.append(product(key_t[own], grad_scores))
    spot = pl.ds(pl.multiple_of(step * tile, tile), tile)
    out_ref[0, spot, :] = (jnp.concatenate(outs, axis=0).T * scale).astype(LOW)

    @pl.when(step == pl.num_programs(1) - 1)
    def _():
        out_ref[1] = key_sum[...].astype(LOW)
        out_ref[2] = value_sum[...].astype(LOW)


def attention_forward(joined):
    rows, wide = joined.shape
    share = wide // 3
    pairs = share // (2 * HEAD)
    tile = min(512, rows)

    def whole(offset):
        return pl.BlockSpec((rows, 2 * HEAD), lambda p, i: (0, offset + p))

    line = pl.BlockSpec((tile, 2 * HEAD), lambda p, i: (i, p))
    return pl.pallas_call(
        forward_kernel,
        grid=(pairs, rows // tile),
        in_specs=[line, whole(pairs), whole(2 * pairs)],
        out_specs=[line, pl.BlockSpec((1, 2, tile), lambda p, i: (p, 0, i))],
        out_shape=[
            jax.ShapeDtypeStruct((rows, share), LOW),
            jax.ShapeDtypeStruct((pairs, 2, rows), FULL),
        ],
        compiler_params=pltpu.CompilerParams(vmem_limit_bytes=48 << 20),
        cost_estimate=CHEAP,
        name="attention_forward",
    )(joined, joined, joined)


def attention_backward(joined, grad_mixed, mixed, log_total, first, count, previous=None):
    rows, wide = joined.shape
    share = wide // 3
    pairs = share // (2 * HEAD)
    members = len(grad_mixed)
    tile = rows // members

    def whole(offset):
        return pl.BlockSpec((rows, 2 * HEAD), lambda p, i: (0, offset + p))

    line = pl.BlockSpec((tile, 2 * HEAD), lambda p, i: (i, first + p))
    grad_line = pl.BlockSpec((tile, 2 * HEAD), lambda p, i: (0, first + p))
    more = [] if previous is None else [previous]
    return pl.pallas_call(
        functools.partial(backward_kernel, members),
        grid=(count, rows // tile),
        in_specs=[
            line,
            whole(pairs + first),
            whole(2 * pairs + first),
            line,
            pl.BlockSpec((1, 2, tile), lambda p, i: (first + p, 0, i)),
        ]
        + [grad_line] * members
        + [pl.BlockSpec(memory_space=pl.ANY)] * len(more),
        out_specs=pl.BlockSpec((3, rows, 2 * HEAD), lambda p, i: (0, 0, first + p)),
        out_shape=jax.ShapeDtypeStruct((3, rows, share), LOW),
        input_output_aliases={5 + members: 0} if more else {},
        scratch_shapes=[pltpu.VMEM((rows, 2 * HEAD), FULL)] * 2,
        compiler_params=params(48),
        cost_estimate=CHEAP,
        name="attention_backward",
    )(joined, joined, joined, mixed, log_total, *grad_mixed, *more)


def first_kernel(pieces, current_ref, bias_ref, gain_ref, shift_ref, *refs):
    mixed, weights = refs[:pieces], refs[pieces : 2 * pieces]
    first_ref, flip_ref, low_ref, unit_ref, factor_ref = refs[2 * pieces :]
    total = current_ref[...].astype(FULL) + bias_ref[...].astype(FULL)
    for part, weight in zip(mixed, weights):
        total = total + product(part[...], weight[...])
    unit, factor = norm_stats(total)
    first = unit * gain_ref[...].astype(FULL) + shift_ref[...].astype(FULL)
    first_ref[...] = first
    low = first.astype(LOW)
    low_ref[...] = low
    flip_ref[...] = low.T
    unit_ref[...] = unit
    factor_ref[...] = factor


def first_half(current, mixed, weights, bias, gain, shift):
    rows, width = current.shape
    tile = 128
    pieces = len(mixed)
    line = pl.BlockSpec((tile, width), lambda i: (i, 0))
    flat = pl.BlockSpec((1, width), lambda i: (0, 0))
    return pl.pallas_call(
        functools.partial(first_kernel, pieces),
        grid=(rows // tile,),
        in_specs=[line, flat, flat, flat]
        + [pl.BlockSpec((tile, block_width), lambda i: (i, 0)) for _, block_width in mixed]
        + [pl.BlockSpec(w.shape, lambda i: (0, 0)) for w in weights],
        out_specs=[
            line,
            pl.BlockSpec((width, tile), lambda i: (0, i)),
            line,
            line,
            pl.BlockSpec((tile, 1), lambda i: (i, 0)),
        ],
        out_shape=[
            jax.ShapeDtypeStruct((rows, width), FULL),
            jax.ShapeDtypeStruct((width, rows), LOW),
            jax.ShapeDtypeStruct((rows, width), LOW),
            jax.ShapeDtypeStruct((rows, width), FULL),
            jax.ShapeDtypeStruct((rows, 1), FULL),
        ],
        compiler_params=params(48),
        cost_estimate=CHEAP,
        name="first_half",
    )(current, bias, gain, shift, *[m for m, _ in mixed], *weights)


def feed_kernel(
    size, unit_rows, place_ref, low_ref, first_ref, seed_ref, inner_ref, inner_bias_ref, outer_ref,
    outer_bias_ref, gain_ref, shift_ref, *refs,
):
    actives = refs[:size]
    slope_ref, result_ref, grad_ref, grad_low_ref, sums_ref, acc, flip = refs[size:]
    step = pl.program_id(0)
    inner = product(low_ref[...], inner_ref[...]) + inner_bias_ref[...].astype(FULL)
    active, slope = gelu_parts(inner)
    active = active.astype(LOW)
    slope_ref[...] = slope.astype(LOW)
    flip[...] = active.T
    rank = place_ref[1]
    tile = flip.shape[0]
    for k in range(size):
        for q in range(tile // (unit_rows * size)):
            line = pl.multiple_of((q * size + (rank ^ k)) * unit_rows, 16)
            actives[k][q * unit_rows : (q + 1) * unit_rows, :] = flip[pl.ds(line, unit_rows), :]
    part = product(active, outer_ref[...])

    @pl.when(step == 0)
    def _():
        acc[...] = part

    @pl.when(step > 0)
    def _():
        acc[...] += part

    @pl.when(step == pl.num_programs(0) - 1)
    def _():
        gain = gain_ref[...].astype(FULL)
        total = first_ref[...] + acc[...] + outer_bias_ref[...].astype(FULL)
        unit, factor = norm_stats(total)
        result_ref[...] = (unit * gain + shift_ref[...].astype(FULL)).astype(LOW)
        seed = seed_ref[...].astype(FULL)
        sums_ref[0:1, :] = column_sum(seed * unit)
        sums_ref[1:2, :] = column_sum(seed)
        grad = norm_pull(unit, factor, gain, seed)
        sums_ref[2:3, :] = column_sum(grad)
        grad_ref[...] = grad
        grad_low_ref[...] = grad.astype(LOW)


def feed_forward(places, size, number, low, first, seeded, inner_weight, inner_bias, outer_weight, outer_bias, gain, shift):
    rows, width = low.shape
    hidden = inner_weight.shape[1]
    tile = 512
    whole = pl.BlockSpec((rows, width), lambda i, s: (0, 0))
    flat = pl.BlockSpec((1, width), lambda i, s: (0, 0))
    across = pl.BlockSpec((rows, tile), lambda i, s: (0, i))
    return pl.pallas_call(
        functools.partial(feed_kernel, size, hidden // number),
        grid_spec=pltpu.PrefetchScalarGridSpec(
            num_scalar_prefetch=1,
            grid=(hidden // tile,),
            in_specs=[
                whole,
                whole,
                whole,
                pl.BlockSpec((width, tile), lambda i, s: (0, i)),
                pl.BlockSpec((1, tile), lambda i, s: (0, i)),
                pl.BlockSpec((tile, width), lambda i, s: (i, 0)),
                flat,
                flat,
                flat,
            ],
            out_specs=[pl.BlockSpec((tile // size, rows), lambda i, s: (i, 0))] * size
            + [across, whole, whole, whole, pl.BlockSpec((8, width), lambda i, s: (0, 0))],
            scratch_shapes=[pltpu.VMEM((rows, width), FULL), pltpu.VMEM((tile, rows), LOW)],
        ),
        out_shape=[jax.ShapeDtypeStruct((hidden // size, rows), LOW)] * size
        + [
            jax.ShapeDtypeStruct((rows, hidden), LOW),
            jax.ShapeDtypeStruct((rows, width), LOW),
            jax.ShapeDtypeStruct((rows, width), FULL),
            jax.ShapeDtypeStruct((rows, width), LOW),
            jax.ShapeDtypeStruct((8, width), FULL),
        ],
        compiler_params=params(),
        cost_estimate=CHEAP,
        name="feed_forward",
    )(places, low, first, seeded, inner_weight, inner_bias, outer_weight, outer_bias, gain, shift)


def feed_back_kernel(
    size, steps, share, place_ref, grad_low_ref, grad_ref, slope_ref, inner_ref, outer_ref, unit_ref,
    factor_ref, gain_ref, *refs,
):
    out_weights, refs = refs[:size], refs[size:]
    inners = refs[:size]
    bias_ref, one_ref, low_ref, sums_ref = refs[size : size + 4]
    cuts = refs[size + 4 : 2 * size + 4]
    mixes = refs[2 * size + 4 : 3 * size + 4]
    acc, keep = refs[3 * size + 4 :]
    step = pl.program_id(0)
    grad_inner = slope_ref[...].astype(FULL) * right_product(grad_low_ref[...], outer_ref[...])
    bias_ref[...] = column_sum(grad_inner)
    grad_inner = grad_inner.astype(LOW)
    for k in range(size):

        @pl.when(step // steps == (k + size - 1) % size)
        def _():
            inners[k][...] = grad_inner

    part = right_product(grad_inner, inner_ref[...])

    @pl.when(step == 0)
    def _():
        acc[...] = part

    @pl.when(step > 0)
    def _():
        acc[...] += part

    @pl.when(step == pl.num_programs(0) - 1)
    def _():
        grad = grad_ref[...] + acc[...]
        unit = unit_ref[...]
        sums_ref[0:1, :] = column_sum(grad * unit)
        sums_ref[1:2, :] = column_sum(grad)
        one = norm_pull(unit, factor_ref[...], gain_ref[...].astype(FULL), grad)
        sums_ref[2:3, :] = column_sum(one)
        one_ref[...] = one
        low = one.astype(LOW)
        low_ref[...] = low
        keep[...] = low
        for k in range(size):
            spot = pl.multiple_of((place_ref[1] ^ k) * share, 128)
            cuts[k][...] = keep[:, pl.ds(spot, share)]
            mixes[k][...] = right_product(low, out_weights[k][...]).astype(LOW)


def feed_back(
    places, size, grad_low, grad, slope, inner_weight, outer_weight, unit, factor, gain, out_weights
):
    rows, width = grad_low.shape
    hidden = inner_weight.shape[1]
    part = hidden // size
    tile = min(512, part)
    steps = part // tile
    share = width // size

    def spot(i, s):
        return (s[1] ^ ((i // steps + 1) % size)) * steps + i % steps

    def own(k):
        start = ((k + size - 1) % size) * steps
        return pl.BlockSpec((rows, tile), lambda i, s: (0, jnp.clip(i - start, 0, steps - 1)))

    whole = pl.BlockSpec((rows, width), lambda i, s: (0, 0))
    return pl.pallas_call(
        functools.partial(feed_back_kernel, size, steps, share),
        grid_spec=pltpu.PrefetchScalarGridSpec(
            num_scalar_prefetch=1,
            grid=(hidden // tile,),
            in_specs=[
                whole,
                whole,
                pl.BlockSpec((rows, tile), lambda i, s: (0, spot(i, s))),
                pl.BlockSpec((width, tile), lambda i, s: (0, spot(i, s))),
                pl.BlockSpec((tile, width), lambda i, s: (spot(i, s), 0)),
                whole,
                pl.BlockSpec((rows, 1), lambda i, s: (0, 0)),
                pl.BlockSpec((1, width), lambda i, s: (0, 0)),
            ]
            + [pl.BlockSpec((share, width), lambda i, s: (0, 0))] * size,
            out_specs=[own(k) for k in range(size)]
            + [
                pl.BlockSpec((1, tile), lambda i, s: (0, spot(i, s))),
                whole,
                whole,
                pl.BlockSpec((8, width), lambda i, s: (0, 0)),
            ]
            + [pl.BlockSpec((rows, share), lambda i, s: (0, 0))] * (2 * size),
            scratch_shapes=[pltpu.VMEM((rows, width), FULL), pltpu.VMEM((rows, width), LOW)],
        ),
        out_shape=[jax.ShapeDtypeStruct((rows, part), LOW)] * size
        + [
            jax.ShapeDtypeStruct((1, hidden), FULL),
            jax.ShapeDtypeStruct((rows, width), FULL),
            jax.ShapeDtypeStruct((rows, width), LOW),
            jax.ShapeDtypeStruct((8, width), FULL),
        ]
        + [jax.ShapeDtypeStruct((rows, share), LOW)] * (2 * size),
        compiler_params=params(),
        cost_estimate=CHEAP,
        name="feed_back",
    )(places, grad_low, grad, slope, inner_weight, outer_weight, unit, factor, gain, *out_weights)


def back_kernel(size, three_ref, weight_ref, *refs):
    step = pl.program_id(0)
    share = three_ref.shape[2]
    total = right_product(three_ref[0], weight_ref[:, 0:share])
    for k in range(1, 3):
        total = total + right_product(three_ref[k], weight_ref[:, k * share : (k + 1) * share])
    steps = pl.num_programs(0) // size
    for k in range(size):

        @pl.when(step // steps == (k + size - 1) % size)
        def _():
            refs[k][...] = total.astype(refs[k].dtype)


def input_back(three, weight, size):
    _, rows, share = three.shape
    width = weight.shape[0]
    own_rows = rows // size
    tile = 256
    steps = own_rows // tile

    def spot(i):
        return ((i // steps + 1) % size) * steps + i % steps

    def own(k):
        start = ((k + size - 1) % size) * steps
        return pl.BlockSpec((tile, width), lambda i: (jnp.clip(i - start, 0, steps - 1), 0))

    return pl.pallas_call(
        functools.partial(back_kernel, size),
        grid=(rows // tile,),
        in_specs=[
            pl.BlockSpec((3, tile, share), lambda i: (0, spot(i), 0)),
            pl.BlockSpec(weight.shape, lambda i: (0, 0)),
        ],
        out_specs=[own(k) for k in range(size)],
        out_shape=[
            jax.ShapeDtypeStruct((own_rows, width), LOW if k else FULL) for k in range(size)
        ],
        compiler_params=params(),
        cost_estimate=CHEAP,
        name="input_back",
    )(three, weight)


def join_kernel(grad_ref, own_ref, masked_ref, *refs):
    total = grad_ref[...] + own_ref[...]
    for ref in refs[:-1]:
        total = total + ref[...].astype(FULL)
    refs[-1][...] = jnp.where(masked_ref[...] > 0.0, 0.0, total).astype(LOW)


def input_join(grad, own, masked, came):
    rows, width = grad.shape
    tile = 128
    line = pl.BlockSpec((tile, width), lambda i: (i, 0))
    return pl.pallas_call(
        join_kernel,
        grid=(rows // tile,),
        in_specs=[line, line, pl.BlockSpec((tile, 1), lambda i: (i, 0))] + [line] * len(came),
        out_specs=line,
        out_shape=jax.ShapeDtypeStruct((rows, width), LOW),
        compiler_params=params(),
        cost_estimate=CHEAP,
        name="input_join",
    )(grad, own, masked, *came)


def part_orders(bits):
    if bits < 3:
        return [(list(range(bits)),) * 2] * 2
    rest = list(range(3, bits))
    return [([0, 2, 1] + rest, [1, 0, 2] + rest), ([2, 1, 0] + rest,) * 2]


def part_depths(lines, weights):
    tiles = lines // 16
    first = round(tiles * weights[0] / sum(weights))
    return [16 * first, 16 * (tiles - first)]


def offset_at(position, order):
    return sum(((position >> (len(order) - 1 - n)) & 1) << order[n] for n in range(len(order)))


def weight_kernel(layout, flips, teams, lines, parts, members, bias, place_ref, *refs):
    number = sum(layout)
    lefts, rights = refs[:number], refs[number : number + members]
    count = 2 * len(parts)
    outs = refs[number + members : number + members + count]
    scratch = refs[number + members + count :]
    flipped = scratch[:members] if flips else lefts
    total = scratch[members if flips else 0]
    step = pl.program_id(0)
    team = place_ref[0]
    half = teams // 2

    def block_at(position, order):
        even, odd = (offset_at(position, o) for o in order)
        return team ^ (even if even == odd else jnp.where(place_ref[1] % 2 == 0, even, odd))

    if flips:

        @pl.when(step == 0)
        def _():
            spot = 0
            for member in range(members):
                start = 0
                for _ in range(layout[member]):
                    wide = lefts[spot].shape[1]
                    flipped[member][start : start + wide, :] = lefts[spot][...].T
                    start, spot = start + wide, spot + 1

    def right(member):
        ref = rights[member]
        return ref[0] if len(ref.shape) == 3 else ref[...]

    def multiply():
        acc = product(flipped[0][...], right(0))
        for member in range(1, members):
            acc = acc + product(flipped[member][...], right(member))
        total[...] = acc.astype(LOW)
        for k, (order, start, deep) in enumerate(parts):
            for position in range(teams):
                line = pl.multiple_of(block_at(position, order) * lines + start, 16)
                outs[2 * k + position // half][position % half, 0] = total[pl.ds(line, deep), :]

    if not bias:
        multiply()
        return

    sums, vectors = scratch[-2:]
    chunks = pl.num_programs(0) - 1

    @pl.when(step < chunks)
    def _():
        multiply()
        sums[pl.ds(step, 1), :] = sum(column_sum(right(m).astype(FULL)) for m in range(members))

    @pl.when(step == chunks)
    def _():
        own = vectors.shape[0]
        for k, first in enumerate(bias[0]):
            for team_row in range(own):
                chunk, lane = divmod(first + team_row * lines, CHUNK)
                vectors[team_row : team_row + 1, k * lines : (k + 1) * lines] = sums[
                    chunk : chunk + 1, lane : lane + lines
                ]
        order = parts[-1][0]
        wide = vectors.shape[1]
        for position in range(teams):
            local = block_at(position, order) - place_ref[1] * (teams // members) - bias[1]
            inside = jnp.logical_and(local >= 0, local < own)
            row = vectors[pl.ds(jnp.clip(local, 0, own - 1), 1), :]
            row = jnp.where(inside, row, 0.0)
            outs[count - 2 + position // half][position % half, 0, 0:16, 0:wide] = jnp.broadcast_to(
                row, (16, wide)
            ).astype(LOW)


def weight_grad(name, lefts, flips, rights, places, teams, width, weights, bias=()):
    members = len(lefts)
    rows = rights[0][1][-2]
    flat = [item for member in lefts for item in member]
    high = sum(a.shape[1] for a, _ in lefts[0]) if flips else lefts[0][0][0].shape[0]
    lines = high // teams
    orders = part_orders(teams.bit_length() - 1)
    parts, start = [], 0
    for order, deep in zip(orders, part_depths(lines, weights)):
        if deep:
            parts.append((order, start, deep))
        start += deep
    half = teams // 2
    chunks = width // CHUNK
    own = bias[2] if bias else 0
    counts = [chunks] * len(parts)
    if bias:
        counts[-1] += 1
    outs = pl.pallas_call(
        functools.partial(
            weight_kernel, [len(m) for m in lefts], flips, teams, lines, parts, members, bias
        ),
        grid_spec=pltpu.PrefetchScalarGridSpec(
            num_scalar_prefetch=1,
            grid=(counts[-1],),
            in_specs=[
                pl.BlockSpec(
                    (rows, array.shape[1]) if flips else array.shape, lambda i, s, b=block: (b, 0)
                )
                for array, block in flat
            ]
            + [
                pl.BlockSpec(shape, lambda i, s, f=index: f(jnp.minimum(i, chunks - 1), s))
                for _, shape, index in rights
            ],
            out_specs=[
                pl.BlockSpec(
                    (half, 1, p[2], CHUNK), lambda i, s, c=c: (0, jnp.minimum(i, c - 1), 0, 0)
                )
                for p, c in zip(parts, counts)
                for _ in range(2)
            ],
            scratch_shapes=[pltpu.VMEM((high, rows), LOW)] * (members if flips else 0)
            + [pltpu.VMEM((high, CHUNK), LOW)]
            + (
                [pltpu.VMEM((chunks, CHUNK), FULL), pltpu.VMEM((own, len(bias[0]) * lines), FULL)]
                if bias
                else []
            ),
        ),
        out_shape=[
            jax.ShapeDtypeStruct((half, c, p[2], CHUNK), LOW)
            for p, c in zip(parts, counts)
            for _ in range(2)
        ],
        compiler_params=params(),
        cost_estimate=CHEAP,
        name="weight_grad",
    )(places, *[array for array, _ in flat], *[array for array, _, _ in rights])
    made = []
    for k, (order, start, deep) in enumerate(parts):
        near, far = (o.reshape(half, counts[k] * deep, CHUNK) for o in outs[2 * k : 2 * k + 2])
        segments = [(name, start, deep, c) for c in range(chunks)]
        if counts[k] > chunks:
            segments.append(("bias", 0, deep, 0))
        made.append(dict(order=order, near=near, far=far, segments=segments))
    return made


def fold_kernel(counts, *refs):
    total = 4 * sum(counts)
    outs = refs[total:]
    spot = 0
    for k, count in enumerate(counts):
        start = 0
        for _ in range(count):
            near_low, near_high, came_low, came_high = refs[spot : spot + 4]
            deep = near_low.shape[1]
            rows = slice(start, start + deep)
            outs[2 * k][:, rows] = (near_low[...].astype(FULL) + came_low[...].astype(FULL)).astype(LOW)
            outs[2 * k + 1][:, rows] = (
                near_high[...].astype(FULL) + came_high[...].astype(FULL)
            ).astype(LOW)
            start, spot = start + deep, spot + 4


def fold(*groups):
    orders = []
    for group in groups:
        for part in group:
            if part["order"] not in orders:
                orders.append(part["order"])
    merged = [[p for g in groups for p in g if p["order"] == order] for order in orders]
    half = merged[0][0]["near"].shape[0] // 2
    operands, in_specs, out_specs, out_shape, counts = [], [], [], [], []
    for parts in merged:
        rows = 0
        for part in parts:
            deep = part["near"].shape[1]
            rows += deep
            low = pl.BlockSpec((1, deep, CHUNK), lambda i: (i, 0, 0))
            high = pl.BlockSpec((1, deep, CHUNK), lambda i: (half + i, 0, 0))
            operands += [part["near"], part["near"], part["came"], part["came"]]
            in_specs += [low, high, low, high]
        counts.append(len(parts))
        out_specs += [pl.BlockSpec((1, rows, CHUNK), lambda i: (i, 0, 0))] * 2
        out_shape += [jax.ShapeDtypeStruct((half, rows, CHUNK), LOW)] * 2
    outs = pl.pallas_call(
        functools.partial(fold_kernel, counts),
        grid=(half,),
        in_specs=in_specs,
        out_specs=out_specs,
        out_shape=out_shape,
        compiler_params=params(60),
        cost_estimate=CHEAP,
        name="fold",
    )(*operands)
    return [
        dict(
            order=tuple(o[1:] for o in parts[0]["order"]),
            near=outs[2 * k],
            far=outs[2 * k + 1],
            segments=[s for p in parts for s in p["segments"]],
        )
        for k, parts in enumerate(merged)
    ]


def final_kernel(layouts, plain, settled, size, lines, place_ref, *refs):
    count = len(layouts)
    outs = refs[2 * count :]
    targets = dict(zip(plain, outs))
    pieces = outs[len(plain) : len(plain) + size]
    if settled:
        targets[None] = outs[-1]
    biases = []
    for k, layout in enumerate(layouts):
        spot = 0
        for name, start, deep, column in layout:
            rows = slice(spot, spot + (16 if name == "bias" else deep))
            value = refs[2 * k][0, rows].astype(FULL) + refs[2 * k + 1][0, rows].astype(FULL)
            spot += deep
            if name == "bias":
                biases.append(value[0:8])
                continue
            targets[name][start : start + deep, column * CHUNK : (column + 1) * CHUNK] = value
    if settled:
        for piece in pieces if biases else ():
            piece[lines : lines + 8, 0:CHUNK] = sum(biases)
        for k in range(size):
            line = pl.multiple_of((place_ref[1] ^ k) * lines, 8)
            pieces[k][0:lines, :] = targets[None][pl.ds(line, lines), :]


def final(parts, places, size, lines, plain, settled):
    layouts, wide, more = [], 0, 0
    for part in parts:
        layout = []
        for name, start, deep, column in part["segments"]:
            if name in plain or name == "bias":
                more = 8 if name == "bias" else more
                layout.append((name, start, deep, column))
            else:
                column += settled[name] // CHUNK
                wide = max(wide, (column + 1) * CHUNK)
                layout.append((None, start, deep, column))
        layouts.append(layout)
    names = list(plain)
    shapes = [jax.ShapeDtypeStruct(plain[n], FULL) for n in names]
    if settled:
        shapes += [jax.ShapeDtypeStruct((lines + more, wide), FULL)] * size
    outs = pl.pallas_call(
        functools.partial(final_kernel, layouts, names, bool(settled), size, lines),
        in_specs=[pl.BlockSpec(memory_space=pltpu.SMEM)]
        + [pl.BlockSpec(memory_space=pltpu.VMEM)] * (2 * len(parts)),
        out_specs=[pl.BlockSpec(memory_space=pltpu.VMEM)] * len(shapes),
        out_shape=shapes,
        scratch_shapes=[pltpu.VMEM((size * lines, wide), FULL)] if settled else [],
        compiler_params=params(32),
        cost_estimate=CHEAP,
        name="final",
    )(places, *[p[n] for p in parts for n in ("near", "came")])
    return dict(zip(names, outs)), outs[len(names) :]


def tie(value, *others):
    return lax.optimization_barrier((value, others))[0]


def per_device(
    inputs,
    mask_pos,
    mask_count,
    replace,
    cotangent,
    query_weight,
    query_bias,
    key_weight,
    value_weight,
    value_bias,
    out_weight,
    out_bias,
    first_gain,
    first_shift,
    inner_weight,
    inner_bias,
    outer_weight,
    outer_bias,
    second_gain,
    second_shift,
):
    groups, rows, width = inputs.shape
    hidden = inner_weight.shape[1]
    slots = mask_pos.shape[1]
    blocks = lax.axis_size("blk")
    number = lax.axis_size("dp") * blocks
    size = blocks // groups
    piece = rows // size
    own_rows = blocks * piece
    teams = number // size
    bits = teams.bit_length() - 1
    place = lax.axis_index("blk")
    flat = lax.axis_index("dp") * blocks + place
    sequence = place // size
    rank = place % size
    team = flat // size
    share = width // size
    hidden_share = hidden // size
    others = range(1, size)

    def hop(array, mask):
        return lax.ppermute(array, BOTH, [(i, i ^ mask) for i in range(number)])

    def cut(array, who, count, axis):
        return lax.dynamic_slice_in_dim(array, who * count, count, axis=axis)

    def swap(make):
        return [make(rank)] + [hop(make(rank ^ k), k) for k in others]

    def absolute(pieces, axis):
        if size == 2:
            first = rank == 0
            return jnp.concatenate(
                [jnp.where(first, pieces[0], pieces[1]), jnp.where(first, pieces[1], pieces[0])],
                axis=axis,
            )
        stacked = jnp.stack(pieces)
        return jnp.concatenate(
            [lax.dynamic_index_in_dim(stacked, q ^ rank, 0, keepdims=False) for q in range(size)],
            axis=axis,
        )

    def send(parts):
        return [
            dict(
                p,
                came=lax.ppermute(
                    p["far"],
                    BOTH,
                    [(i, i ^ (size << p["order"][i % size % 2][0])) for i in range(number)],
                ),
            )
            for p in parts
        ]

    def far(parts):
        return [p["far"] for p in parts]

    def sync(values, *groups):
        values, came = lax.optimization_barrier((values, [[p["came"] for p in g] for g in groups]))
        made = [[dict(p, came=c) for p, c in zip(g, cs)] for g, cs in zip(groups, came)]
        return (values, *made)

    def after(parts, *values):
        came = lax.optimization_barrier(([p["came"] for p in parts], values))[0]
        return [dict(p, came=c) for p, c in zip(parts, came)]

    def sum_vectors(vectors):
        lines = jnp.concatenate([v.reshape(number, 1, -1) for v in vectors], axis=2)
        return lax.all_to_all(lines, BOTH, 0, 0)

    def cut_vectors(lines, vectors):
        lines = jnp.sum(lines, axis=(0, 1))
        spots, start = [], 0
        for v in vectors:
            spots.append(lines[start : start + v.shape[0] // number])
            start += v.shape[0] // number
        return spots

    def line(vector):
        return vector.reshape(1, -1)

    arrived = lax.all_to_all(inputs.reshape(blocks, piece, width), "blk", 0, 0)
    lane = jnp.arange(own_rows, dtype=jnp.int32)
    positions = (lane // piece) * rows + rank * piece + lane % piece
    my_pos = lax.dynamic_index_in_dim(mask_pos, sequence, 0, keepdims=False)
    my_count = lax.dynamic_index_in_dim(mask_count, sequence, 0, keepdims=False)
    live = jnp.arange(slots, dtype=jnp.int32) < my_count
    matches = (my_pos[None, :] == positions[:, None]) & live[None, :]
    select = matches.astype(LOW)
    masked = jnp.any(matches, axis=1)[:, None]
    fresh = lax.dynamic_index_in_dim(replace, sequence, 0, keepdims=False)
    pulled = lax.dynamic_index_in_dim(cotangent, sequence, 0, keepdims=False)
    swapped = product(select, fresh).astype(LOW)
    seeded = product(select, pulled).astype(LOW)
    places = jnp.stack([team, rank]).astype(jnp.int32)
    heads_weight = jnp.concatenate(
        [cut(w, rank, share, 1) for w in (query_weight, key_weight, value_weight)], axis=1
    )
    heads_bias = jnp.concatenate(
        [
            cut(query_bias, rank, share, 0),
            jnp.zeros((share,), LOW),
            cut(value_bias, rank, share, 0),
        ]
    )
    out_weights = [cut(out_weight, rank ^ k, share, 0) for k in range(size)]

    arrived = tie(arrived, swapped, seeded, heads_weight, heads_bias, out_weights, masked)
    current = jnp.where(masked, swapped, arrived.reshape(own_rows, width))
    currents = [current] + [hop(current, k) for k in others]
    joined = product(jnp.concatenate(currents, axis=0), heads_weight) + heads_bias.astype(FULL)
    joined = joined.astype(LOW)
    mixed_heads, log_total = attention_forward(joined)

    mixed_parts = mixed_heads.reshape(size, own_rows, share)
    mixed_here = [mixed_parts[0]] + [hop(mixed_parts[k], k) for k in others]
    mixed_away = []
    for k in others:
        row = []
        for q in range(size):
            if q == 0:
                row.append((mixed_heads, k))
            else:
                row.append((hop(mixed_parts[k ^ q], q), 0))
        mixed_away.append(row)

    first, first_flip, first_low, unit_one, factor_one = first_half(
        current,
        [(m, share) for m in [mixed_heads] + mixed_here[1:]],
        out_weights,
        line(out_bias),
        line(first_gain),
        line(first_shift),
    )
    firsts = [first_flip] + [hop(first_flip, k) for k in others]
    fed = feed_forward(
        places, size, number, first_low, first, seeded, inner_weight, line(inner_bias),
        outer_weight, line(outer_bias), line(second_gain), line(second_shift),
    )
    actives = [fed[0]] + [hop(fed[k], k) for k in others]
    slope, result, grad_two, grad_two_low, second_sums = fed[size:]

    def home(array):
        return lax.all_to_all(array.reshape(blocks, piece, width), "blk", 0, 0)

    def wide(array):
        return array.reshape(groups, rows, width).astype(FULL)

    grad_twos = [grad_two_low] + [hop(grad_two_low, k) for k in others]

    def plain(array):
        return (array, (own_rows, CHUNK), lambda i, s: (0, i))

    layer_out = home(result)
    back = feed_back(
        places, size, grad_two_low, grad_two, slope, inner_weight, outer_weight, unit_one, factor_one,
        line(first_gain), out_weights,
    )
    (back, layer_out) = lax.optimization_barrier((back, layer_out))
    grad_twos[0] = tie(grad_two_low, back)
    layer_out = wide(layer_out)
    grad_inners = [back[0]] + [hop(back[k], k) for k in others]
    inner_bias_grad, grad_one, grad_one_low, first_sums = back[size : size + 4]
    grad_ones = [back[size + 4]] + [hop(back[size + 4 + k], k) for k in others]
    grad_mixed = back[2 * size + 4 : 3 * size + 4]
    grad_mixed = [grad_mixed[0]] + [hop(grad_mixed[k], k) for k in others]
    outer_parts = weight_grad(
        "outer", [[(a, 0)] for a in actives], False, [plain(g) for g in grad_twos], places, teams, width,
        (2, 1),
    )
    grad_inners[0] = tie(grad_inners[0], far(outer_parts))
    outer_parts = send(outer_parts)
    inner_parts = weight_grad(
        "inner", [[(f, 0)] for f in firsts], False, [plain(g) for g in grad_inners], places, teams,
        hidden_share, (3, 1),
    )
    grad_ones[0] = tie(grad_ones[0], far(inner_parts))
    inner_parts = send(inner_parts)
    out_parts = weight_grad(
        "out", [[(m, 0) for m in [mixed_heads] + mixed_here[1:]]] + mixed_away, True,
        [plain(g) for g in grad_ones],
        jnp.stack([team ^ (rank * (teams // size)), rank]).astype(jnp.int32), teams, share, (1, 0),
    )
    grad_mixed[0] = tie(grad_mixed[0], far(out_parts))
    out_parts = send(out_parts)
    vectors = (
        first_sums[2], first_sums[0], first_sums[1], inner_bias_grad[0], second_sums[2], second_sums[0],
        second_sums[1],
    )
    vector_lines = sum_vectors(vectors)

    pairs = share // (2 * HEAD)
    number_of = 2 if share // 2 % CHUNK == 0 else 1
    count = pairs // number_of
    part = share // number_of
    chunks = part // CHUNK
    team_rows = teams // size // number_of

    def three_grad(three, group):
        return weight_grad(
            f"three{group}", [[(c, 0)] for c in currents], True,
            [
                (
                    three,
                    (1, own_rows, CHUNK),
                    lambda i, s, k=k: (i // chunks, k, group * chunks + i % chunks),
                )
                for k in range(size)
            ],
            places, teams, 3 * part, (3, 1), ((0, 2 * part), group * team_rows, team_rows),
        )

    three = attention_backward(joined, grad_mixed, mixed_heads, log_total, 0, count)
    (three, vector_lines), outer_parts, inner_parts, out_parts = sync(
        (three, vector_lines), outer_parts, inner_parts, out_parts
    )
    early = fold(outer_parts, inner_parts, out_parts)
    three = tie(three, far(early))
    early = send(early)
    late = []
    if number_of == 2:
        late = three_grad(three, 0)
        three = tie(three, far(late))
        late = send(late)
        three = attention_backward(joined, grad_mixed, mixed_heads, log_total, count, count, three)
    three, early, late = sync(three, early, late)
    early = fold(early)
    three = tie(three, far(early))
    early = send(early)
    more = three_grad(three, number_of - 1)
    (three, _), early = sync((three, far(more)), early)
    more = send(more)
    early = fold(early)
    three = tie(three, far(early))
    early_one, early_two = send(early[:1]), early[1:]
    back = input_back(three, heads_weight, size)
    back_away = [hop(back[k], k) for k in others]
    input_grad = input_join(grad_one, back[0], masked.astype(FULL), back_away)
    home_grad = home(input_grad)
    _, more, early_one = sync(input_grad, more, early_one)
    late = fold(late, more) if late else fold(more)
    for p, f in zip(early_two, tie(far(early_two), far(late))):
        p["far"] = f
    late, early_two = send(late), send(early_two)
    while len((early_one + early_two)[0]["order"][0]) > 1:
        early_one, early_two = send(fold(early_one + early_two)), []

    lines = width // number
    _, late, early_two = sync(far(late), late, early_two)
    if len(late[0]["order"][0]) > 1:
        late = fold(late)
        early_one = [dict(p, near=tie(p["near"], far(late))) for p in early_one]
        home_grad = tie(home_grad, far(late))
        late = send(late)
    made, early = final(
        early_one + early_two, places, size, lines, {"outer": (hidden // number, width)},
        {"inner": 0, "out": hidden_share},
    )
    outer_weight_grad = made["outer"]
    early_away = [hop(early[k], k) for k in others]
    input_grad = wide(home_grad)
    late = after(late, input_grad, outer_weight_grad)
    while len(late[0]["order"][0]) > 1:
        late = fold(late)
        early_away = tie(early_away, far(late))
        late = send(late)
    early = [early[0]] + early_away
    inner_weight_grad = absolute([e[:, :hidden_share] for e in early], 1)
    out_weight_grad = absolute([e[:, hidden_share:] for e in early], 1)
    _, late = final(
        after(late, inner_weight_grad, out_weight_grad), places, size, lines, {},
        {f"three{g}": g * 3 * part for g in range(number_of)},
    )
    late = [late[0]] + [hop(late[k], k) for k in others]

    def three_columns(e, k):
        cuts = [
            e[:lines, (g * 3 + k) * part : (g * 3 + k + 1) * part] for g in range(number_of)
        ]
        return jnp.concatenate(cuts, axis=1)

    three_grads = [absolute([three_columns(e, k) for e in late], 1) for k in range(3)]
    team_lines = width // teams
    biases = sum(e[lines, : 2 * team_lines] for e in late).reshape(2, team_lines)
    biases = cut(biases, rank, lines, 1)
    spots = [biases[0], biases[1]] + cut_vectors(vector_lines, vectors)

    return (
        layer_out,
        input_grad,
        three_grads[0],
        spots[0],
        three_grads[1],
        three_grads[2],
        spots[1],
        out_weight_grad,
        spots[2],
        spots[3],
        spots[4],
        inner_weight_grad,
        spots[5],
        outer_weight_grad,
        spots[6],
        spots[7],
        spots[8],
    )


def solution(mesh):
    split = P("dp", "blk", None)
    row = P("dp")
    both = P(BOTH)
    in_specs = (split, row, row, row, row) + (P(),) * 15
    out_specs = (split, split) + (both,) * 15
    return jax.shard_map(
        per_device, mesh=mesh, in_specs=in_specs, out_specs=out_specs, check_vma=False
    )
```

```python
import functools
import math

import jax
import jax.numpy as jnp
from jax import lax
from jax.experimental import pallas as pl
from jax.experimental.pallas import tpu as pltpu
from jax.sharding import PartitionSpec as P

HEAD = 64
EPSILON = 1e-05
BOTH = ("dp", "blk")
LOW = jnp.bfloat16
FULL = jnp.float32
CHUNK = 256
CHEAP = pl.CostEstimate(flops=1, bytes_accessed=1, transcendentals=0)


def product(left, right):
    return jnp.dot(left, right, preferred_element_type=FULL)


def right_product(left, right):
    return lax.dot_general(left, right, (((1,), (1,)), ((), ())), preferred_element_type=FULL)


def norm_stats(hidden):
    center = hidden - jnp.mean(hidden, axis=-1, keepdims=True)
    spread = jnp.mean(center * center, axis=-1, keepdims=True)
    factor = lax.rsqrt(spread + EPSILON)
    return center * factor, factor


def norm_pull(unit, factor, gain, grad):
    scaled = grad * gain
    inner = jnp.mean(scaled, axis=-1, keepdims=True)
    along = jnp.mean(scaled * unit, axis=-1, keepdims=True)
    return factor * (scaled - inner - unit * along)


def column_sum(array):
    return jnp.sum(array, axis=0, keepdims=True)


def gelu_parts(inner):
    bell = jnp.exp(-0.5 * inner * inner)
    t = 1.0 / (1.0 + (0.3275911 * math.sqrt(0.5)) * jnp.abs(inner))
    poly = 0.5 * 1.061405429
    for c in (-1.453152027, 1.421413741, -0.284496736, 0.254829592):
        poly = poly * t + 0.5 * c
    tail = poly * t * bell
    below = jnp.where(inner >= 0.0, 1.0 - tail, tail)
    return inner * below, below + inner * bell * (1.0 / math.sqrt(2.0 * math.pi))


def params(mib=40):
    return pltpu.CompilerParams(vmem_limit_bytes=mib << 20)


def forward_kernel(query_ref, key_ref, value_ref, mixed_ref, log_ref):
    lane = lax.broadcasted_iota(jnp.int32, (1, 2 * HEAD), 1)
    query = query_ref[...] * LOW(1.0 / math.sqrt(HEAD))
    key = key_ref[...]
    value_t = value_ref[...].T
    outs = []
    for head in range(2):
        mine = (lane < HEAD) if head == 0 else (lane >= HEAD)
        scores = right_product(key, jnp.where(mine, query, LOW(0)))
        highest = jnp.max(scores, axis=0, keepdims=True)
        expon = jnp.exp(scores - highest)
        total = jnp.sum(expon, axis=0, keepdims=True)
        out = product(value_t[head * HEAD : (head + 1) * HEAD], expon.astype(LOW))
        outs.append(out * (1.0 / total))
        log_ref[0, head : head + 1, :] = highest + jnp.log(total)
    mixed_ref[...] = jnp.concatenate(outs, axis=0).T.astype(LOW)


def backward_kernel(
    members, query_ref, key_ref, value_ref, mixed_ref, log_ref, *refs
):
    grads = refs[:members]
    out_ref, key_sum, value_sum = refs[-3:]
    step = pl.program_id(1)

    @pl.when(step == 0)
    def _():
        key_sum[...] = jnp.zeros_like(key_sum)
        value_sum[...] = jnp.zeros_like(value_sum)

    scale = 1.0 / math.sqrt(HEAD)
    lane = lax.broadcasted_iota(jnp.int32, (1, 2 * HEAD), 1)
    query = query_ref[...] * LOW(scale)
    key = key_ref[...]
    value = value_ref[...]
    grad = grads[0][...]
    for k in range(1, members):
        grad = jnp.where(step == k, grads[k][...], grad)
    tile = query.shape[0]
    both = (grad.astype(FULL) * mixed_ref[...].astype(FULL)).T
    key_t = key.T
    outs = []
    for head in range(2):
        mine = (lane < HEAD) if head == 0 else (lane >= HEAD)
        own = slice(head * HEAD, (head + 1) * HEAD)
        delta = jnp.sum(both[own], axis=0, keepdims=True)
        query_one = jnp.where(mine, query, LOW(0))
        grad_one = jnp.where(mine, grad, LOW(0))
        shares = jnp.exp(right_product(key, query_one) - log_ref[0, head : head + 1, :])
        grad_shares = right_product(value, grad_one)
        grad_scores = (shares * (grad_shares - delta)).astype(LOW)
        value_sum[...] += product(shares.astype(LOW), grad_one)
        key_sum[...] += product(grad_scores, query_one)
        outs.append(product(key_t[own], grad_scores))
    spot = pl.ds(pl.multiple_of(step * tile, tile), tile)
    out_ref[0, spot, :] = (jnp.concatenate(outs, axis=0).T * scale).astype(LOW)

    @pl.when(step == pl.num_programs(1) - 1)
    def _():
        out_ref[1] = key_sum[...].astype(LOW)
        out_ref[2] = value_sum[...].astype(LOW)


def attention_forward(joined):
    rows, wide = joined.shape
    share = wide // 3
    pairs = share // (2 * HEAD)
    tile = min(512, rows)

    def whole(offset):
        return pl.BlockSpec((rows, 2 * HEAD), lambda p, i: (0, offset + p))

    line = pl.BlockSpec((tile, 2 * HEAD), lambda p, i: (i, p))
    return pl.pallas_call(
        forward_kernel,
        grid=(pairs, rows // tile),
        in_specs=[line, whole(pairs), whole(2 * pairs)],
        out_specs=[line, pl.BlockSpec((1, 2, tile), lambda p, i: (p, 0, i))],
        out_shape=[
            jax.ShapeDtypeStruct((rows, share), LOW),
            jax.ShapeDtypeStruct((pairs, 2, rows), FULL),
        ],
        compiler_params=params(48),
        cost_estimate=CHEAP,
        name="attention_forward",
    )(joined, joined, joined)


def attention_backward(joined, grad_mixed, mixed, log_total, first, count, previous=None):
    rows, wide = joined.shape
    share = wide // 3
    pairs = share // (2 * HEAD)
    members = len(grad_mixed)
    tile = rows // members

    def whole(offset):
        return pl.BlockSpec((rows, 2 * HEAD), lambda p, i: (0, offset + p))

    line = pl.BlockSpec((tile, 2 * HEAD), lambda p, i: (i, first + p))
    grad_line = pl.BlockSpec((tile, 2 * HEAD), lambda p, i: (0, first + p))
    more = [] if previous is None else [previous]
    return pl.pallas_call(
        functools.partial(backward_kernel, members),
        grid=(count, rows // tile),
        in_specs=[
            line,
            whole(pairs + first),
            whole(2 * pairs + first),
            line,
            pl.BlockSpec((1, 2, tile), lambda p, i: (first + p, 0, i)),
        ]
        + [grad_line] * members
        + [pl.BlockSpec(memory_space=pl.ANY)] * len(more),
        out_specs=pl.BlockSpec((3, rows, 2 * HEAD), lambda p, i: (0, 0, first + p)),
        out_shape=jax.ShapeDtypeStruct((3, rows, share), LOW),
        input_output_aliases={5 + members: 0} if more else {},
        scratch_shapes=[pltpu.VMEM((rows, 2 * HEAD), FULL)] * 2,
        compiler_params=params(48),
        cost_estimate=CHEAP,
        name="attention_backward",
    )(joined, joined, joined, mixed, log_total, *grad_mixed, *more)


def rows_kernel(sequence_ref, count_ref, position_ref, listed_ref, replace_ref, cotangent_ref, *refs):
    swapped_ref, seeded_ref, masked_ref = refs
    count = count_ref[sequence_ref[0]]
    listed = listed_ref[0]
    live = lax.broadcasted_iota(jnp.int32, listed.shape, 1) < count
    matches = jnp.where(live, listed, -1) == position_ref[...]
    select = matches.astype(FULL)
    masked_ref[...] = jnp.max(select, axis=1, keepdims=True)
    select = select.astype(LOW)
    swapped_ref[...] = product(select, replace_ref[0]).astype(LOW)
    seeded_ref[...] = product(select, cotangent_ref[0]).astype(LOW)


def masked_rows(sequence, mask_count, positions, mask_pos, replace, cotangent):
    rows = positions.shape[0]
    _, slots, width = replace.shape
    line = pl.BlockSpec((1, slots, width), lambda i, s, c: (s[0], 0, 0))
    return pl.pallas_call(
        rows_kernel,
        grid_spec=pltpu.PrefetchScalarGridSpec(
            num_scalar_prefetch=2,
            grid=(1,),
            in_specs=[
                pl.BlockSpec((rows, 1), lambda i, s, c: (0, 0)),
                pl.BlockSpec((1, 1, slots), lambda i, s, c: (s[0], 0, 0)),
                line,
                line,
            ],
            out_specs=[
                pl.BlockSpec((rows, width), lambda i, s, c: (0, 0)),
                pl.BlockSpec((rows, width), lambda i, s, c: (0, 0)),
                pl.BlockSpec((rows, 1), lambda i, s, c: (0, 0)),
            ],
        ),
        out_shape=[
            jax.ShapeDtypeStruct((rows, width), LOW),
            jax.ShapeDtypeStruct((rows, width), LOW),
            jax.ShapeDtypeStruct((rows, 1), FULL),
        ],
        compiler_params=params(),
        cost_estimate=CHEAP,
        name="masked_rows",
    )(sequence, mask_count, positions, mask_pos.reshape(-1, 1, slots), replace, cotangent)


def first_kernel(pieces, current_ref, bias_ref, gain_ref, shift_ref, *refs):
    mixed, weights = refs[:pieces], refs[pieces : 2 * pieces]
    first_ref, flip_ref, low_ref, unit_ref, factor_ref = refs[2 * pieces :]
    total = current_ref[...].astype(FULL) + bias_ref[...].astype(FULL)
    for part, weight in zip(mixed, weights):
        total = total + product(part[...], weight[...])
    unit, factor = norm_stats(total)
    first = unit * gain_ref[...].astype(FULL) + shift_ref[...].astype(FULL)
    first_ref[...] = first
    low = first.astype(LOW)
    low_ref[...] = low
    flip_ref[...] = low.T
    unit_ref[...] = unit
    factor_ref[...] = factor


def first_half(current, mixed, weights, bias, gain, shift):
    rows, width = current.shape
    tile = 128
    pieces = len(mixed)
    line = pl.BlockSpec((tile, width), lambda i: (i, 0))
    flat = pl.BlockSpec((1, width), lambda i: (0, 0))
    return pl.pallas_call(
        functools.partial(first_kernel, pieces),
        grid=(rows // tile,),
        in_specs=[line, flat, flat, flat]
        + [pl.BlockSpec((tile, block_width), lambda i: (i, 0)) for _, block_width in mixed]
        + [pl.BlockSpec(w.shape, lambda i: (0, 0)) for w in weights],
        out_specs=[
            line,
            pl.BlockSpec((width, tile), lambda i: (0, i)),
            line,
            line,
            pl.BlockSpec((tile, 1), lambda i: (i, 0)),
        ],
        out_shape=[
            jax.ShapeDtypeStruct((rows, width), FULL),
            jax.ShapeDtypeStruct((width, rows), LOW),
            jax.ShapeDtypeStruct((rows, width), LOW),
            jax.ShapeDtypeStruct((rows, width), FULL),
            jax.ShapeDtypeStruct((rows, 1), FULL),
        ],
        compiler_params=params(60),
        cost_estimate=CHEAP,
        name="first_half",
    )(current, bias, gain, shift, *[m for m, _ in mixed], *weights)


def feed_kernel(
    size, unit_rows, place_ref, low_ref, first_ref, seed_ref, inner_ref, inner_bias_ref, outer_ref,
    outer_bias_ref, gain_ref, shift_ref, *refs,
):
    actives = refs[:size]
    slope_ref, result_ref, grad_ref, grad_low_ref, sums_ref, acc, flip = refs[size:]
    step = pl.program_id(0)
    inner = product(low_ref[...], inner_ref[...]) + inner_bias_ref[...].astype(FULL)
    active, slope = gelu_parts(inner)
    active = active.astype(LOW)
    slope_ref[...] = slope.astype(LOW)
    flip[...] = active.T
    rank = place_ref[1]
    tile = flip.shape[0]
    for k in range(size):
        for q in range(tile // (unit_rows * size)):
            line = pl.multiple_of((q * size + (rank ^ k)) * unit_rows, 16)
            actives[k][q * unit_rows : (q + 1) * unit_rows, :] = flip[pl.ds(line, unit_rows), :]
    part = product(active, outer_ref[...])

    @pl.when(step == 0)
    def _():
        acc[...] = part

    @pl.when(step > 0)
    def _():
        acc[...] += part

    @pl.when(step == pl.num_programs(0) - 1)
    def _():
        gain = gain_ref[...].astype(FULL)
        total = first_ref[...] + acc[...] + outer_bias_ref[...].astype(FULL)
        unit, factor = norm_stats(total)
        result_ref[...] = (unit * gain + shift_ref[...].astype(FULL)).astype(LOW)
        seed = seed_ref[...].astype(FULL)
        sums_ref[0:1, :] = column_sum(seed * unit)
        sums_ref[1:2, :] = column_sum(seed)
        grad = norm_pull(unit, factor, gain, seed)
        sums_ref[2:3, :] = column_sum(grad)
        grad_ref[...] = grad
        grad_low_ref[...] = grad.astype(LOW)


def feed_forward(places, size, number, low, first, seeded, inner_weight, inner_bias, outer_weight, outer_bias, gain, shift):
    rows, width = low.shape
    hidden = inner_weight.shape[1]
    tile = 512
    whole = pl.BlockSpec((rows, width), lambda i, s: (0, 0))
    flat = pl.BlockSpec((1, width), lambda i, s: (0, 0))
    across = pl.BlockSpec((rows, tile), lambda i, s: (0, i))
    return pl.pallas_call(
        functools.partial(feed_kernel, size, hidden // number),
        grid_spec=pltpu.PrefetchScalarGridSpec(
            num_scalar_prefetch=1,
            grid=(hidden // tile,),
            in_specs=[
                whole,
                whole,
                whole,
                pl.BlockSpec((width, tile), lambda i, s: (0, i)),
                pl.BlockSpec((1, tile), lambda i, s: (0, i)),
                pl.BlockSpec((tile, width), lambda i, s: (i, 0)),
                flat,
                flat,
                flat,
            ],
            out_specs=[pl.BlockSpec((tile // size, rows), lambda i, s: (i, 0))] * size
            + [across, whole, whole, whole, pl.BlockSpec((8, width), lambda i, s: (0, 0))],
            scratch_shapes=[pltpu.VMEM((rows, width), FULL), pltpu.VMEM((tile, rows), LOW)],
        ),
        out_shape=[jax.ShapeDtypeStruct((hidden // size, rows), LOW)] * size
        + [
            jax.ShapeDtypeStruct((rows, hidden), LOW),
            jax.ShapeDtypeStruct((rows, width), LOW),
            jax.ShapeDtypeStruct((rows, width), FULL),
            jax.ShapeDtypeStruct((rows, width), LOW),
            jax.ShapeDtypeStruct((8, width), FULL),
        ],
        compiler_params=params(60),
        cost_estimate=CHEAP,
        name="feed_forward",
    )(places, low, first, seeded, inner_weight, inner_bias, outer_weight, outer_bias, gain, shift)


def feed_back_kernel(
    size, steps, share, place_ref, grad_low_ref, grad_ref, slope_ref, inner_ref, outer_ref, unit_ref,
    factor_ref, gain_ref, *refs,
):
    out_weights, refs = refs[:size], refs[size:]
    inners = refs[:size]
    bias_ref, one_ref, low_ref, sums_ref = refs[size : size + 4]
    cuts = refs[size + 4 : 2 * size + 4]
    mixes = refs[2 * size + 4 : 3 * size + 4]
    acc, keep = refs[3 * size + 4 :]
    step = pl.program_id(0)
    grad_inner = slope_ref[...].astype(FULL) * right_product(grad_low_ref[...], outer_ref[...])
    bias_ref[...] = column_sum(grad_inner)
    grad_inner = grad_inner.astype(LOW)
    for k in range(size):

        @pl.when(step // steps == (k + size - 1) % size)
        def _():
            inners[k][...] = grad_inner

    part = right_product(grad_inner, inner_ref[...])

    @pl.when(step == 0)
    def _():
        acc[...] = part

    @pl.when(step > 0)
    def _():
        acc[...] += part

    @pl.when(step == pl.num_programs(0) - 1)
    def _():
        grad = grad_ref[...] + acc[...]
        unit = unit_ref[...]
        sums_ref[0:1, :] = column_sum(grad * unit)
        sums_ref[1:2, :] = column_sum(grad)
        one = norm_pull(unit, factor_ref[...], gain_ref[...].astype(FULL), grad)
        sums_ref[2:3, :] = column_sum(one)
        one_ref[...] = one
        low = one.astype(LOW)
        low_ref[...] = low
        keep[...] = low
        for k in range(size):
            spot = pl.multiple_of((place_ref[1] ^ k) * share, 128)
            cuts[k][...] = keep[:, pl.ds(spot, share)]
            mixes[k][...] = right_product(low, out_weights[k][...]).astype(LOW)


def feed_back(
    places, size, grad_low, grad, slope, inner_weight, outer_weight, unit, factor, gain, out_weights
):
    rows, width = grad_low.shape
    hidden = inner_weight.shape[1]
    part = hidden // size
    tile = min(512, part)
    steps = part // tile
    share = width // size

    def spot(i, s):
        return (s[1] ^ ((i // steps + 1) % size)) * steps + i % steps

    def own(k):
        start = ((k + size - 1) % size) * steps
        return pl.BlockSpec((rows, tile), lambda i, s: (0, jnp.clip(i - start, 0, steps - 1)))

    whole = pl.BlockSpec((rows, width), lambda i, s: (0, 0))
    return pl.pallas_call(
        functools.partial(feed_back_kernel, size, steps, share),
        grid_spec=pltpu.PrefetchScalarGridSpec(
            num_scalar_prefetch=1,
            grid=(hidden // tile,),
            in_specs=[
                whole,
                whole,
                pl.BlockSpec((rows, tile), lambda i, s: (0, spot(i, s))),
                pl.BlockSpec((width, tile), lambda i, s: (0, spot(i, s))),
                pl.BlockSpec((tile, width), lambda i, s: (spot(i, s), 0)),
                whole,
                pl.BlockSpec((rows, 1), lambda i, s: (0, 0)),
                pl.BlockSpec((1, width), lambda i, s: (0, 0)),
            ]
            + [pl.BlockSpec((share, width), lambda i, s: (0, 0))] * size,
            out_specs=[own(k) for k in range(size)]
            + [
                pl.BlockSpec((1, tile), lambda i, s: (0, spot(i, s))),
                whole,
                whole,
                pl.BlockSpec((8, width), lambda i, s: (0, 0)),
            ]
            + [pl.BlockSpec((rows, share), lambda i, s: (0, 0))] * (2 * size),
            scratch_shapes=[pltpu.VMEM((rows, width), FULL), pltpu.VMEM((rows, width), LOW)],
        ),
        out_shape=[jax.ShapeDtypeStruct((rows, part), LOW)] * size
        + [
            jax.ShapeDtypeStruct((1, hidden), FULL),
            jax.ShapeDtypeStruct((rows, width), FULL),
            jax.ShapeDtypeStruct((rows, width), LOW),
            jax.ShapeDtypeStruct((8, width), FULL),
        ]
        + [jax.ShapeDtypeStruct((rows, share), LOW)] * (2 * size),
        compiler_params=params(60),
        cost_estimate=CHEAP,
        name="feed_back",
    )(places, grad_low, grad, slope, inner_weight, outer_weight, unit, factor, gain, *out_weights)


def back_kernel(size, place_ref, grad_ref, masked_ref, *refs):
    threes, weights, out_ref = refs[:size], refs[size:-1], refs[-1]
    total = grad_ref[...]
    for k in range(size):
        for n in range(3):
            total = total + right_product(threes[k][n], weights[3 * k + n][...])
    out_ref[...] = jnp.where(masked_ref[...] > 0.0, 0.0, total).astype(LOW)


def input_back(places, threes, weights, grad, masked):
    size = len(threes)
    rows, width = grad.shape
    share = threes[0].shape[2]
    tile = min(256, rows)
    line = pl.BlockSpec((tile, width), lambda i, s: (i, 0))
    return pl.pallas_call(
        functools.partial(back_kernel, size),
        grid_spec=pltpu.PrefetchScalarGridSpec(
            num_scalar_prefetch=1,
            grid=(rows // tile,),
            in_specs=[line, pl.BlockSpec((tile, 1), lambda i, s: (i, 0))]
            + [pl.BlockSpec((3, tile, share), lambda i, s: (0, i, 0))] * size
            + [
                pl.BlockSpec((width, share), lambda i, s, k=k: (0, s[1] ^ k))
                for k in range(size)
                for _ in range(3)
            ],
            out_specs=line,
        ),
        out_shape=jax.ShapeDtypeStruct((rows, width), LOW),
        compiler_params=params(),
        cost_estimate=CHEAP,
        name="input_back",
    )(places, grad, masked, *threes, *(list(weights) * size))


def part_orders(bits):
    if bits < 3:
        return [(list(range(bits)),) * 2] * 2
    rest = list(range(3, bits))
    return [([0, 2, 1] + rest, [1, 0, 2] + rest), ([2, 1, 0] + rest,) * 2]


def part_depths(lines, weights):
    tiles = lines // 16
    first = round(tiles * weights[0] / sum(weights))
    return [16 * first, 16 * (tiles - first)]


def offset_at(position, order):
    return sum(((position >> (len(order) - 1 - n)) & 1) << order[n] for n in range(len(order)))


def weight_kernel(layout, flips, teams, lines, parts, members, bias, extra, place_ref, *refs):
    number = sum(layout)
    lefts, rights = refs[:number], refs[number : number + members]
    count = 2 * len(parts)
    singles, refs = refs[number + members : number + members + extra], refs[number + members + extra :]
    outs, scratch = refs[:count], refs[count:]
    flipped = scratch[:members] if flips else lefts
    total = scratch[members if flips else 0]
    step = pl.program_id(0)
    team = place_ref[0]
    half = teams // 2

    def block_at(position, order):
        even, odd = (offset_at(position, o) for o in order)
        return team ^ (even if even == odd else jnp.where(place_ref[1] % 2 == 0, even, odd))

    if flips:

        @pl.when(step == 0)
        def _():
            spot = 0
            for member in range(members):
                start = 0
                for _ in range(layout[member]):
                    wide = lefts[spot].shape[1]
                    flipped[member][start : start + wide, :] = lefts[spot][...].T
                    start, spot = start + wide, spot + 1

    def right(member):
        ref = rights[member]
        return ref[0] if len(ref.shape) == 3 else ref[...]

    def multiply():
        acc = product(flipped[0][...], right(0))
        for member in range(1, members):
            acc = acc + product(flipped[member][...], right(member))
        total[...] = acc.astype(LOW)
        for k, (order, start, deep) in enumerate(parts):
            for position in range(teams):
                line = pl.multiple_of(block_at(position, order) * lines + start, 16)
                outs[2 * k + position // half][position % half, 0] = total[pl.ds(line, deep), :]

    if not bias and not extra:
        multiply()
        return

    chunks = pl.num_programs(0) - 1
    last = outs[count - 2 : count]
    order = parts[-1][0]
    if extra:
        vectors = scratch[-1]

        @pl.when(step < chunks)
        def _():
            multiply()

        @pl.when(step == chunks)
        def _():
            inner = singles[-1].shape[1] // teams
            for row in range(teams):
                for k in range(6):
                    vectors[row : row + 1, k * lines : (k + 1) * lines] = singles[k // 3][
                        k % 3 : k % 3 + 1, row * lines : (row + 1) * lines
                    ]
                vectors[row : row + 1, 6 * lines : 6 * lines + inner] = singles[2][
                    :, row * inner : (row + 1) * inner
                ]
            deep = lax.broadcasted_iota(jnp.int32, (16, CHUNK), 0)
            for position in range(teams):
                row = vectors[pl.ds(block_at(position, order), 1), :]
                value = jnp.zeros((16, CHUNK), FULL)
                for k in range(vectors.shape[1] // CHUNK):
                    piece = jnp.broadcast_to(row[:, k * CHUNK : (k + 1) * CHUNK], (16, CHUNK))
                    value = jnp.where(deep == k, piece, value)
                last[position // half][position % half, 0, 0:16, :] = value.astype(LOW)

        return

    sums, vectors = scratch[-2:]

    @pl.when(step < chunks)
    def _():
        multiply()
        sums[pl.ds(step, 1), :] = sum(column_sum(right(m).astype(FULL)) for m in range(members))

    @pl.when(step == chunks)
    def _():
        own = vectors.shape[0]
        for k, first in enumerate(bias[0]):
            for team_row in range(own):
                chunk, lane = divmod(first + team_row * lines, CHUNK)
                vectors[team_row : team_row + 1, k * lines : (k + 1) * lines] = sums[
                    chunk : chunk + 1, lane : lane + lines
                ]
        wide = vectors.shape[1]
        for position in range(teams):
            local = block_at(position, order) - place_ref[1] * (teams // members) - bias[1]
            inside = jnp.logical_and(local >= 0, local < own)
            row = vectors[pl.ds(jnp.clip(local, 0, own - 1), 1), :]
            row = jnp.where(inside, row, 0.0)
            last[position // half][position % half, 0, 0:16, 0:wide] = jnp.broadcast_to(
                row, (16, wide)
            ).astype(LOW)


def weight_grad(name, lefts, flips, rights, places, teams, width, weights, bias=(), sums=(), mib=60):
    members = len(lefts)
    rows = rights[0][1][-2]
    flat = [item for member in lefts for item in member]
    high = sum(a.shape[1] for a, _ in lefts[0]) if flips else lefts[0][0][0].shape[0]
    lines = high // teams
    orders = part_orders(teams.bit_length() - 1)
    parts, start = [], 0
    for order, deep in zip(orders, part_depths(lines, weights)):
        if deep:
            parts.append((order, start, deep))
        start += deep
    half = teams // 2
    chunks = width // CHUNK
    own = bias[2] if bias else 0
    if sums:
        sums_wide = 6 * lines + sums[-1].shape[1] // teams
        sums_wide = -(-sums_wide // CHUNK) * CHUNK
    counts = [chunks] * len(parts)
    if bias or sums:
        counts[-1] += 1
    outs = pl.pallas_call(
        functools.partial(
            weight_kernel, [len(m) for m in lefts], flips, teams, lines, parts, members, bias, len(sums)
        ),
        grid_spec=pltpu.PrefetchScalarGridSpec(
            num_scalar_prefetch=1,
            grid=(counts[-1],),
            in_specs=[
                pl.BlockSpec(
                    (rows, array.shape[1]) if flips else array.shape, lambda i, s, b=block: (b, 0)
                )
                for array, block in flat
            ]
            + [
                pl.BlockSpec(shape, lambda i, s, f=index: f(jnp.minimum(i, chunks - 1), s))
                for _, shape, index in rights
            ]
            + [pl.BlockSpec(a.shape, lambda i, s: (0, 0)) for a in sums],
            out_specs=[
                pl.BlockSpec(
                    (half, 1, p[2], CHUNK), lambda i, s, c=c: (0, jnp.minimum(i, c - 1), 0, 0)
                )
                for p, c in zip(parts, counts)
                for _ in range(2)
            ],
            scratch_shapes=[pltpu.VMEM((high, rows), LOW)] * (members if flips else 0)
            + [pltpu.VMEM((high, CHUNK), LOW)]
            + (
                [pltpu.VMEM((chunks, CHUNK), FULL), pltpu.VMEM((own, len(bias[0]) * lines), FULL)]
                if bias
                else [pltpu.VMEM((teams, sums_wide), FULL)] if sums else []
            ),
        ),
        out_shape=[
            jax.ShapeDtypeStruct((half, c, p[2], CHUNK), LOW)
            for p, c in zip(parts, counts)
            for _ in range(2)
        ],
        compiler_params=params(mib),
        cost_estimate=CHEAP,
        name="weight_grad",
    )(places, *[array for array, _ in flat], *[array for array, _, _ in rights], *sums)
    made = []
    for k, (order, start, deep) in enumerate(parts):
        near, far = (o.reshape(half, counts[k] * deep, CHUNK) for o in outs[2 * k : 2 * k + 2])
        segments = [(name, start, deep, c) for c in range(chunks)]
        if counts[k] > chunks:
            segments.append(("bias", 0, deep, 0))
        made.append(dict(order=order, near=near, far=far, segments=segments))
    return made


def fold_kernel(counts, *refs):
    total = 4 * sum(counts)
    outs = refs[total:]
    spot = 0
    for k, count in enumerate(counts):
        start = 0
        for _ in range(count):
            near_low, near_high, came_low, came_high = refs[spot : spot + 4]
            deep = near_low.shape[1]
            rows = slice(start, start + deep)
            outs[2 * k][:, rows] = (near_low[...].astype(FULL) + came_low[...].astype(FULL)).astype(LOW)
            outs[2 * k + 1][:, rows] = (
                near_high[...].astype(FULL) + came_high[...].astype(FULL)
            ).astype(LOW)
            start, spot = start + deep, spot + 4


def fold(*groups):
    orders = []
    for group in groups:
        for part in group:
            if part["order"] not in orders:
                orders.append(part["order"])
    merged = [[p for g in groups for p in g if p["order"] == order] for order in orders]
    half = merged[0][0]["near"].shape[0] // 2
    operands, in_specs, out_specs, out_shape, counts = [], [], [], [], []
    for parts in merged:
        rows = 0
        for part in parts:
            deep = part["near"].shape[1]
            rows += deep
            low = pl.BlockSpec((1, deep, CHUNK), lambda i: (i, 0, 0))
            high = pl.BlockSpec((1, deep, CHUNK), lambda i: (half + i, 0, 0))
            operands += [part["near"], part["near"], part["came"], part["came"]]
            in_specs += [low, high, low, high]
        counts.append(len(parts))
        out_specs += [pl.BlockSpec((1, rows, CHUNK), lambda i: (i, 0, 0))] * 2
        out_shape += [jax.ShapeDtypeStruct((half, rows, CHUNK), LOW)] * 2
    outs = pl.pallas_call(
        functools.partial(fold_kernel, counts),
        grid=(half,),
        in_specs=in_specs,
        out_specs=out_specs,
        out_shape=out_shape,
        compiler_params=params(60 if len(operands) > 12 else 40),
        cost_estimate=CHEAP,
        name="fold",
    )(*operands)
    return [
        dict(
            order=tuple(o[1:] for o in parts[0]["order"]),
            near=outs[2 * k],
            far=outs[2 * k + 1],
            segments=[s for p in parts for s in p["segments"]],
        )
        for k, parts in enumerate(merged)
    ]


def final_kernel(layouts, plain, settled, size, lines, place_ref, *refs):
    count = len(layouts)
    outs = refs[2 * count :]
    targets = dict(zip(plain, outs))
    pieces = outs[len(plain) : len(plain) + size]
    if settled:
        targets[None] = outs[-1]
    biases = []
    for k, layout in enumerate(layouts):
        spot = 0
        for name, start, deep, column in layout:
            rows = slice(spot, spot + (16 if name == "bias" else deep))
            value = refs[2 * k][0, rows].astype(FULL) + refs[2 * k + 1][0, rows].astype(FULL)
            spot += deep
            if name == "bias":
                biases.append(value[0:8])
                continue
            targets[name][start : start + deep, column * CHUNK : (column + 1) * CHUNK] = value
    if settled:
        for piece in pieces if biases else ():
            piece[lines : lines + 8, 0:CHUNK] = sum(biases)
        for k in range(size):
            line = pl.multiple_of((place_ref[1] ^ k) * lines, 8)
            pieces[k][0:lines, :] = targets[None][pl.ds(line, lines), :]


def final(parts, places, size, lines, plain, settled):
    layouts, wide, more = [], 0, 0
    for part in parts:
        layout = []
        for name, start, deep, column in part["segments"]:
            if name in plain or name == "bias":
                more = 8 if name == "bias" else more
                layout.append((name, start, deep, column))
            else:
                column += settled[name] // CHUNK
                wide = max(wide, (column + 1) * CHUNK)
                layout.append((None, start, deep, column))
        layouts.append(layout)
    names = list(plain)
    shapes = [jax.ShapeDtypeStruct(plain[n], FULL) for n in names]
    if settled:
        shapes += [jax.ShapeDtypeStruct((lines + more, wide), FULL)] * size
    outs = pl.pallas_call(
        functools.partial(final_kernel, layouts, names, bool(settled), size, lines),
        in_specs=[pl.BlockSpec(memory_space=pltpu.SMEM)]
        + [pl.BlockSpec(memory_space=pltpu.VMEM)] * (2 * len(parts)),
        out_specs=[pl.BlockSpec(memory_space=pltpu.VMEM)] * len(shapes),
        out_shape=shapes,
        scratch_shapes=[pltpu.VMEM((size * lines, wide), FULL)] if settled else [],
        compiler_params=params(32),
        cost_estimate=CHEAP,
        name="final",
    )(places, *[p[n] for p in parts for n in ("near", "came")])
    return dict(zip(names, outs)), outs[len(names) :]


def tie(value, *others):
    return lax.optimization_barrier((value, others))[0]


def per_device(
    inputs,
    mask_pos,
    mask_count,
    replace,
    cotangent,
    query_weight,
    query_bias,
    key_weight,
    value_weight,
    value_bias,
    out_weight,
    out_bias,
    first_gain,
    first_shift,
    inner_weight,
    inner_bias,
    outer_weight,
    outer_bias,
    second_gain,
    second_shift,
):
    groups, rows, width = inputs.shape
    hidden = inner_weight.shape[1]
    blocks = lax.axis_size("blk")
    number = lax.axis_size("dp") * blocks
    size = blocks // groups
    piece = rows // size
    own_rows = blocks * piece
    teams = number // size
    bits = teams.bit_length() - 1
    place = lax.axis_index("blk")
    flat = lax.axis_index("dp") * blocks + place
    sequence = place // size
    rank = place % size
    team = flat // size
    share = width // size
    hidden_share = hidden // size
    others = range(1, size)

    def hop(array, mask):
        return lax.ppermute(array, BOTH, [(i, i ^ mask) for i in range(number)])

    def cut(array, who, count, axis):
        return lax.dynamic_slice_in_dim(array, who * count, count, axis=axis)

    def swap(make):
        return [make(rank)] + [hop(make(rank ^ k), k) for k in others]

    def absolute(pieces, axis):
        if size == 2:
            first = rank == 0
            return jnp.concatenate(
                [jnp.where(first, pieces[0], pieces[1]), jnp.where(first, pieces[1], pieces[0])],
                axis=axis,
            )
        stacked = jnp.stack(pieces)
        return jnp.concatenate(
            [lax.dynamic_index_in_dim(stacked, q ^ rank, 0, keepdims=False) for q in range(size)],
            axis=axis,
        )

    def send(parts):
        return [
            dict(
                p,
                came=lax.ppermute(
                    p["far"],
                    BOTH,
                    [(i, i ^ (size << p["order"][i % size % 2][0])) for i in range(number)],
                ),
            )
            for p in parts
        ]

    def far(parts):
        return [p["far"] for p in parts]

    def sync(values, *groups):
        values, came = lax.optimization_barrier((values, [[p["came"] for p in g] for g in groups]))
        made = [[dict(p, came=c) for p, c in zip(g, cs)] for g, cs in zip(groups, came)]
        return (values, *made)

    def after(parts, *values):
        came = lax.optimization_barrier(([p["came"] for p in parts], values))[0]
        return [dict(p, came=c) for p, c in zip(parts, came)]

    def line(vector):
        return vector.reshape(1, -1)

    arrived = lax.all_to_all(inputs.reshape(blocks, piece, width), "blk", 0, 0)
    lane = jnp.arange(own_rows, dtype=jnp.int32)
    positions = (lane // piece) * rows + rank * piece + lane % piece
    swapped, seeded, masked = masked_rows(
        sequence.reshape(1).astype(jnp.int32), mask_count, positions.reshape(-1, 1), mask_pos, replace, cotangent
    )
    places = jnp.stack([team, rank]).astype(jnp.int32)
    heads_weight = jnp.concatenate(
        [cut(w, rank, share, 1) for w in (query_weight, key_weight, value_weight)], axis=1
    )
    heads_bias = jnp.concatenate(
        [
            cut(query_bias, rank, share, 0),
            jnp.zeros((share,), LOW),
            cut(value_bias, rank, share, 0),
        ]
    )
    out_weights = [cut(out_weight, rank ^ k, share, 0) for k in range(size)]

    arrived = tie(arrived, swapped, seeded, heads_weight, heads_bias, out_weights, masked)
    current = jnp.where(masked > 0.0, swapped, arrived.reshape(own_rows, width))
    currents = [current] + [hop(current, k) for k in others]
    joined = product(jnp.concatenate(currents, axis=0), heads_weight) + heads_bias.astype(FULL)
    joined = joined.astype(LOW)
    mixed_heads, log_total = attention_forward(joined)

    mixed_parts = mixed_heads.reshape(size, own_rows, share)
    mixed_here = [mixed_parts[0]] + [hop(mixed_parts[k], k) for k in others]
    mixed_away = []
    for k in others:
        row = []
        for q in range(size):
            if q == 0:
                row.append((mixed_heads, k))
            else:
                row.append((hop(mixed_parts[k ^ q], q), 0))
        mixed_away.append(row)

    first, first_flip, first_low, unit_one, factor_one = first_half(
        current,
        [(m, share) for m in [mixed_heads] + mixed_here[1:]],
        out_weights,
        line(out_bias),
        line(first_gain),
        line(first_shift),
    )
    firsts = [first_flip] + [hop(first_flip, k) for k in others]
    fed = feed_forward(
        places, size, number, first_low, first, seeded, inner_weight, line(inner_bias),
        outer_weight, line(outer_bias), line(second_gain), line(second_shift),
    )
    actives = [fed[0]] + [hop(fed[k], k) for k in others]
    slope, result, grad_two, grad_two_low, second_sums = fed[size:]

    def home(array):
        return lax.all_to_all(array.reshape(blocks, piece, width), "blk", 0, 0)

    def wide(array):
        return array.reshape(groups, rows, width).astype(FULL)

    grad_twos = [grad_two_low] + [hop(grad_two_low, k) for k in others]

    def plain(array):
        return (array, (own_rows, CHUNK), lambda i, s: (0, i))

    layer_out = home(result)
    back = feed_back(
        places, size, grad_two_low, grad_two, slope, inner_weight, outer_weight, unit_one, factor_one,
        line(first_gain), out_weights,
    )
    back, layer_out, grad_twos, actives = lax.optimization_barrier((back, layer_out, grad_twos, actives))
    layer_out = wide(layer_out)
    grad_inners = [back[0]] + [hop(back[k], k) for k in others]
    inner_bias_grad, grad_one, grad_one_low, first_sums = back[size : size + 4]
    grad_ones = [back[size + 4]] + [hop(back[size + 4 + k], k) for k in others]
    grad_mixed = back[2 * size + 4 : 3 * size + 4]
    grad_mixed = [grad_mixed[0]] + [hop(grad_mixed[k], k) for k in others]
    outer_parts = weight_grad(
        "outer", [[(a, 0)] for a in actives], False, [plain(g) for g in grad_twos], places, teams, width,
        (2, 1),
    )
    grad_ones[0] = tie(grad_ones[0], far(outer_parts))
    outer_parts = send(outer_parts)
    out_parts = weight_grad(
        "out", [[(m, 0) for m in [mixed_heads] + mixed_here[1:]]] + mixed_away, True,
        [plain(g) for g in grad_ones],
        jnp.stack([team ^ (rank * (teams // size)), rank]).astype(jnp.int32), teams, share, (1, 0),
    )
    grad_inners[0] = tie(grad_inners[0], far(out_parts))
    out_parts = send(out_parts)
    inner_parts = weight_grad(
        "inner", [[(f, 0)] for f in firsts], False, [plain(g) for g in grad_inners], places, teams,
        hidden_share, (3, 1), sums=(first_sums, second_sums, inner_bias_grad),
    )
    fars, outer_parts = sync(far(inner_parts), outer_parts)
    inner_parts = send([dict(p, far=f) for p, f in zip(inner_parts, fars)])
    grad_mixed[0] = tie(grad_mixed[0], fars)

    pairs = share // (2 * HEAD)
    number_of = 2 if share // 2 % CHUNK == 0 else 1
    count = pairs // number_of
    part = share // number_of
    chunks = part // CHUNK
    team_rows = teams // size // number_of

    def three_grad(three, group):
        return weight_grad(
            f"three{group}", [[(c, 0)] for c in currents], True,
            [
                (
                    three,
                    (1, own_rows, CHUNK),
                    lambda i, s, k=k: (i // chunks, k, group * chunks + i % chunks),
                )
                for k in range(size)
            ],
            places, teams, 3 * part, (3, 1), ((0, 2 * part), group * team_rows, team_rows), mib=40,
        )

    three = attention_backward(joined, grad_mixed, mixed_heads, log_total, 0, count)
    late = []
    if number_of == 2:
        late = three_grad(three, 0)
        three = tie(three, far(late))
        late = send(late)
    three, inner_parts, out_parts = sync(three, inner_parts, out_parts)
    early = fold(outer_parts, inner_parts, out_parts)
    three = tie(three, far(early))
    early = send(early)
    if number_of == 2:
        three = attention_backward(joined, grad_mixed, mixed_heads, log_total, count, count, three)
    three, early, late = sync(three, early, late)
    early = fold(early)
    three = tie(three, far(early))
    threes = [three] + [hop(three[:, k * own_rows : (k + 1) * own_rows], k) for k in others]
    early = send(early)
    more = three_grad(three, number_of - 1)
    (threes, fars), early = sync((threes, far(more)), early)
    more = send([dict(p, far=f) for p, f in zip(more, fars)])
    early = fold(early)
    threes[0] = tie(threes[0], far(early))
    early_one, early_two = send(early[:1]), early[1:]
    input_grad = input_back(places, threes, (query_weight, key_weight, value_weight), grad_one, masked)
    home_grad = home(input_grad)
    _, more, early_one = sync((input_grad, layer_out), more, early_one)
    late = fold(late, more) if late else fold(more)
    for p, f in zip(early_two, tie(far(early_two), far(late))):
        p["far"] = f
    late, early_two = send(late), send(early_two)
    while len((early_one + early_two)[0]["order"][0]) > 1:
        early_one, early_two = send(fold(early_one + early_two)), []

    lines = width // number
    _, late, early_two = sync(far(late), late, early_two)
    if len(late[0]["order"][0]) > 1:
        late = fold(late)
        early_one = [dict(p, near=tie(p["near"], far(late))) for p in early_one]
        home_grad = tie(home_grad, far(late))
        late = send(late)
    made, early = final(
        early_one + early_two, places, size, lines, {"outer": (hidden // number, width)},
        {"inner": 0, "out": hidden_share},
    )
    outer_weight_grad = made["outer"]
    early_away = [hop(early[k], k) for k in others]
    input_grad = wide(home_grad)
    late = after(late, input_grad, outer_weight_grad)
    while len(late[0]["order"][0]) > 1:
        late = fold(late)
        early_away = tie(early_away, far(late))
        late = send(late)
    early = [early[0]] + early_away
    inner_weight_grad = absolute([e[:lines, :hidden_share] for e in early], 1)
    out_weight_grad = absolute([e[:lines, hidden_share:] for e in early], 1)
    team_lines, team_hidden = width // teams, hidden // teams
    flat_rows = -(-(6 * team_lines + team_hidden) // CHUNK)
    flat = sum(e[lines : lines + flat_rows, :CHUNK] for e in early).reshape(1, -1)
    six = cut(flat[:, : 6 * team_lines].reshape(6, team_lines), rank, lines, 1)
    inner_bias_grad = cut(
        flat[:, 6 * team_lines : 6 * team_lines + team_hidden], rank, team_hidden // size, 1
    )
    _, late = final(
        after(late, inner_weight_grad, out_weight_grad), places, size, lines, {},
        {f"three{g}": g * 3 * part for g in range(number_of)},
    )
    late = [late[0]] + [hop(late[k], k) for k in others]

    def three_columns(e, k):
        cuts = [
            e[:lines, (g * 3 + k) * part : (g * 3 + k + 1) * part] for g in range(number_of)
        ]
        return jnp.concatenate(cuts, axis=1)

    three_grads = [absolute([three_columns(e, k) for e in late], 1) for k in range(3)]
    biases = sum(e[lines, : 2 * team_lines] for e in late).reshape(2, team_lines)
    biases = cut(biases, rank, lines, 1)
    spots = [biases[0], biases[1], six[2], six[0], six[1], inner_bias_grad[0], six[5], six[3], six[4]]

    return (
        layer_out,
        input_grad,
        three_grads[0],
        spots[0],
        three_grads[1],
        three_grads[2],
        spots[1],
        out_weight_grad,
        spots[2],
        spots[3],
        spots[4],
        inner_weight_grad,
        spots[5],
        outer_weight_grad,
        spots[6],
        spots[7],
        spots[8],
    )


def solution(mesh):
    split = P("dp", "blk", None)
    row = P("dp")
    both = P(BOTH)
    in_specs = (split, row, row, row, row) + (P(),) * 15
    out_specs = (split, split) + (both,) * 15
    return jax.shard_map(
        per_device, mesh=mesh, in_specs=in_specs, out_specs=out_specs, check_vma=False
    )
```

```python
import functools
import math

import jax
import jax.numpy as jnp
from jax import lax
from jax.experimental import pallas as pl
from jax.experimental.pallas import tpu as pltpu
from jax.sharding import PartitionSpec as P

HEAD = 64
EPSILON = 1e-05
BOTH = ("dp", "blk")
LOW = jnp.bfloat16
FULL = jnp.float32
CHUNK = 256
BACK = 512
LINES = 128
CHEAP = pl.CostEstimate(flops=1, bytes_accessed=1, transcendentals=0)


def product(left, right):
    return jnp.dot(left, right, preferred_element_type=FULL)


def right_product(left, right):
    return lax.dot_general(left, right, (((1,), (1,)), ((), ())), preferred_element_type=FULL)


def norm_stats(hidden):
    center = hidden - jnp.mean(hidden, axis=-1, keepdims=True)
    spread = jnp.mean(center * center, axis=-1, keepdims=True)
    factor = lax.rsqrt(spread + EPSILON)
    return center * factor, factor


def norm_pull(unit, factor, gain, grad):
    scaled = grad * gain
    inner = jnp.mean(scaled, axis=-1, keepdims=True)
    along = jnp.mean(scaled * unit, axis=-1, keepdims=True)
    return factor * (scaled - inner - unit * along)


def column_sum(array):
    return jnp.sum(array, axis=0, keepdims=True)


def gelu_parts(inner):
    bell = jnp.exp(-0.5 * inner * inner)
    t = 1.0 / (1.0 + (0.3275911 * math.sqrt(0.5)) * jnp.abs(inner))
    poly = 0.5 * 1.061405429
    for c in (-1.453152027, 1.421413741, -0.284496736, 0.254829592):
        poly = poly * t + 0.5 * c
    tail = poly * t * bell
    below = jnp.where(inner >= 0.0, 1.0 - tail, tail)
    return inner * below, below + inner * bell * (1.0 / math.sqrt(2.0 * math.pi))


def params(mib=40):
    return pltpu.CompilerParams(vmem_limit_bytes=mib << 20)


def forward_kernel(query_ref, key_ref, value_ref, mixed_ref, log_ref):
    lane = lax.broadcasted_iota(jnp.int32, (1, 2 * HEAD), 1)
    query = query_ref[...] * LOW(1.0 / math.sqrt(HEAD))
    key = key_ref[...]
    value_t = value_ref[...].T
    outs = []
    for head in range(2):
        mine = (lane < HEAD) if head == 0 else (lane >= HEAD)
        scores = right_product(key, jnp.where(mine, query, LOW(0)))
        highest = jnp.max(scores, axis=0, keepdims=True)
        expon = jnp.exp(scores - highest)
        total = jnp.sum(expon, axis=0, keepdims=True)
        out = product(value_t[head * HEAD : (head + 1) * HEAD], expon.astype(LOW))
        outs.append(out * (1.0 / total))
        log_ref[0, head : head + 1, :] = highest + jnp.log(total)
    mixed_ref[...] = jnp.concatenate(outs, axis=0).T.astype(LOW)


def backward_kernel(
    members, query_ref, key_ref, value_ref, mixed_ref, log_ref, *refs
):
    grads = refs[:members]
    out_ref, key_sum, value_sum = refs[-3:]
    step = pl.program_id(1)

    @pl.when(step == 0)
    def _():
        key_sum[...] = jnp.zeros_like(key_sum)
        value_sum[...] = jnp.zeros_like(value_sum)

    scale = 1.0 / math.sqrt(HEAD)
    lane = lax.broadcasted_iota(jnp.int32, (1, 2 * HEAD), 1)
    query = query_ref[...] * LOW(scale)
    key = key_ref[...]
    value = value_ref[...]
    tile = query.shape[0]
    together = tile // grads[0].shape[0]
    pieces = []
    for k in range(together):
        piece = grads[k][...]
        for other in range(k + together, members, together):
            piece = jnp.where(step == other // together, grads[other][...], piece)
        pieces.append(piece)
    grad = jnp.concatenate(pieces, axis=0)
    both = (grad.astype(FULL) * mixed_ref[...].astype(FULL)).T
    key_t = key.T
    outs = []
    for head in range(2):
        mine = (lane < HEAD) if head == 0 else (lane >= HEAD)
        own = slice(head * HEAD, (head + 1) * HEAD)
        delta = jnp.sum(both[own], axis=0, keepdims=True)
        query_one = jnp.where(mine, query, LOW(0))
        grad_one = jnp.where(mine, grad, LOW(0))
        shares = jnp.exp(right_product(key, query_one) - log_ref[0, head : head + 1, :])
        grad_shares = right_product(value, grad_one)
        grad_scores = (shares * (grad_shares - delta)).astype(LOW)
        value_sum[...] += product(shares.astype(LOW), grad_one)
        key_sum[...] += product(grad_scores, query_one)
        outs.append(product(key_t[own], grad_scores))
    spot = pl.ds(pl.multiple_of(step * tile, tile), tile)
    out_ref[0, spot, :] = (jnp.concatenate(outs, axis=0).T * scale).astype(LOW)

    @pl.when(step == pl.num_programs(1) - 1)
    def _():
        out_ref[1] = key_sum[...].astype(LOW)
        out_ref[2] = value_sum[...].astype(LOW)


def attention_forward(joined):
    rows, wide = joined.shape
    share = wide // 3
    pairs = share // (2 * HEAD)
    tile = min(1024, rows)

    def whole(offset):
        return pl.BlockSpec((rows, 2 * HEAD), lambda p, i: (0, offset + p))

    line = pl.BlockSpec((tile, 2 * HEAD), lambda p, i: (i, p))
    return pl.pallas_call(
        forward_kernel,
        grid=(pairs, rows // tile),
        in_specs=[line, whole(pairs), whole(2 * pairs)],
        out_specs=[line, pl.BlockSpec((1, 2, tile), lambda p, i: (p, 0, i))],
        out_shape=[
            jax.ShapeDtypeStruct((rows, share), LOW),
            jax.ShapeDtypeStruct((pairs, 2, rows), FULL),
        ],
        compiler_params=params(48),
        cost_estimate=CHEAP,
        name="attention_forward",
    )(joined, joined, joined)


def attention_backward(joined, grad_mixed, mixed, log_total, first, count, previous=None):
    rows, wide = joined.shape
    share = wide // 3
    pairs = share // (2 * HEAD)
    members = len(grad_mixed)
    own_rows = rows // members
    tile = own_rows * max(1, BACK // own_rows)

    def whole(offset):
        return pl.BlockSpec((rows, 2 * HEAD), lambda p, i: (0, offset + p))

    line = pl.BlockSpec((tile, 2 * HEAD), lambda p, i: (i, first + p))
    grad_line = pl.BlockSpec((own_rows, 2 * HEAD), lambda p, i: (0, first + p))
    more = [] if previous is None else [previous]
    return pl.pallas_call(
        functools.partial(backward_kernel, members),
        grid=(count, rows // tile),
        in_specs=[
            line,
            whole(pairs + first),
            whole(2 * pairs + first),
            line,
            pl.BlockSpec((1, 2, tile), lambda p, i: (first + p, 0, i)),
        ]
        + [grad_line] * members
        + [pl.BlockSpec(memory_space=pl.ANY)] * len(more),
        out_specs=pl.BlockSpec((3, rows, 2 * HEAD), lambda p, i: (0, 0, first + p)),
        out_shape=jax.ShapeDtypeStruct((3, rows, share), LOW),
        input_output_aliases={5 + members: 0} if more else {},
        scratch_shapes=[pltpu.VMEM((rows, 2 * HEAD), FULL)] * 2,
        compiler_params=params(48),
        cost_estimate=CHEAP,
        name="attention_backward",
    )(joined, joined, joined, mixed, log_total, *grad_mixed, *more)


def rows_kernel(sequence_ref, count_ref, position_ref, listed_ref, replace_ref, cotangent_ref, *refs):
    swapped_ref, seeded_ref, masked_ref = refs
    count = count_ref[sequence_ref[0]]
    listed = listed_ref[0]
    live = lax.broadcasted_iota(jnp.int32, listed.shape, 1) < count
    matches = jnp.where(live, listed, -1) == position_ref[...]
    select = matches.astype(FULL)
    masked_ref[...] = jnp.max(select, axis=1, keepdims=True)
    select = select.astype(LOW)
    swapped_ref[...] = product(select, replace_ref[0]).astype(LOW)
    seeded_ref[...] = product(select, cotangent_ref[0]).astype(LOW)


def masked_rows(sequence, mask_count, positions, mask_pos, replace, cotangent):
    rows = positions.shape[0]
    _, slots, width = replace.shape
    line = pl.BlockSpec((1, slots, width), lambda i, s, c: (s[0], 0, 0))
    return pl.pallas_call(
        rows_kernel,
        grid_spec=pltpu.PrefetchScalarGridSpec(
            num_scalar_prefetch=2,
            grid=(1,),
            in_specs=[
                pl.BlockSpec((rows, 1), lambda i, s, c: (0, 0)),
                pl.BlockSpec((1, 1, slots), lambda i, s, c: (s[0], 0, 0)),
                line,
                line,
            ],
            out_specs=[
                pl.BlockSpec((rows, width), lambda i, s, c: (0, 0)),
                pl.BlockSpec((rows, width), lambda i, s, c: (0, 0)),
                pl.BlockSpec((rows, 1), lambda i, s, c: (0, 0)),
            ],
        ),
        out_shape=[
            jax.ShapeDtypeStruct((rows, width), LOW),
            jax.ShapeDtypeStruct((rows, width), LOW),
            jax.ShapeDtypeStruct((rows, 1), FULL),
        ],
        compiler_params=params(),
        cost_estimate=CHEAP,
        name="masked_rows",
    )(sequence, mask_count, positions, mask_pos.reshape(-1, 1, slots), replace, cotangent)


def first_kernel(pieces, current_ref, bias_ref, gain_ref, shift_ref, *refs):
    mixed, weights = refs[:pieces], refs[pieces : 2 * pieces]
    first_ref, flip_ref, low_ref, unit_ref, factor_ref = refs[2 * pieces :]
    total = current_ref[...].astype(FULL) + bias_ref[...].astype(FULL)
    for part, weight in zip(mixed, weights):
        total = total + product(part[...], weight[...])
    unit, factor = norm_stats(total)
    first = unit * gain_ref[...].astype(FULL) + shift_ref[...].astype(FULL)
    first_ref[...] = first
    low = first.astype(LOW)
    low_ref[...] = low
    flip_ref[...] = low.T
    unit_ref[...] = unit
    factor_ref[...] = factor


def row_of(k, width):
    return pl.BlockSpec((None, 1, width), lambda *_: (k, 0, 0))


def first_half(current, mixed, weights, small):
    rows, width = current.shape
    tile = 128
    pieces = len(mixed)
    line = pl.BlockSpec((tile, width), lambda i: (i, 0))
    return pl.pallas_call(
        functools.partial(first_kernel, pieces),
        grid=(rows // tile,),
        in_specs=[line] + [row_of(k, width) for k in (0, 1, 2)]
        + [pl.BlockSpec((tile, block_width), lambda i: (i, 0)) for _, block_width in mixed]
        + [pl.BlockSpec(w.shape, lambda i: (0, 0)) for w in weights],
        out_specs=[
            line,
            pl.BlockSpec((width, tile), lambda i: (0, i)),
            line,
            line,
            pl.BlockSpec((tile, 1), lambda i: (i, 0)),
        ],
        out_shape=[
            jax.ShapeDtypeStruct((rows, width), FULL),
            jax.ShapeDtypeStruct((width, rows), LOW),
            jax.ShapeDtypeStruct((rows, width), LOW),
            jax.ShapeDtypeStruct((rows, width), FULL),
            jax.ShapeDtypeStruct((rows, 1), FULL),
        ],
        compiler_params=params(60),
        cost_estimate=CHEAP,
        name="first_half",
    )(current, small, small, small, *[m for m, _ in mixed], *weights)


def feed_kernel(
    size, unit_rows, place_ref, low_ref, first_ref, seed_ref, inner_ref, inner_bias_ref, outer_ref,
    outer_bias_ref, gain_ref, shift_ref, *refs,
):
    actives = refs[:size]
    slope_ref, result_ref, grad_ref, grad_low_ref, sums_ref, acc, flip = refs[size:]
    step = pl.program_id(0)
    inner = product(low_ref[...], inner_ref[...]) + inner_bias_ref[...].astype(FULL)
    active, slope = gelu_parts(inner)
    active = active.astype(LOW)
    slope_ref[...] = slope.astype(LOW)
    flip[...] = active.T
    rank = place_ref[1]
    tile = flip.shape[0]
    for k in range(size):
        for q in range(tile // (unit_rows * size)):
            line = pl.multiple_of((q * size + (rank ^ k)) * unit_rows, 16)
            actives[k][q * unit_rows : (q + 1) * unit_rows, :] = flip[pl.ds(line, unit_rows), :]
    part = product(active, outer_ref[...])

    @pl.when(step == 0)
    def _():
        acc[...] = part

    @pl.when(step > 0)
    def _():
        acc[...] += part

    @pl.when(step == pl.num_programs(0) - 1)
    def _():
        gain = gain_ref[...].astype(FULL)
        shift = shift_ref[...].astype(FULL)
        bias = outer_bias_ref[...].astype(FULL)

        def some(block, sums):
            lines = pl.ds(pl.multiple_of(block * LINES, LINES), LINES)
            unit, factor = norm_stats(first_ref[lines, :] + acc[lines, :] + bias)
            result_ref[lines, :] = (unit * gain + shift).astype(LOW)
            seed = seed_ref[lines, :].astype(FULL)
            grad = norm_pull(unit, factor, gain, seed)
            grad_ref[lines, :] = grad
            grad_low_ref[lines, :] = grad.astype(LOW)
            more = (column_sum(seed * unit), column_sum(seed), column_sum(grad))
            return tuple(x + y for x, y in zip(sums, more))

        sums = lax.fori_loop(0, acc.shape[0] // LINES, some, (jnp.zeros_like(gain),) * 3)
        for k in range(3):
            sums_ref[k : k + 1, :] = sums[k]


def feed_forward(
    places, size, number, low, first, seeded, inner_weight, inner_bias, outer_weight, small
):
    rows, width = low.shape
    hidden = inner_weight.shape[1]
    tile = 512
    whole = pl.BlockSpec((rows, width), lambda i, s: (0, 0))
    across = pl.BlockSpec((rows, tile), lambda i, s: (0, i))
    return pl.pallas_call(
        functools.partial(feed_kernel, size, hidden // number),
        grid_spec=pltpu.PrefetchScalarGridSpec(
            num_scalar_prefetch=1,
            grid=(hidden // tile,),
            in_specs=[
                whole,
                whole,
                whole,
                pl.BlockSpec((width, tile), lambda i, s: (0, i)),
                pl.BlockSpec((1, tile), lambda i, s: (0, i)),
                pl.BlockSpec((tile, width), lambda i, s: (i, 0)),
            ]
            + [row_of(k, width) for k in (3, 4, 5)],
            out_specs=[pl.BlockSpec((tile // size, rows), lambda i, s: (i, 0))] * size
            + [across, whole, whole, whole, pl.BlockSpec((8, width), lambda i, s: (0, 0))],
            scratch_shapes=[pltpu.VMEM((rows, width), FULL), pltpu.VMEM((tile, rows), LOW)],
        ),
        out_shape=[jax.ShapeDtypeStruct((hidden // size, rows), LOW)] * size
        + [
            jax.ShapeDtypeStruct((rows, hidden), LOW),
            jax.ShapeDtypeStruct((rows, width), LOW),
            jax.ShapeDtypeStruct((rows, width), FULL),
            jax.ShapeDtypeStruct((rows, width), LOW),
            jax.ShapeDtypeStruct((8, width), FULL),
        ],
        compiler_params=params(60),
        cost_estimate=CHEAP,
        name="feed_forward",
    )(places, low, first, seeded, inner_weight, inner_bias, outer_weight, small, small, small)


def feed_back_kernel(
    size, steps, share, place_ref, grad_low_ref, grad_ref, slope_ref, inner_ref, outer_ref, unit_ref,
    factor_ref, gain_ref, *refs,
):
    out_weights, refs = refs[:size], refs[size:]
    inners = refs[:size]
    bias_ref, one_ref, low_ref, sums_ref = refs[size : size + 4]
    cuts = refs[size + 4 : 2 * size + 4]
    mixes = refs[2 * size + 4 : 3 * size + 4]
    acc, keep = refs[3 * size + 4 :]
    step = pl.program_id(0)
    grad_inner = slope_ref[...].astype(FULL) * right_product(grad_low_ref[...], outer_ref[...])
    bias_ref[...] = column_sum(grad_inner)
    grad_inner = grad_inner.astype(LOW)
    for k in range(size):

        @pl.when(step // steps == (k + size - 1) % size)
        def _():
            inners[k][...] = grad_inner

    part = right_product(grad_inner, inner_ref[...])

    @pl.when(step == 0)
    def _():
        acc[...] = part

    @pl.when(step > 0)
    def _():
        acc[...] += part

    @pl.when(step == pl.num_programs(0) - 1)
    def _():
        gain = gain_ref[...].astype(FULL)

        def some(block, sums):
            lines = pl.ds(pl.multiple_of(block * LINES, LINES), LINES)
            grad = grad_ref[lines, :] + acc[lines, :]
            unit = unit_ref[lines, :]
            one = norm_pull(unit, factor_ref[lines, :], gain, grad)
            one_ref[lines, :] = one
            low = one.astype(LOW)
            low_ref[lines, :] = low
            keep[lines, :] = low
            more = (column_sum(grad * unit), column_sum(grad), column_sum(one))
            return tuple(x + y for x, y in zip(sums, more))

        sums = lax.fori_loop(0, acc.shape[0] // LINES, some, (jnp.zeros_like(gain),) * 3)
        for k in range(3):
            sums_ref[k : k + 1, :] = sums[k]
        low = keep[...]
        for k in range(size):
            spot = pl.multiple_of((place_ref[1] ^ k) * share, 128)
            cuts[k][...] = keep[:, pl.ds(spot, share)]
            mixes[k][...] = right_product(low, out_weights[k][...]).astype(LOW)


def feed_back(
    places, size, grad_low, grad, slope, inner_weight, outer_weight, unit, factor, small, out_weights
):
    rows, width = grad_low.shape
    hidden = inner_weight.shape[1]
    part = hidden // size
    tile = min(512, part)
    steps = part // tile
    share = width // size

    def spot(i, s):
        return (s[1] ^ ((i // steps + 1) % size)) * steps + i % steps

    def own(k):
        start = ((k + size - 1) % size) * steps
        return pl.BlockSpec((rows, tile), lambda i, s: (0, jnp.clip(i - start, 0, steps - 1)))

    whole = pl.BlockSpec((rows, width), lambda i, s: (0, 0))
    return pl.pallas_call(
        functools.partial(feed_back_kernel, size, steps, share),
        grid_spec=pltpu.PrefetchScalarGridSpec(
            num_scalar_prefetch=1,
            grid=(hidden // tile,),
            in_specs=[
                whole,
                whole,
                pl.BlockSpec((rows, tile), lambda i, s: (0, spot(i, s))),
                pl.BlockSpec((width, tile), lambda i, s: (0, spot(i, s))),
                pl.BlockSpec((tile, width), lambda i, s: (spot(i, s), 0)),
                whole,
                pl.BlockSpec((rows, 1), lambda i, s: (0, 0)),
                row_of(1, width),
            ]
            + [pl.BlockSpec((share, width), lambda i, s: (0, 0))] * size,
            out_specs=[own(k) for k in range(size)]
            + [
                pl.BlockSpec((1, tile), lambda i, s: (0, spot(i, s))),
                whole,
                whole,
                pl.BlockSpec((8, width), lambda i, s: (0, 0)),
            ]
            + [pl.BlockSpec((rows, share), lambda i, s: (0, 0))] * (2 * size),
            scratch_shapes=[pltpu.VMEM((rows, width), FULL), pltpu.VMEM((rows, width), LOW)],
        ),
        out_shape=[jax.ShapeDtypeStruct((rows, part), LOW)] * size
        + [
            jax.ShapeDtypeStruct((1, hidden), FULL),
            jax.ShapeDtypeStruct((rows, width), FULL),
            jax.ShapeDtypeStruct((rows, width), LOW),
            jax.ShapeDtypeStruct((8, width), FULL),
        ]
        + [jax.ShapeDtypeStruct((rows, share), LOW)] * (2 * size),
        compiler_params=params(60),
        cost_estimate=CHEAP,
        name="feed_back",
    )(places, grad_low, grad, slope, inner_weight, outer_weight, unit, factor, small, *out_weights)


def back_kernel(size, place_ref, grad_ref, masked_ref, *refs):
    threes, weights, out_ref = refs[:size], refs[size:-1], refs[-1]
    total = grad_ref[...]
    for k in range(size):
        for n in range(3):
            total = total + right_product(threes[k][n], weights[3 * k + n][...])
    out_ref[...] = jnp.where(masked_ref[...] > 0.0, 0.0, total).astype(LOW)


def input_back(places, threes, weights, grad, masked):
    size = len(threes)
    rows, width = grad.shape
    share = threes[0].shape[2]
    tile = min(256, rows)
    line = pl.BlockSpec((tile, width), lambda i, s: (i, 0))
    return pl.pallas_call(
        functools.partial(back_kernel, size),
        grid_spec=pltpu.PrefetchScalarGridSpec(
            num_scalar_prefetch=1,
            grid=(rows // tile,),
            in_specs=[line, pl.BlockSpec((tile, 1), lambda i, s: (i, 0))]
            + [pl.BlockSpec((3, tile, share), lambda i, s: (0, i, 0))] * size
            + [
                pl.BlockSpec((width, share), lambda i, s, k=k: (0, s[1] ^ k))
                for k in range(size)
                for _ in range(3)
            ],
            out_specs=line,
        ),
        out_shape=jax.ShapeDtypeStruct((rows, width), LOW),
        compiler_params=params(),
        cost_estimate=CHEAP,
        name="input_back",
    )(places, grad, masked, *threes, *(list(weights) * size))


def part_orders(bits):
    if bits < 3:
        return [(list(range(bits)),) * 2] * 2
    rest = list(range(3, bits))
    return [([0, 2, 1] + rest, [1, 0, 2] + rest), ([2, 1, 0] + rest,) * 2]


def part_depths(lines, weights):
    tiles = lines // 16
    first = round(tiles * weights[0] / sum(weights))
    return [16 * first, 16 * (tiles - first)]


def offset_at(position, order):
    return sum(((position >> (len(order) - 1 - n)) & 1) << order[n] for n in range(len(order)))


def weight_kernel(layout, flips, teams, lines, parts, members, bias, extra, place_ref, *refs):
    number = sum(layout)
    lefts, rights = refs[:number], refs[number : number + members]
    count = 2 * len(parts)
    singles, refs = refs[number + members : number + members + extra], refs[number + members + extra :]
    outs, scratch = refs[:count], refs[count:]
    flipped = scratch[:members] if flips else lefts
    total = scratch[members if flips else 0]
    step = pl.program_id(0)
    team = place_ref[0]
    half = teams // 2

    def block_at(position, order):
        even, odd = (offset_at(position, o) for o in order)
        return team ^ (even if even == odd else jnp.where(place_ref[1] % 2 == 0, even, odd))

    if flips:

        @pl.when(step == 0)
        def _():
            spot = 0
            for member in range(members):
                start = 0
                for _ in range(layout[member]):
                    wide = lefts[spot].shape[1]
                    flipped[member][start : start + wide, :] = lefts[spot][...].T
                    start, spot = start + wide, spot + 1

    def right(member):
        ref = rights[member]
        return ref[0] if len(ref.shape) == 3 else ref[...]

    def multiply():
        acc = product(flipped[0][...], right(0))
        for member in range(1, members):
            acc = acc + product(flipped[member][...], right(member))
        total[...] = acc.astype(LOW)
        for k, (order, start, deep) in enumerate(parts):
            for position in range(teams):
                line = pl.multiple_of(block_at(position, order) * lines + start, 16)
                outs[2 * k + position // half][position % half, 0] = total[pl.ds(line, deep), :]

    if not bias and not extra:
        multiply()
        return

    chunks = pl.num_programs(0) - 1
    last = outs[count - 2 : count]
    order = parts[-1][0]
    if extra:
        vectors = scratch[-1]

        @pl.when(step < chunks)
        def _():
            multiply()

        @pl.when(step == chunks)
        def _():
            inner = singles[-1].shape[1] // teams
            for row in range(teams):
                for k in range(6):
                    vectors[row : row + 1, k * lines : (k + 1) * lines] = singles[k // 3][
                        k % 3 : k % 3 + 1, row * lines : (row + 1) * lines
                    ]
                vectors[row : row + 1, 6 * lines : 6 * lines + inner] = singles[2][
                    :, row * inner : (row + 1) * inner
                ]
            deep = lax.broadcasted_iota(jnp.int32, (16, CHUNK), 0)
            for position in range(teams):
                row = vectors[pl.ds(block_at(position, order), 1), :]
                value = jnp.zeros((16, CHUNK), FULL)
                for k in range(vectors.shape[1] // CHUNK):
                    piece = jnp.broadcast_to(row[:, k * CHUNK : (k + 1) * CHUNK], (16, CHUNK))
                    value = jnp.where(deep == k, piece, value)
                last[position // half][position % half, 0, 0:16, :] = value.astype(LOW)

        return

    sums, vectors = scratch[-2:]

    @pl.when(step < chunks)
    def _():
        multiply()
        sums[pl.ds(step, 1), :] = sum(column_sum(right(m).astype(FULL)) for m in range(members))

    @pl.when(step == chunks)
    def _():
        own = vectors.shape[0]
        for k, first in enumerate(bias[0]):
            for team_row in range(own):
                chunk, lane = divmod(first + team_row * lines, CHUNK)
                vectors[team_row : team_row + 1, k * lines : (k + 1) * lines] = sums[
                    chunk : chunk + 1, lane : lane + lines
                ]
        wide = vectors.shape[1]
        for position in range(teams):
            local = block_at(position, order) - place_ref[1] * (teams // members) - bias[1]
            inside = jnp.logical_and(local >= 0, local < own)
            row = vectors[pl.ds(jnp.clip(local, 0, own - 1), 1), :]
            row = jnp.where(inside, row, 0.0)
            last[position // half][position % half, 0, 0:16, 0:wide] = jnp.broadcast_to(
                row, (16, wide)
            ).astype(LOW)


def weight_grad(name, lefts, flips, rights, places, teams, width, weights, bias=(), sums=(), mib=60):
    members = len(lefts)
    rows = rights[0][1][-2]
    flat = [item for member in lefts for item in member]
    high = sum(a.shape[1] for a, _ in lefts[0]) if flips else lefts[0][0][0].shape[0]
    lines = high // teams
    orders = part_orders(teams.bit_length() - 1)
    parts, start = [], 0
    for order, deep in zip(orders, part_depths(lines, weights)):
        if deep:
            parts.append((order, start, deep))
        start += deep
    half = teams // 2
    chunks = width // CHUNK
    own = bias[2] if bias else 0
    if sums:
        sums_wide = 6 * lines + sums[-1].shape[1] // teams
        sums_wide = -(-sums_wide // CHUNK) * CHUNK
    counts = [chunks] * len(parts)
    if bias or sums:
        counts[-1] += 1
    outs = pl.pallas_call(
        functools.partial(
            weight_kernel, [len(m) for m in lefts], flips, teams, lines, parts, members, bias, len(sums)
        ),
        grid_spec=pltpu.PrefetchScalarGridSpec(
            num_scalar_prefetch=1,
            grid=(counts[-1],),
            in_specs=[
                pl.BlockSpec(
                    (rows, array.shape[1]) if flips else array.shape, lambda i, s, b=block: (b, 0)
                )
                for array, block in flat
            ]
            + [
                pl.BlockSpec(shape, lambda i, s, f=index: f(jnp.minimum(i, chunks - 1), s))
                for _, shape, index in rights
            ]
            + [pl.BlockSpec(a.shape, lambda i, s: (0, 0)) for a in sums],
            out_specs=[
                pl.BlockSpec(
                    (half, 1, p[2], CHUNK), lambda i, s, c=c: (0, jnp.minimum(i, c - 1), 0, 0)
                )
                for p, c in zip(parts, counts)
                for _ in range(2)
            ],
            scratch_shapes=[pltpu.VMEM((high, rows), LOW)] * (members if flips else 0)
            + [pltpu.VMEM((high, CHUNK), LOW)]
            + (
                [pltpu.VMEM((chunks, CHUNK), FULL), pltpu.VMEM((own, len(bias[0]) * lines), FULL)]
                if bias
                else [pltpu.VMEM((teams, sums_wide), FULL)] if sums else []
            ),
        ),
        out_shape=[
            jax.ShapeDtypeStruct((half, c, p[2], CHUNK), LOW)
            for p, c in zip(parts, counts)
            for _ in range(2)
        ],
        compiler_params=params(mib),
        cost_estimate=CHEAP,
        name="weight_grad",
    )(places, *[array for array, _ in flat], *[array for array, _, _ in rights], *sums)
    made = []
    for k, (order, start, deep) in enumerate(parts):
        near, far = (o.reshape(half, counts[k] * deep, CHUNK) for o in outs[2 * k : 2 * k + 2])
        segments = [(name, start, deep, c) for c in range(chunks)]
        if counts[k] > chunks:
            segments.append(("bias", 0, deep, 0))
        made.append(dict(order=order, near=near, far=far, segments=segments))
    return made


def fold_kernel(counts, *refs):
    total = 4 * sum(counts)
    outs = refs[total:]
    spot = 0
    for k, count in enumerate(counts):
        start = 0
        for _ in range(count):
            near_low, near_high, came_low, came_high = refs[spot : spot + 4]
            deep = near_low.shape[1]
            rows = slice(start, start + deep)
            outs[2 * k][:, rows] = (near_low[...].astype(FULL) + came_low[...].astype(FULL)).astype(LOW)
            outs[2 * k + 1][:, rows] = (
                near_high[...].astype(FULL) + came_high[...].astype(FULL)
            ).astype(LOW)
            start, spot = start + deep, spot + 4


def fold(*groups):
    orders = []
    for group in groups:
        for part in group:
            if part["order"] not in orders:
                orders.append(part["order"])
    merged = [[p for g in groups for p in g if p["order"] == order] for order in orders]
    half = merged[0][0]["near"].shape[0] // 2
    operands, in_specs, out_specs, out_shape, counts = [], [], [], [], []
    for parts in merged:
        rows = 0
        for part in parts:
            deep = part["near"].shape[1]
            rows += deep
            low = pl.BlockSpec((1, deep, CHUNK), lambda i: (i, 0, 0))
            high = pl.BlockSpec((1, deep, CHUNK), lambda i: (half + i, 0, 0))
            operands += [part["near"], part["near"], part["came"], part["came"]]
            in_specs += [low, high, low, high]
        counts.append(len(parts))
        out_specs += [pl.BlockSpec((1, rows, CHUNK), lambda i: (i, 0, 0))] * 2
        out_shape += [jax.ShapeDtypeStruct((half, rows, CHUNK), LOW)] * 2
    outs = pl.pallas_call(
        functools.partial(fold_kernel, counts),
        grid=(half,),
        in_specs=in_specs,
        out_specs=out_specs,
        out_shape=out_shape,
        compiler_params=params(60 if len(operands) > 16 else 40),
        cost_estimate=CHEAP,
        name="fold",
    )(*operands)
    return [
        dict(
            order=tuple(o[1:] for o in parts[0]["order"]),
            near=outs[2 * k],
            far=outs[2 * k + 1],
            segments=[s for p in parts for s in p["segments"]],
        )
        for k, parts in enumerate(merged)
    ]


def final_kernel(layouts, plain, settled, size, lines, place_ref, *refs):
    count = len(layouts)
    outs = refs[2 * count :]
    targets = dict(zip(plain, outs))
    pieces = outs[len(plain) : len(plain) + size]
    if settled:
        targets[None] = outs[-1]
    biases = []
    for k, layout in enumerate(layouts):
        spot = 0
        for name, start, deep, column in layout:
            rows = slice(spot, spot + (16 if name == "bias" else deep))
            value = refs[2 * k][0, rows].astype(FULL) + refs[2 * k + 1][0, rows].astype(FULL)
            spot += deep
            if name == "bias":
                biases.append(value[0:8])
                continue
            targets[name][start : start + deep, column * CHUNK : (column + 1) * CHUNK] = value
    if settled:
        for piece in pieces if biases else ():
            piece[lines : lines + 8, 0:CHUNK] = sum(biases)
        for k in range(size):
            line = pl.multiple_of((place_ref[1] ^ k) * lines, 8)
            pieces[k][0:lines, :] = targets[None][pl.ds(line, lines), :]


def final(parts, places, size, lines, plain, settled):
    layouts, wide, more = [], 0, 0
    for part in parts:
        layout = []
        for name, start, deep, column in part["segments"]:
            if name in plain or name == "bias":
                more = 8 if name == "bias" else more
                layout.append((name, start, deep, column))
            else:
                column += settled[name] // CHUNK
                wide = max(wide, (column + 1) * CHUNK)
                layout.append((None, start, deep, column))
        layouts.append(layout)
    names = list(plain)
    shapes = [jax.ShapeDtypeStruct(plain[n], FULL) for n in names]
    if settled:
        shapes += [jax.ShapeDtypeStruct((lines + more, wide), FULL)] * size
    outs = pl.pallas_call(
        functools.partial(final_kernel, layouts, names, bool(settled), size, lines),
        in_specs=[pl.BlockSpec(memory_space=pltpu.SMEM)]
        + [pl.BlockSpec(memory_space=pltpu.VMEM)] * (2 * len(parts)),
        out_specs=[pl.BlockSpec(memory_space=pltpu.VMEM)] * len(shapes),
        out_shape=shapes,
        scratch_shapes=[pltpu.VMEM((size * lines, wide), FULL)] if settled else [],
        compiler_params=params(32),
        cost_estimate=CHEAP,
        name="final",
    )(places, *[p[n] for p in parts for n in ("near", "came")])
    return dict(zip(names, outs)), outs[len(names) :]


def tie(value, *others):
    return lax.optimization_barrier((value, others))[0]


def per_device(
    inputs,
    mask_pos,
    mask_count,
    replace,
    cotangent,
    query_weight,
    query_bias,
    key_weight,
    value_weight,
    value_bias,
    out_weight,
    out_bias,
    first_gain,
    first_shift,
    inner_weight,
    inner_bias,
    outer_weight,
    outer_bias,
    second_gain,
    second_shift,
):
    groups, rows, width = inputs.shape
    hidden = inner_weight.shape[1]
    blocks = lax.axis_size("blk")
    number = lax.axis_size("dp") * blocks
    size = blocks // groups
    piece = rows // size
    own_rows = blocks * piece
    teams = number // size
    bits = teams.bit_length() - 1
    place = lax.axis_index("blk")
    flat = lax.axis_index("dp") * blocks + place
    sequence = place // size
    rank = place % size
    team = flat // size
    share = width // size
    hidden_share = hidden // size
    others = range(1, size)

    def hop(array, mask):
        return lax.ppermute(array, BOTH, [(i, i ^ mask) for i in range(number)])

    def cut(array, who, count, axis):
        return lax.dynamic_slice_in_dim(array, who * count, count, axis=axis)

    def swap(make):
        return [make(rank)] + [hop(make(rank ^ k), k) for k in others]

    def absolute(pieces, axis):
        if size == 2:
            first = rank == 0
            return jnp.concatenate(
                [jnp.where(first, pieces[0], pieces[1]), jnp.where(first, pieces[1], pieces[0])],
                axis=axis,
            )
        stacked = jnp.stack(pieces)
        return jnp.concatenate(
            [lax.dynamic_index_in_dim(stacked, q ^ rank, 0, keepdims=False) for q in range(size)],
            axis=axis,
        )

    def send(parts):
        return [
            dict(
                p,
                came=lax.ppermute(
                    p["far"],
                    BOTH,
                    [(i, i ^ (size << p["order"][i % size % 2][0])) for i in range(number)],
                ),
            )
            for p in parts
        ]

    def far(parts):
        return [p["far"] for p in parts]

    def sync(values, *groups):
        values, came = lax.optimization_barrier((values, [[p["came"] for p in g] for g in groups]))
        made = [[dict(p, came=c) for p, c in zip(g, cs)] for g, cs in zip(groups, came)]
        return (values, *made)

    def after(parts, *values):
        came = lax.optimization_barrier(([p["came"] for p in parts], values))[0]
        return [dict(p, came=c) for p, c in zip(parts, came)]

    arrived = lax.all_to_all(inputs.reshape(blocks, piece, width), "blk", 0, 0)
    lane = jnp.arange(own_rows, dtype=jnp.int32)
    positions = (lane // piece) * rows + rank * piece + lane % piece
    swapped, seeded, masked = masked_rows(
        sequence.reshape(1).astype(jnp.int32), mask_count, positions.reshape(-1, 1), mask_pos, replace, cotangent
    )
    places = jnp.stack([team, rank]).astype(jnp.int32)
    heads_weight = jnp.concatenate(
        [cut(w, rank, share, 1) for w in (query_weight, key_weight, value_weight)], axis=1
    )
    heads_bias = jnp.concatenate(
        [
            cut(query_bias, rank, share, 0),
            jnp.zeros((share,), LOW),
            cut(value_bias, rank, share, 0),
        ]
    )
    out_weights = [cut(out_weight, rank ^ k, share, 0) for k in range(size)]

    small = (out_bias, first_gain, first_shift, outer_bias, second_gain, second_shift)
    small = jnp.stack(small).astype(FULL).reshape(-1, 1, width)
    inner_line = inner_bias.reshape(1, -1)
    arrived = tie(arrived, small, inner_line, swapped, seeded, heads_weight, heads_bias, out_weights, masked)
    current = jnp.where(masked > 0.0, swapped, arrived.reshape(own_rows, width))
    currents = [current] + [hop(current, k) for k in others]
    joined = product(jnp.concatenate(currents, axis=0), heads_weight) + heads_bias.astype(FULL)
    joined = joined.astype(LOW)
    mixed_heads, log_total = attention_forward(joined)

    mixed_parts = mixed_heads.reshape(size, own_rows, share)
    mixed_here = [mixed_parts[0]] + [hop(mixed_parts[k], k) for k in others]
    mixed_away = []
    for k in others:
        row = []
        for q in range(size):
            if q == 0:
                row.append((mixed_heads, k))
            else:
                row.append((hop(mixed_parts[k ^ q], q), 0))
        mixed_away.append(row)

    first, first_flip, first_low, unit_one, factor_one = first_half(
        current,
        [(m, share) for m in [mixed_heads] + mixed_here[1:]],
        out_weights,
        small,
    )
    firsts = [first_flip] + [hop(first_flip, k) for k in others]
    fed = feed_forward(
        places, size, number, first_low, first, seeded, inner_weight, inner_line, outer_weight, small
    )
    actives = [fed[0]] + [hop(fed[k], k) for k in others]
    slope, result, grad_two, grad_two_low, second_sums = fed[size:]

    def home(array):
        return lax.all_to_all(array.reshape(blocks, piece, width), "blk", 0, 0)

    def wide(array):
        return array.reshape(groups, rows, width).astype(FULL)

    grad_twos = [grad_two_low] + [hop(grad_two_low, k) for k in others]

    def plain(array):
        return (array, (own_rows, CHUNK), lambda i, s: (0, i))

    layer_out = home(result)
    back = feed_back(
        places, size, grad_two_low, grad_two, slope, inner_weight, outer_weight, unit_one, factor_one,
        small, out_weights,
    )
    back, layer_out, grad_twos, actives = lax.optimization_barrier((back, layer_out, grad_twos, actives))
    layer_out = wide(layer_out)
    grad_inners = [back[0]] + [hop(back[k], k) for k in others]
    inner_bias_grad, grad_one, grad_one_low, first_sums = back[size : size + 4]
    grad_ones = [back[size + 4]] + [hop(back[size + 4 + k], k) for k in others]
    grad_mixed = back[2 * size + 4 : 3 * size + 4]
    grad_mixed = [grad_mixed[0]] + [hop(grad_mixed[k], k) for k in others]
    outer_parts = weight_grad(
        "outer", [[(a, 0)] for a in actives], False, [plain(g) for g in grad_twos], places, teams, width,
        (2, 1),
    )
    grad_ones[0] = tie(grad_ones[0], far(outer_parts))
    outer_parts = send(outer_parts)
    out_parts = weight_grad(
        "out", [[(m, 0) for m in [mixed_heads] + mixed_here[1:]]] + mixed_away, True,
        [plain(g) for g in grad_ones],
        jnp.stack([team ^ (rank * (teams // size)), rank]).astype(jnp.int32), teams, share, (1, 0),
    )
    grad_inners[0] = tie(grad_inners[0], far(out_parts))
    out_parts = send(out_parts)
    inner_parts = weight_grad(
        "inner", [[(f, 0)] for f in firsts], False, [plain(g) for g in grad_inners], places, teams,
        hidden_share, (3, 1), sums=(first_sums, second_sums, inner_bias_grad),
    )
    fars, outer_parts = sync(far(inner_parts), outer_parts)
    inner_parts = send([dict(p, far=f) for p, f in zip(inner_parts, fars)])
    grad_mixed[0] = tie(grad_mixed[0], fars)

    pairs = share // (2 * HEAD)
    number_of = 2 if share // 2 % CHUNK == 0 else 1
    count = pairs // number_of
    part = share // number_of
    chunks = part // CHUNK
    team_rows = teams // size // number_of

    def three_grad(three, group):
        return weight_grad(
            f"three{group}", [[(c, 0)] for c in currents], True,
            [
                (
                    three,
                    (1, own_rows, CHUNK),
                    lambda i, s, k=k: (i // chunks, k, group * chunks + i % chunks),
                )
                for k in range(size)
            ],
            places, teams, 3 * part, (3, 1), ((0, 2 * part), group * team_rows, team_rows), mib=40,
        )

    three = attention_backward(joined, grad_mixed, mixed_heads, log_total, 0, count)
    late = []
    if number_of == 2:
        late = three_grad(three, 0)
        three = tie(three, far(late))
        late = send(late)
    three, inner_parts, out_parts = sync(three, inner_parts, out_parts)
    early = fold(outer_parts, inner_parts, out_parts)
    three = tie(three, far(early))
    early = send(early)
    if number_of == 2:
        three = attention_backward(joined, grad_mixed, mixed_heads, log_total, count, count, three)
    three, early, late = sync(three, early, late)
    early = fold(early)
    three = tie(three, far(early))
    threes = [three] + [hop(three[:, k * own_rows : (k + 1) * own_rows], k) for k in others]
    early = send(early)
    more = three_grad(three, number_of - 1)
    (threes, fars), early = sync((threes, far(more)), early)
    more = send([dict(p, far=f) for p, f in zip(more, fars)])
    early = fold(early)
    threes[0] = tie(threes[0], far(early))
    early_one, early_two = send(early[:1]), early[1:]
    input_grad = input_back(places, threes, (query_weight, key_weight, value_weight), grad_one, masked)
    home_grad = home(input_grad)
    _, more, early_one = sync((input_grad, layer_out), more, early_one)
    late = fold(late, more) if late else fold(more)
    for p, f in zip(early_two, tie(far(early_two), far(late))):
        p["far"] = f
    late, early_two = send(late), send(early_two)
    while len((early_one + early_two)[0]["order"][0]) > 1:
        early_one, early_two = send(fold(early_one + early_two)), []

    lines = width // number
    _, late, early_two = sync(far(late), late, early_two)
    if len(late[0]["order"][0]) > 1:
        late = fold(late)
        early_one = [dict(p, near=tie(p["near"], far(late))) for p in early_one]
        home_grad = tie(home_grad, far(late))
        late = send(late)
    made, early = final(
        early_one + early_two, places, size, lines, {"outer": (hidden // number, width)},
        {"inner": 0, "out": hidden_share},
    )
    outer_weight_grad = made["outer"]
    early_away = [hop(early[k], k) for k in others]
    input_grad = wide(home_grad)
    late = after(late, input_grad, outer_weight_grad)
    while len(late[0]["order"][0]) > 1:
        late = fold(late)
        early_away = tie(early_away, far(late))
        late = send(late)
    early = [early[0]] + early_away
    inner_weight_grad = absolute([e[:lines, :hidden_share] for e in early], 1)
    out_weight_grad = absolute([e[:lines, hidden_share:] for e in early], 1)
    team_lines, team_hidden = width // teams, hidden // teams
    flat_rows = -(-(6 * team_lines + team_hidden) // CHUNK)
    flat = sum(e[lines : lines + flat_rows, :CHUNK] for e in early).reshape(1, -1)
    six = cut(flat[:, : 6 * team_lines].reshape(6, team_lines), rank, lines, 1)
    inner_bias_grad = cut(
        flat[:, 6 * team_lines : 6 * team_lines + team_hidden], rank, team_hidden // size, 1
    )
    _, late = final(
        after(late, inner_weight_grad, out_weight_grad), places, size, lines, {},
        {f"three{g}": g * 3 * part for g in range(number_of)},
    )
    late = [late[0]] + [hop(late[k], k) for k in others]

    def three_columns(e, k):
        cuts = [
            e[:lines, (g * 3 + k) * part : (g * 3 + k + 1) * part] for g in range(number_of)
        ]
        return jnp.concatenate(cuts, axis=1)

    three_grads = [absolute([three_columns(e, k) for e in late], 1) for k in range(3)]
    biases = sum(e[lines, : 2 * team_lines] for e in late).reshape(2, team_lines)
    biases = cut(biases, rank, lines, 1)
    spots = [biases[0], biases[1], six[2], six[0], six[1], inner_bias_grad[0], six[5], six[3], six[4]]

    return (
        layer_out,
        input_grad,
        three_grads[0],
        spots[0],
        three_grads[1],
        three_grads[2],
        spots[1],
        out_weight_grad,
        spots[2],
        spots[3],
        spots[4],
        inner_weight_grad,
        spots[5],
        outer_weight_grad,
        spots[6],
        spots[7],
        spots[8],
    )


def solution(mesh):
    split = P("dp", "blk", None)
    row = P("dp")
    both = P(BOTH)
    in_specs = (split, row, row, row, row) + (P(),) * 15
    out_specs = (split, split) + (both,) * 15
    return jax.shard_map(
        per_device, mesh=mesh, in_specs=in_specs, out_specs=out_specs, check_vma=False
    )
```

```python
import functools
import math

import jax
import jax.numpy as jnp
from jax import lax
from jax.experimental import pallas as pl
from jax.experimental.pallas import tpu as pltpu
from jax.sharding import PartitionSpec as P

HEAD = 64
EPSILON = 1e-05
BOTH = ("dp", "blk")
LOW = jnp.bfloat16
FULL = jnp.float32
CHUNK = 256
BACK = 512
LINES = 128
CHEAP = pl.CostEstimate(flops=1, bytes_accessed=1, transcendentals=0)


def product(left, right):
    return jnp.dot(left, right, preferred_element_type=FULL)


def right_product(left, right):
    return lax.dot_general(left, right, (((1,), (1,)), ((), ())), preferred_element_type=FULL)


def norm_stats(hidden):
    center = hidden - jnp.mean(hidden, axis=-1, keepdims=True)
    spread = jnp.mean(center * center, axis=-1, keepdims=True)
    factor = lax.rsqrt(spread + EPSILON)
    return center * factor, factor


def norm_pull(unit, factor, gain, grad):
    scaled = grad * gain
    inner = jnp.mean(scaled, axis=-1, keepdims=True)
    along = jnp.mean(scaled * unit, axis=-1, keepdims=True)
    return factor * (scaled - inner - unit * along)


def column_sum(array):
    return jnp.sum(array, axis=0, keepdims=True)


def gelu_parts(inner):
    bell = jnp.exp(-0.5 * inner * inner)
    t = 1.0 / (1.0 + (0.3275911 * math.sqrt(0.5)) * jnp.abs(inner))
    poly = 0.5 * 1.061405429
    for c in (-1.453152027, 1.421413741, -0.284496736, 0.254829592):
        poly = poly * t + 0.5 * c
    tail = poly * t * bell
    below = jnp.where(inner >= 0.0, 1.0 - tail, tail)
    return inner * below, below + inner * bell * (1.0 / math.sqrt(2.0 * math.pi))


def params(mib=36):
    return pltpu.CompilerParams(vmem_limit_bytes=mib << 20)


def forward_kernel(query_ref, key_ref, value_ref, mixed_ref, log_ref):
    lane = lax.broadcasted_iota(jnp.int32, (1, 2 * HEAD), 1)
    query = query_ref[...] * LOW(1.0 / math.sqrt(HEAD))
    key = key_ref[...]
    value_t = value_ref[...].T
    outs = []
    for head in range(2):
        mine = (lane < HEAD) if head == 0 else (lane >= HEAD)
        scores = right_product(key, jnp.where(mine, query, LOW(0)))
        highest = jnp.max(scores, axis=0, keepdims=True)
        expon = jnp.exp(scores - highest)
        total = jnp.sum(expon, axis=0, keepdims=True)
        out = product(value_t[head * HEAD : (head + 1) * HEAD], expon.astype(LOW))
        outs.append(out * (1.0 / total))
        log_ref[0, head : head + 1, :] = highest + jnp.log(total)
    mixed_ref[...] = jnp.concatenate(outs, axis=0).T.astype(LOW)


def backward_kernel(
    members, query_ref, key_ref, value_ref, mixed_ref, log_ref, *refs
):
    grads = refs[:members]
    out_ref, key_sum, value_sum = refs[-3:]
    step = pl.program_id(1)

    @pl.when(step == 0)
    def _():
        key_sum[...] = jnp.zeros_like(key_sum)
        value_sum[...] = jnp.zeros_like(value_sum)

    scale = 1.0 / math.sqrt(HEAD)
    lane = lax.broadcasted_iota(jnp.int32, (1, 2 * HEAD), 1)
    query = query_ref[...] * LOW(scale)
    key = key_ref[...]
    value = value_ref[...]
    tile = query.shape[0]
    together = tile // grads[0].shape[0]
    pieces = []
    for k in range(together):
        piece = grads[k][...]
        for other in range(k + together, members, together):
            piece = jnp.where(step == other // together, grads[other][...], piece)
        pieces.append(piece)
    grad = jnp.concatenate(pieces, axis=0)
    both = (grad.astype(FULL) * mixed_ref[...].astype(FULL)).T
    key_t = key.T
    outs = []
    for head in range(2):
        mine = (lane < HEAD) if head == 0 else (lane >= HEAD)
        own = slice(head * HEAD, (head + 1) * HEAD)
        delta = jnp.sum(both[own], axis=0, keepdims=True)
        query_one = jnp.where(mine, query, LOW(0))
        grad_one = jnp.where(mine, grad, LOW(0))
        shares = jnp.exp(right_product(key, query_one) - log_ref[0, head : head + 1, :])
        grad_shares = right_product(value, grad_one)
        grad_scores = (shares * (grad_shares - delta)).astype(LOW)
        value_sum[...] += product(shares.astype(LOW), grad_one)
        key_sum[...] += product(grad_scores, query_one)
        outs.append(product(key_t[own], grad_scores))
    spot = pl.ds(pl.multiple_of(step * tile, tile), tile)
    out_ref[0, spot, :] = (jnp.concatenate(outs, axis=0).T * scale).astype(LOW)

    @pl.when(step == pl.num_programs(1) - 1)
    def _():
        out_ref[1] = key_sum[...].astype(LOW)
        out_ref[2] = value_sum[...].astype(LOW)


def attention_forward(joined):
    rows, wide = joined.shape
    share = wide // 3
    pairs = share // (2 * HEAD)
    tile = min(1024, rows)

    def whole(offset):
        return pl.BlockSpec((rows, 2 * HEAD), lambda p, i: (0, offset + p))

    line = pl.BlockSpec((tile, 2 * HEAD), lambda p, i: (i, p))
    return pl.pallas_call(
        forward_kernel,
        grid=(pairs, rows // tile),
        in_specs=[line, whole(pairs), whole(2 * pairs)],
        out_specs=[line, pl.BlockSpec((1, 2, tile), lambda p, i: (p, 0, i))],
        out_shape=[
            jax.ShapeDtypeStruct((rows, share), LOW),
            jax.ShapeDtypeStruct((pairs, 2, rows), FULL),
        ],
        compiler_params=params(40),
        cost_estimate=CHEAP,
        name="attention_forward",
    )(joined, joined, joined)


def attention_backward(joined, grad_mixed, mixed, log_total, first, count, previous=None):
    rows, wide = joined.shape
    share = wide // 3
    pairs = share // (2 * HEAD)
    members = len(grad_mixed)
    own_rows = rows // members
    tile = own_rows * max(1, BACK // own_rows)

    def whole(offset):
        return pl.BlockSpec((rows, 2 * HEAD), lambda p, i: (0, offset + p))

    line = pl.BlockSpec((tile, 2 * HEAD), lambda p, i: (i, first + p))
    grad_line = pl.BlockSpec((own_rows, 2 * HEAD), lambda p, i: (0, first + p))
    more = [] if previous is None else [previous]
    return pl.pallas_call(
        functools.partial(backward_kernel, members),
        grid=(count, rows // tile),
        in_specs=[
            line,
            whole(pairs + first),
            whole(2 * pairs + first),
            line,
            pl.BlockSpec((1, 2, tile), lambda p, i: (first + p, 0, i)),
        ]
        + [grad_line] * members
        + [pl.BlockSpec(memory_space=pl.ANY)] * len(more),
        out_specs=pl.BlockSpec((3, rows, 2 * HEAD), lambda p, i: (0, 0, first + p)),
        out_shape=jax.ShapeDtypeStruct((3, rows, share), LOW),
        input_output_aliases={5 + members: 0} if more else {},
        scratch_shapes=[pltpu.VMEM((rows, 2 * HEAD), FULL)] * 2,
        compiler_params=params(40),
        cost_estimate=CHEAP,
        name="attention_backward",
    )(joined, joined, joined, mixed, log_total, *grad_mixed, *more)


def rows_kernel(sequence_ref, count_ref, position_ref, listed_ref, replace_ref, cotangent_ref, *refs):
    swapped_ref, seeded_ref, masked_ref = refs
    count = count_ref[sequence_ref[0]]
    listed = listed_ref[0]
    live = lax.broadcasted_iota(jnp.int32, listed.shape, 1) < count
    matches = jnp.where(live, listed, -1) == position_ref[...]
    select = matches.astype(FULL)
    masked_ref[...] = jnp.max(select, axis=1, keepdims=True)
    select = select.astype(LOW)
    swapped_ref[...] = product(select, replace_ref[0]).astype(LOW)
    seeded_ref[...] = product(select, cotangent_ref[0]).astype(LOW)


def masked_rows(sequence, mask_count, positions, mask_pos, replace, cotangent):
    rows = positions.shape[0]
    _, slots, width = replace.shape
    line = pl.BlockSpec((1, slots, width), lambda i, s, c: (s[0], 0, 0))
    return pl.pallas_call(
        rows_kernel,
        grid_spec=pltpu.PrefetchScalarGridSpec(
            num_scalar_prefetch=2,
            grid=(1,),
            in_specs=[
                pl.BlockSpec((rows, 1), lambda i, s, c: (0, 0)),
                pl.BlockSpec((1, 1, slots), lambda i, s, c: (s[0], 0, 0)),
                line,
                line,
            ],
            out_specs=[
                pl.BlockSpec((rows, width), lambda i, s, c: (0, 0)),
                pl.BlockSpec((rows, width), lambda i, s, c: (0, 0)),
                pl.BlockSpec((rows, 1), lambda i, s, c: (0, 0)),
            ],
        ),
        out_shape=[
            jax.ShapeDtypeStruct((rows, width), LOW),
            jax.ShapeDtypeStruct((rows, width), LOW),
            jax.ShapeDtypeStruct((rows, 1), FULL),
        ],
        compiler_params=params(),
        cost_estimate=CHEAP,
        name="masked_rows",
    )(sequence, mask_count, positions, mask_pos.reshape(-1, 1, slots), replace, cotangent)


def first_kernel(pieces, current_ref, bias_ref, gain_ref, shift_ref, *refs):
    mixed, weights = refs[:pieces], refs[pieces : 2 * pieces]
    first_ref, flip_ref, low_ref, unit_ref, factor_ref = refs[2 * pieces :]
    total = current_ref[...].astype(FULL) + bias_ref[...].astype(FULL)
    for part, weight in zip(mixed, weights):
        total = total + product(part[...], weight[...])
    unit, factor = norm_stats(total)
    first = unit * gain_ref[...].astype(FULL) + shift_ref[...].astype(FULL)
    first_ref[...] = first
    low = first.astype(LOW)
    low_ref[...] = low
    flip_ref[...] = low.T
    unit_ref[...] = unit
    factor_ref[...] = factor


def row_of(k, width):
    return pl.BlockSpec((None, 1, width), lambda *_: (k, 0, 0))


def first_half(current, mixed, weights, small):
    rows, width = current.shape
    tile = 256
    pieces = len(mixed)
    line = pl.BlockSpec((tile, width), lambda i: (i, 0))
    return pl.pallas_call(
        functools.partial(first_kernel, pieces),
        grid=(rows // tile,),
        in_specs=[line] + [row_of(k, width) for k in (0, 1, 2)]
        + [pl.BlockSpec((tile, block_width), lambda i: (i, 0)) for _, block_width in mixed]
        + [pl.BlockSpec(w.shape, lambda i: (0, 0)) for w in weights],
        out_specs=[
            line,
            pl.BlockSpec((width, tile), lambda i: (0, i)),
            line,
            line,
            pl.BlockSpec((tile, 1), lambda i: (i, 0)),
        ],
        out_shape=[
            jax.ShapeDtypeStruct((rows, width), FULL),
            jax.ShapeDtypeStruct((width, rows), LOW),
            jax.ShapeDtypeStruct((rows, width), LOW),
            jax.ShapeDtypeStruct((rows, width), FULL),
            jax.ShapeDtypeStruct((rows, 1), FULL),
        ],
        compiler_params=params(60),
        cost_estimate=CHEAP,
        name="first_half",
    )(current, small, small, small, *[m for m, _ in mixed], *weights)


def feed_kernel(
    size, unit_rows, place_ref, low_ref, first_ref, seed_ref, inner_ref, inner_bias_ref, outer_ref,
    outer_bias_ref, gain_ref, shift_ref, *refs,
):
    actives = refs[:size]
    slope_ref, result_ref, grad_ref, grad_low_ref, sums_ref, acc, flip, seeds = refs[size:]
    step = pl.program_id(0)
    inner = product(low_ref[...], inner_ref[...]) + inner_bias_ref[...].astype(FULL)
    active, slope = gelu_parts(inner)
    active = active.astype(LOW)
    slope_ref[...] = slope.astype(LOW)
    flip[...] = active.T
    rank = place_ref[1]
    tile = flip.shape[0]
    for k in range(size):
        for q in range(tile // (unit_rows * size)):
            line = pl.multiple_of((q * size + (rank ^ k)) * unit_rows, 16)
            actives[k][q * unit_rows : (q + 1) * unit_rows, :] = flip[pl.ds(line, unit_rows), :]
    part = product(active, outer_ref[...])

    @pl.when(step == 0)
    def _():
        acc[...] = part

    @pl.when(step > 0)
    def _():
        acc[...] += part

    deep = first_ref.shape[0]
    here = pl.ds(pl.multiple_of(step * deep, deep), deep)
    acc[here, :] += first_ref[...]
    seeds[here, :] = seed_ref[...]

    @pl.when(step == pl.num_programs(0) - 1)
    def _():
        gain = gain_ref[...].astype(FULL)
        shift = shift_ref[...].astype(FULL)
        bias = outer_bias_ref[...].astype(FULL)

        def some(block, sums):
            lines = pl.ds(pl.multiple_of(block * LINES, LINES), LINES)
            unit, factor = norm_stats(acc[lines, :] + bias)
            result_ref[lines, :] = (unit * gain + shift).astype(LOW)
            seed = seeds[lines, :].astype(FULL)
            grad = norm_pull(unit, factor, gain, seed)
            grad_ref[lines, :] = grad
            grad_low_ref[lines, :] = grad.astype(LOW)
            more = (column_sum(seed * unit), column_sum(seed), column_sum(grad))
            return tuple(x + y for x, y in zip(sums, more))

        sums = lax.fori_loop(0, acc.shape[0] // LINES, some, (jnp.zeros_like(gain),) * 3)
        for k in range(3):
            sums_ref[k : k + 1, :] = sums[k]


def feed_forward(
    places, size, number, low, first, seeded, inner_weight, inner_bias, outer_weight, small
):
    rows, width = low.shape
    hidden = inner_weight.shape[1]
    tile = 512
    whole = pl.BlockSpec((rows, width), lambda i, s: (0, 0))
    line = pl.BlockSpec((rows * tile // hidden, width), lambda i, s: (i, 0))
    across = pl.BlockSpec((rows, tile), lambda i, s: (0, i))
    return pl.pallas_call(
        functools.partial(feed_kernel, size, hidden // number),
        grid_spec=pltpu.PrefetchScalarGridSpec(
            num_scalar_prefetch=1,
            grid=(hidden // tile,),
            in_specs=[
                whole,
                line,
                line,
                pl.BlockSpec((width, tile), lambda i, s: (0, i)),
                pl.BlockSpec((1, tile), lambda i, s: (0, i)),
                pl.BlockSpec((tile, width), lambda i, s: (i, 0)),
            ]
            + [row_of(k, width) for k in (3, 4, 5)],
            out_specs=[pl.BlockSpec((tile // size, rows), lambda i, s: (i, 0))] * size
            + [across, whole, whole, whole, pl.BlockSpec((8, width), lambda i, s: (0, 0))],
            scratch_shapes=[pltpu.VMEM((rows, width), FULL), pltpu.VMEM((tile, rows), LOW)]
            + [pltpu.VMEM((rows, width), LOW)],
        ),
        out_shape=[jax.ShapeDtypeStruct((hidden // size, rows), LOW)] * size
        + [
            jax.ShapeDtypeStruct((rows, hidden), LOW),
            jax.ShapeDtypeStruct((rows, width), LOW),
            jax.ShapeDtypeStruct((rows, width), FULL),
            jax.ShapeDtypeStruct((rows, width), LOW),
            jax.ShapeDtypeStruct((8, width), FULL),
        ],
        compiler_params=params(60),
        cost_estimate=CHEAP,
        name="feed_forward",
    )(places, low, first, seeded, inner_weight, inner_bias, outer_weight, small, small, small)


def feed_back_kernel(
    size, steps, share, place_ref, grad_low_ref, grad_ref, slope_ref, inner_ref, outer_ref, unit_ref,
    factor_ref, gain_ref, *refs,
):
    out_weights, refs = refs[:size], refs[size:]
    inners = refs[:size]
    bias_ref, one_ref, low_ref, sums_ref = refs[size : size + 4]
    cuts = refs[size + 4 : 2 * size + 4]
    mixes = refs[2 * size + 4 : 3 * size + 4]
    acc, keep, units, weights = refs[3 * size + 4 :]
    step = pl.program_id(0)
    grad_inner = slope_ref[...].astype(FULL) * right_product(grad_low_ref[...], outer_ref[...])
    bias_ref[...] = column_sum(grad_inner)
    grad_inner = grad_inner.astype(LOW)
    for k in range(size):

        @pl.when(step // steps == (k + size - 1) % size)
        def _():
            inners[k][...] = grad_inner

    part = right_product(grad_inner, inner_ref[...])

    @pl.when(step == 0)
    def _():
        acc[...] = part

    @pl.when(step > 0)
    def _():
        acc[...] += part

    deep = grad_ref.shape[0]
    here = pl.ds(pl.multiple_of(step * deep, deep), deep)
    acc[here, :] += grad_ref[...]
    units[here, :] = unit_ref[...]
    deep = out_weights[0].shape[0]
    here = pl.ds(pl.multiple_of(step * deep, deep), deep)
    for k in range(size):
        weights[k, here, :] = out_weights[k][...]

    @pl.when(step == pl.num_programs(0) - 1)
    def _():
        gain = gain_ref[...].astype(FULL)

        def some(block, sums):
            lines = pl.ds(pl.multiple_of(block * LINES, LINES), LINES)
            grad = acc[lines, :]
            unit = units[lines, :]
            one = norm_pull(unit, factor_ref[lines, :], gain, grad)
            one_ref[lines, :] = one
            low = one.astype(LOW)
            low_ref[lines, :] = low
            keep[lines, :] = low
            more = (column_sum(grad * unit), column_sum(grad), column_sum(one))
            return tuple(x + y for x, y in zip(sums, more))

        sums = lax.fori_loop(0, acc.shape[0] // LINES, some, (jnp.zeros_like(gain),) * 3)
        for k in range(3):
            sums_ref[k : k + 1, :] = sums[k]
        low = keep[...]
        for k in range(size):
            spot = pl.multiple_of((place_ref[1] ^ k) * share, 128)
            cuts[k][...] = keep[:, pl.ds(spot, share)]
            mixes[k][...] = right_product(low, weights[k]).astype(LOW)


def feed_back(
    places, size, grad_low, grad, slope, inner_weight, outer_weight, unit, factor, small, out_weights
):
    rows, width = grad_low.shape
    hidden = inner_weight.shape[1]
    part = hidden // size
    tile = min(512, part)
    steps = part // tile
    share = width // size

    def spot(i, s):
        return (s[1] ^ ((i // steps + 1) % size)) * steps + i % steps

    def own(k):
        start = ((k + size - 1) % size) * steps
        return pl.BlockSpec((rows, tile), lambda i, s: (0, jnp.clip(i - start, 0, steps - 1)))

    whole = pl.BlockSpec((rows, width), lambda i, s: (0, 0))
    line = pl.BlockSpec((rows * tile // hidden, width), lambda i, s: (i, 0))
    return pl.pallas_call(
        functools.partial(feed_back_kernel, size, steps, share),
        grid_spec=pltpu.PrefetchScalarGridSpec(
            num_scalar_prefetch=1,
            grid=(hidden // tile,),
            in_specs=[
                whole,
                line,
                pl.BlockSpec((rows, tile), lambda i, s: (0, spot(i, s))),
                pl.BlockSpec((width, tile), lambda i, s: (0, spot(i, s))),
                pl.BlockSpec((tile, width), lambda i, s: (spot(i, s), 0)),
                line,
                pl.BlockSpec((rows, 1), lambda i, s: (0, 0)),
                row_of(1, width),
            ]
            + [pl.BlockSpec((share * tile // hidden, width), lambda i, s: (i, 0))] * size,
            out_specs=[own(k) for k in range(size)]
            + [
                pl.BlockSpec((1, tile), lambda i, s: (0, spot(i, s))),
                whole,
                whole,
                pl.BlockSpec((8, width), lambda i, s: (0, 0)),
            ]
            + [pl.BlockSpec((rows, share), lambda i, s: (0, 0))] * (2 * size),
            scratch_shapes=[
                pltpu.VMEM((rows, width), FULL),
                pltpu.VMEM((rows, width), LOW),
                pltpu.VMEM((rows, width), FULL),
                pltpu.VMEM((size, share, width), LOW),
            ],
        ),
        out_shape=[jax.ShapeDtypeStruct((rows, part), LOW)] * size
        + [
            jax.ShapeDtypeStruct((1, hidden), FULL),
            jax.ShapeDtypeStruct((rows, width), FULL),
            jax.ShapeDtypeStruct((rows, width), LOW),
            jax.ShapeDtypeStruct((8, width), FULL),
        ]
        + [jax.ShapeDtypeStruct((rows, share), LOW)] * (2 * size),
        compiler_params=params(60),
        cost_estimate=CHEAP,
        name="feed_back",
    )(places, grad_low, grad, slope, inner_weight, outer_weight, unit, factor, small, *out_weights)


def back_kernel(size, place_ref, grad_ref, masked_ref, *refs):
    threes, weights, out_ref = refs[:size], refs[size:-1], refs[-1]
    total = grad_ref[...]
    for k in range(size):
        for n in range(3):
            total = total + right_product(threes[k][n], weights[3 * k + n][...])
    out_ref[...] = jnp.where(masked_ref[...] > 0.0, 0.0, total).astype(LOW)


def input_back(places, threes, weights, grad, masked):
    size = len(threes)
    rows, width = grad.shape
    share = threes[0].shape[2]
    tile = min(256, rows)
    line = pl.BlockSpec((tile, width), lambda i, s: (i, 0))
    return pl.pallas_call(
        functools.partial(back_kernel, size),
        grid_spec=pltpu.PrefetchScalarGridSpec(
            num_scalar_prefetch=1,
            grid=(rows // tile,),
            in_specs=[line, pl.BlockSpec((tile, 1), lambda i, s: (i, 0))]
            + [pl.BlockSpec((3, tile, share), lambda i, s: (0, i, 0))] * size
            + [
                pl.BlockSpec((width, share), lambda i, s, k=k: (0, s[1] ^ k))
                for k in range(size)
                for _ in range(3)
            ],
            out_specs=line,
        ),
        out_shape=jax.ShapeDtypeStruct((rows, width), LOW),
        compiler_params=params(),
        cost_estimate=CHEAP,
        name="input_back",
    )(places, grad, masked, *threes, *(list(weights) * size))


def part_orders(bits):
    if bits < 3:
        return [(list(range(bits)),) * 2] * 2
    rest = list(range(3, bits))
    return [([0, 2, 1] + rest, [1, 0, 2] + rest), ([2, 1, 0] + rest,) * 2]


def part_depths(lines, weights):
    tiles = lines // 16
    first = round(tiles * weights[0] / sum(weights))
    return [16 * first, 16 * (tiles - first)]


def offset_at(position, order):
    return sum(((position >> (len(order) - 1 - n)) & 1) << order[n] for n in range(len(order)))


def weight_kernel(layout, flips, teams, lines, parts, members, bias, extra, place_ref, *refs):
    number = sum(layout)
    lefts, rights = refs[:number], refs[number : number + members]
    count = 2 * len(parts)
    singles, refs = refs[number + members : number + members + extra], refs[number + members + extra :]
    outs, scratch = refs[:count], refs[count:]
    flipped = scratch[:members] if flips else lefts
    total = scratch[members if flips else 0]
    step = pl.program_id(0)
    team = place_ref[0]
    half = teams // 2

    def block_at(position, order):
        even, odd = (offset_at(position, o) for o in order)
        return team ^ (even if even == odd else jnp.where(place_ref[1] % 2 == 0, even, odd))

    if flips:

        @pl.when(step == 0)
        def _():
            spot = 0
            for member in range(members):
                start = 0
                for _ in range(layout[member]):
                    wide = lefts[spot].shape[1]
                    flipped[member][start : start + wide, :] = lefts[spot][...].T
                    start, spot = start + wide, spot + 1

    def right(member):
        ref = rights[member]
        return ref[0] if len(ref.shape) == 3 else ref[...]

    def multiply():
        acc = product(flipped[0][...], right(0))
        for member in range(1, members):
            acc = acc + product(flipped[member][...], right(member))
        total[...] = acc.astype(LOW)
        for k, (order, start, deep) in enumerate(parts):
            for position in range(teams):
                line = pl.multiple_of(block_at(position, order) * lines + start, 16)
                outs[2 * k + position // half][position % half, 0] = total[pl.ds(line, deep), :]

    if not bias and not extra:
        multiply()
        return

    chunks = pl.num_programs(0) - 1
    last = outs[count - 2 : count]
    order = parts[-1][0]
    if extra:
        vectors = scratch[-1]

        @pl.when(step < chunks)
        def _():
            multiply()

        @pl.when(step == chunks)
        def _():
            inner = singles[-1].shape[1] // teams
            for row in range(teams):
                for k in range(6):
                    vectors[row : row + 1, k * lines : (k + 1) * lines] = singles[k // 3][
                        k % 3 : k % 3 + 1, row * lines : (row + 1) * lines
                    ]
                vectors[row : row + 1, 6 * lines : 6 * lines + inner] = singles[2][
                    :, row * inner : (row + 1) * inner
                ]
            deep = lax.broadcasted_iota(jnp.int32, (16, CHUNK), 0)
            for position in range(teams):
                row = vectors[pl.ds(block_at(position, order), 1), :]
                value = jnp.zeros((16, CHUNK), FULL)
                for k in range(vectors.shape[1] // CHUNK):
                    piece = jnp.broadcast_to(row[:, k * CHUNK : (k + 1) * CHUNK], (16, CHUNK))
                    value = jnp.where(deep == k, piece, value)
                last[position // half][position % half, 0, 0:16, :] = value.astype(LOW)

        return

    sums, vectors = scratch[-2:]

    @pl.when(step < chunks)
    def _():
        multiply()
        sums[pl.ds(step, 1), :] = sum(column_sum(right(m).astype(FULL)) for m in range(members))

    @pl.when(step == chunks)
    def _():
        own = vectors.shape[0]
        for k, first in enumerate(bias[0]):
            for team_row in range(own):
                chunk, lane = divmod(first + team_row * lines, CHUNK)
                vectors[team_row : team_row + 1, k * lines : (k + 1) * lines] = sums[
                    chunk : chunk + 1, lane : lane + lines
                ]
        wide = vectors.shape[1]
        for position in range(teams):
            local = block_at(position, order) - place_ref[1] * (teams // members) - bias[1]
            inside = jnp.logical_and(local >= 0, local < own)
            row = vectors[pl.ds(jnp.clip(local, 0, own - 1), 1), :]
            row = jnp.where(inside, row, 0.0)
            last[position // half][position % half, 0, 0:16, 0:wide] = jnp.broadcast_to(
                row, (16, wide)
            ).astype(LOW)


def weight_grad(name, lefts, flips, rights, places, teams, width, weights, bias=(), sums=(), mib=60):
    members = len(lefts)
    rows = rights[0][1][-2]
    flat = [item for member in lefts for item in member]
    high = sum(a.shape[1] for a, _ in lefts[0]) if flips else lefts[0][0][0].shape[0]
    lines = high // teams
    orders = part_orders(teams.bit_length() - 1)
    parts, start = [], 0
    for order, deep in zip(orders, part_depths(lines, weights)):
        if deep:
            parts.append((order, start, deep))
        start += deep
    half = teams // 2
    chunks = width // CHUNK
    own = bias[2] if bias else 0
    if sums:
        sums_wide = 6 * lines + sums[-1].shape[1] // teams
        sums_wide = -(-sums_wide // CHUNK) * CHUNK
    counts = [chunks] * len(parts)
    if bias or sums:
        counts[-1] += 1
    outs = pl.pallas_call(
        functools.partial(
            weight_kernel, [len(m) for m in lefts], flips, teams, lines, parts, members, bias, len(sums)
        ),
        grid_spec=pltpu.PrefetchScalarGridSpec(
            num_scalar_prefetch=1,
            grid=(counts[-1],),
            in_specs=[
                pl.BlockSpec(
                    (rows, array.shape[1]) if flips else array.shape, lambda i, s, b=block: (b, 0)
                )
                for array, block in flat
            ]
            + [
                pl.BlockSpec(shape, lambda i, s, f=index: f(jnp.minimum(i, chunks - 1), s))
                for _, shape, index in rights
            ]
            + [pl.BlockSpec(a.shape, lambda i, s: (0, 0)) for a in sums],
            out_specs=[
                pl.BlockSpec(
                    (half, 1, p[2], CHUNK), lambda i, s, c=c: (0, jnp.minimum(i, c - 1), 0, 0)
                )
                for p, c in zip(parts, counts)
                for _ in range(2)
            ],
            scratch_shapes=[pltpu.VMEM((high, rows), LOW)] * (members if flips else 0)
            + [pltpu.VMEM((high, CHUNK), LOW)]
            + (
                [pltpu.VMEM((chunks, CHUNK), FULL), pltpu.VMEM((own, len(bias[0]) * lines), FULL)]
                if bias
                else [pltpu.VMEM((teams, sums_wide), FULL)] if sums else []
            ),
        ),
        out_shape=[
            jax.ShapeDtypeStruct((half, c, p[2], CHUNK), LOW)
            for p, c in zip(parts, counts)
            for _ in range(2)
        ],
        compiler_params=params(mib),
        cost_estimate=CHEAP,
        name="weight_grad",
    )(places, *[array for array, _ in flat], *[array for array, _, _ in rights], *sums)
    made = []
    for k, (order, start, deep) in enumerate(parts):
        near, far = (o.reshape(half, counts[k] * deep, CHUNK) for o in outs[2 * k : 2 * k + 2])
        segments = [(name, start, deep, c) for c in range(chunks)]
        if counts[k] > chunks:
            segments.append(("bias", 0, deep, 0))
        made.append(dict(order=order, near=near, far=far, segments=segments))
    return made


def fold_kernel(counts, *refs):
    outs = refs[4 * sum(counts) :]
    spot = 0
    for k, count in enumerate(counts):
        start = 0
        for _ in range(count):
            near_low, near_high, came_low, came_high = refs[spot : spot + 4]
            deep = near_low.shape[1]
            rows = slice(start, start + deep)
            outs[2 * k][:, rows] = (near_low[...].astype(FULL) + came_low[...].astype(FULL)).astype(LOW)
            outs[2 * k + 1][:, rows] = (
                near_high[...].astype(FULL) + came_high[...].astype(FULL)
            ).astype(LOW)
            start, spot = start + deep, spot + 4


def fold(*groups, join=False):
    skip = 1 if join else 0
    merged = {}
    for group in groups:
        for part in group:
            key = str([o[skip:] for o in part["order"]])
            merged.setdefault(key, []).append(part)
    merged = list(merged.values())
    half = merged[0][0]["near"].shape[0] // 2
    operands, in_specs, out_specs, out_shape, counts = [], [], [], [], []
    for parts in merged:
        rows = 0
        for part in parts:
            deep = part["near"].shape[1]
            rows += deep
            low = pl.BlockSpec((1, deep, CHUNK), lambda i: (i, 0, 0))
            high = pl.BlockSpec((1, deep, CHUNK), lambda i: (half + i, 0, 0))
            operands += [part["near"], part["near"], part["came"], part["came"]]
            in_specs += [low, high, low, high]
        counts.append(len(parts))
        out_specs += [pl.BlockSpec((1, rows, CHUNK), lambda i: (i, 0, 0))] * 2
        out_shape += [jax.ShapeDtypeStruct((half, rows, CHUNK), LOW)] * 2
    outs = pl.pallas_call(
        functools.partial(fold_kernel, counts),
        grid=(half,),
        in_specs=in_specs,
        out_specs=out_specs,
        out_shape=out_shape,
        compiler_params=params(48 if len(operands) > 16 else 40),
        cost_estimate=CHEAP,
        name="fold",
    )(*operands)
    return [
        dict(
            order=tuple(o[1:] for o in parts[0]["order"]),
            near=outs[2 * k],
            far=outs[2 * k + 1],
            segments=[s for p in parts for s in p["segments"]],
        )
        for k, parts in enumerate(merged)
    ]


def final_kernel(layouts, plain, settled, size, lines, place_ref, *refs):
    count = len(layouts)
    outs = refs[2 * count :]
    targets = dict(zip(plain, outs))
    pieces = outs[len(plain) : len(plain) + size]
    if settled:
        targets[None] = outs[-1]
    biases = []
    for k, layout in enumerate(layouts):
        spot = 0
        for name, start, deep, column in layout:
            rows = slice(spot, spot + (16 if name == "bias" else deep))
            value = refs[2 * k][0, rows].astype(FULL) + refs[2 * k + 1][0, rows].astype(FULL)
            spot += deep
            if name == "bias":
                biases.append(value[0:8])
                continue
            targets[name][start : start + deep, column * CHUNK : (column + 1) * CHUNK] = value
    if settled:
        for piece in pieces if biases else ():
            piece[lines : lines + 8, 0:CHUNK] = sum(biases)
        for k in range(size):
            line = pl.multiple_of((place_ref[1] ^ k) * lines, 8)
            pieces[k][0:lines, :] = targets[None][pl.ds(line, lines), :]


def final(parts, places, size, lines, plain, settled):
    layouts, wide, more = [], 0, 0
    for part in parts:
        layout = []
        for name, start, deep, column in part["segments"]:
            if name in plain or name == "bias":
                more = 8 if name == "bias" else more
                layout.append((name, start, deep, column))
            else:
                column += settled[name] // CHUNK
                wide = max(wide, (column + 1) * CHUNK)
                layout.append((None, start, deep, column))
        layouts.append(layout)
    names = list(plain)
    shapes = [jax.ShapeDtypeStruct(plain[n], FULL) for n in names]
    if settled:
        shapes += [jax.ShapeDtypeStruct((lines + more, wide), FULL)] * size
    outs = pl.pallas_call(
        functools.partial(final_kernel, layouts, names, bool(settled), size, lines),
        in_specs=[pl.BlockSpec(memory_space=pltpu.SMEM)]
        + [pl.BlockSpec(memory_space=pltpu.VMEM)] * (2 * len(parts)),
        out_specs=[pl.BlockSpec(memory_space=pltpu.VMEM)] * len(shapes),
        out_shape=shapes,
        scratch_shapes=[pltpu.VMEM((size * lines, wide), FULL)] if settled else [],
        compiler_params=params(32),
        cost_estimate=CHEAP,
        name="final",
    )(places, *[p[n] for p in parts for n in ("near", "came")])
    return dict(zip(names, outs)), outs[len(names) :]


def tie(value, *others):
    return lax.optimization_barrier((value, others))[0]


def per_device(
    inputs,
    mask_pos,
    mask_count,
    replace,
    cotangent,
    query_weight,
    query_bias,
    key_weight,
    value_weight,
    value_bias,
    out_weight,
    out_bias,
    first_gain,
    first_shift,
    inner_weight,
    inner_bias,
    outer_weight,
    outer_bias,
    second_gain,
    second_shift,
):
    groups, rows, width = inputs.shape
    hidden = inner_weight.shape[1]
    blocks = lax.axis_size("blk")
    number = lax.axis_size("dp") * blocks
    size = blocks // groups
    piece = rows // size
    own_rows = blocks * piece
    teams = number // size
    bits = teams.bit_length() - 1
    place = lax.axis_index("blk")
    flat = lax.axis_index("dp") * blocks + place
    sequence = place // size
    rank = place % size
    team = flat // size
    share = width // size
    hidden_share = hidden // size
    others = range(1, size)

    def hop(array, mask):
        return lax.ppermute(array, BOTH, [(i, i ^ mask) for i in range(number)])

    def cut(array, who, count, axis):
        return lax.dynamic_slice_in_dim(array, who * count, count, axis=axis)

    def swap(make):
        return [make(rank)] + [hop(make(rank ^ k), k) for k in others]

    def absolute(pieces, axis):
        if size == 2:
            first = rank == 0
            return jnp.concatenate(
                [jnp.where(first, pieces[0], pieces[1]), jnp.where(first, pieces[1], pieces[0])],
                axis=axis,
            )
        stacked = jnp.stack(pieces)
        return jnp.concatenate(
            [lax.dynamic_index_in_dim(stacked, q ^ rank, 0, keepdims=False) for q in range(size)],
            axis=axis,
        )

    def send(parts):
        return [
            dict(
                p,
                came=lax.ppermute(
                    p["far"],
                    BOTH,
                    [(i, i ^ (size << p["order"][i % size % 2][0])) for i in range(number)],
                ),
            )
            for p in parts
        ]

    def far(parts):
        return [p["far"] for p in parts]

    def sync(values, *groups):
        values, came = lax.optimization_barrier((values, [[p["came"] for p in g] for g in groups]))
        made = [[dict(p, came=c) for p, c in zip(g, cs)] for g, cs in zip(groups, came)]
        return (values, *made)

    def after(parts, *values):
        came = lax.optimization_barrier(([p["came"] for p in parts], values))[0]
        return [dict(p, came=c) for p, c in zip(parts, came)]

    arrived = lax.all_to_all(inputs.reshape(blocks, piece, width), "blk", 0, 0)
    lane = jnp.arange(own_rows, dtype=jnp.int32)
    positions = (lane // piece) * rows + rank * piece + lane % piece
    swapped, seeded, masked = masked_rows(
        sequence.reshape(1).astype(jnp.int32), mask_count, positions.reshape(-1, 1), mask_pos, replace, cotangent
    )
    places = jnp.stack([team, rank]).astype(jnp.int32)
    heads_weight = jnp.concatenate(
        [cut(w, rank, share, 1) for w in (query_weight, key_weight, value_weight)], axis=1
    )
    heads_bias = jnp.concatenate(
        [
            cut(query_bias, rank, share, 0),
            jnp.zeros((share,), LOW),
            cut(value_bias, rank, share, 0),
        ]
    )
    out_weights = [cut(out_weight, rank ^ k, share, 0) for k in range(size)]

    small = (out_bias, first_gain, first_shift, outer_bias, second_gain, second_shift)
    small = jnp.stack(small).astype(FULL).reshape(-1, 1, width)
    inner_line = inner_bias.reshape(1, -1)
    arrived = tie(arrived, small, inner_line, swapped, seeded, heads_weight, heads_bias, out_weights, masked)
    current = jnp.where(masked > 0.0, swapped, arrived.reshape(own_rows, width))
    currents = [current] + [hop(current, k) for k in others]
    joined = product(jnp.concatenate(currents, axis=0), heads_weight) + heads_bias.astype(FULL)
    joined = joined.astype(LOW)
    mixed_heads, log_total = attention_forward(joined)

    mixed_parts = mixed_heads.reshape(size, own_rows, share)
    mixed_here = [mixed_parts[0]] + [hop(mixed_parts[k], k) for k in others]
    mixed_away = []
    for k in others:
        row = []
        for q in range(size):
            if q == 0:
                row.append((mixed_heads, k))
            else:
                row.append((hop(mixed_parts[k ^ q], q), 0))
        mixed_away.append(row)

    first, first_flip, first_low, unit_one, factor_one = first_half(
        current,
        [(m, share) for m in [mixed_heads] + mixed_here[1:]],
        out_weights,
        small,
    )
    firsts = [first_flip] + [hop(first_flip, k) for k in others]
    fed = feed_forward(
        places, size, number, first_low, first, seeded, inner_weight, inner_line, outer_weight, small
    )
    actives = [fed[0]] + [hop(fed[k], k) for k in others]
    slope, result, grad_two, grad_two_low, second_sums = fed[size:]

    def home(array):
        return lax.all_to_all(array.reshape(blocks, piece, width), "blk", 0, 0)

    def wide(array):
        return array.reshape(groups, rows, width).astype(FULL)

    grad_twos = [grad_two_low] + [hop(grad_two_low, k) for k in others]

    def plain(array):
        return (array, (own_rows, CHUNK), lambda i, s: (0, i))

    layer_out = home(result)
    back = feed_back(
        places, size, grad_two_low, grad_two, slope, inner_weight, outer_weight, unit_one, factor_one,
        small, out_weights,
    )
    back, layer_out, grad_twos, actives = lax.optimization_barrier((back, layer_out, grad_twos, actives))
    layer_out = wide(layer_out)
    grad_inners = [back[0]] + [hop(back[k], k) for k in others]
    inner_bias_grad, grad_one, grad_one_low, first_sums = back[size : size + 4]
    grad_ones = [back[size + 4]] + [hop(back[size + 4 + k], k) for k in others]
    grad_mixed = back[2 * size + 4 : 3 * size + 4]
    grad_mixed = [grad_mixed[0]] + [hop(grad_mixed[k], k) for k in others]
    outer_parts = weight_grad(
        "outer", [[(a, 0)] for a in actives], False, [plain(g) for g in grad_twos], places, teams, width,
        (2, 1),
    )
    grad_ones[0] = tie(grad_ones[0], far(outer_parts))
    outer_parts = send(outer_parts)
    out_parts = weight_grad(
        "out", [[(m, 0) for m in [mixed_heads] + mixed_here[1:]]] + mixed_away, True,
        [plain(g) for g in grad_ones],
        jnp.stack([team ^ (rank * (teams // size)), rank]).astype(jnp.int32), teams, share, (1, 0),
    )
    grad_inners[0] = tie(grad_inners[0], far(out_parts))
    out_parts = send(out_parts)
    inner_parts = weight_grad(
        "inner", [[(f, 0)] for f in firsts], False, [plain(g) for g in grad_inners], places, teams,
        hidden_share, (3, 1), sums=(first_sums, second_sums, inner_bias_grad),
    )
    fars, outer_parts = sync(far(inner_parts), outer_parts)
    inner_parts = send([dict(p, far=f) for p, f in zip(inner_parts, fars)])
    grad_mixed[0] = tie(grad_mixed[0], fars)

    pairs = share // (2 * HEAD)
    number_of = 2 if share // 2 % CHUNK == 0 else 1
    count = pairs // number_of
    part = share // number_of
    chunks = part // CHUNK
    team_rows = teams // size // number_of

    def three_grad(three, group):
        return weight_grad(
            f"three{group}", [[(c, 0)] for c in currents], True,
            [
                (
                    three,
                    (1, own_rows, CHUNK),
                    lambda i, s, k=k: (i // chunks, k, group * chunks + i % chunks),
                )
                for k in range(size)
            ],
            places, teams, 3 * part, (3, 1), ((0, 2 * part), group * team_rows, team_rows), mib=40,
        )

    three = attention_backward(joined, grad_mixed, mixed_heads, log_total, 0, count)
    late = []
    if number_of == 2:
        late = three_grad(three, 0)
        three = tie(three, far(late))
        late = send(late)
    three, inner_parts, out_parts = sync(three, inner_parts, out_parts)
    early = fold(outer_parts, inner_parts, out_parts)
    three = tie(three, far(early))
    early = send(early)
    if number_of == 2:
        three = attention_backward(joined, grad_mixed, mixed_heads, log_total, count, count, three)
    three, early, late = sync(three, early, late)
    early = fold(early)
    three = tie(three, far(early))
    threes = [three] + [hop(three[:, k * own_rows : (k + 1) * own_rows], k) for k in others]
    early = send(early)
    more = three_grad(three, number_of - 1)
    (threes, fars), early = sync((threes, far(more)), early)
    more = send([dict(p, far=f) for p, f in zip(more, fars)])
    early = fold(early)
    threes[0] = tie(threes[0], far(early))
    early_one, early_two = send(early[:1]), early[1:]
    input_grad = input_back(places, threes, (query_weight, key_weight, value_weight), grad_one, masked)
    home_grad = home(input_grad)
    _, more, early_one = sync((input_grad, layer_out), more, early_one)
    late = fold(late, more) if late else fold(more)
    for p, f in zip(early_two, tie(far(early_two), far(late))):
        p["far"] = f
    late, early_two = send(late), send(early_two)
    while len((early_one + early_two)[0]["order"][0]) > 1:
        early_one, early_two = send(fold(early_one + early_two)), []

    lines = width // number
    _, late, early_two = sync(far(late), late, early_two)
    if len(late[0]["order"][0]) > 1:
        late = fold(late)
        early_one = [dict(p, near=tie(p["near"], far(late))) for p in early_one]
        home_grad = tie(home_grad, far(late))
        late = send(late)
    made, early = final(
        early_one + early_two, places, size, lines, {"outer": (hidden // number, width)},
        {"inner": 0, "out": hidden_share},
    )
    outer_weight_grad = made["outer"]
    early_away = [hop(early[k], k) for k in others]
    input_grad = wide(home_grad)
    late = after(late, input_grad, outer_weight_grad)
    while len(late[0]["order"][0]) > 1:
        late = fold(late, join=len(late[0]["order"][0]) == 2)
        early_away = tie(early_away, far(late))
        late = send(late)
    early = [early[0]] + early_away
    inner_weight_grad = absolute([e[:lines, :hidden_share] for e in early], 1)
    out_weight_grad = absolute([e[:lines, hidden_share:] for e in early], 1)
    team_lines, team_hidden = width // teams, hidden // teams
    flat_rows = -(-(6 * team_lines + team_hidden) // CHUNK)
    flat = sum(e[lines : lines + flat_rows, :CHUNK] for e in early).reshape(1, -1)
    six = cut(flat[:, : 6 * team_lines].reshape(6, team_lines), rank, lines, 1)
    inner_bias_grad = cut(
        flat[:, 6 * team_lines : 6 * team_lines + team_hidden], rank, team_hidden // size, 1
    )
    _, late = final(
        after(late, inner_weight_grad, out_weight_grad), places, size, lines, {},
        {f"three{g}": g * 3 * part for g in range(number_of)},
    )
    late = [late[0]] + [hop(late[k], k) for k in others]

    def three_columns(e, k):
        cuts = [
            e[:lines, (g * 3 + k) * part : (g * 3 + k + 1) * part] for g in range(number_of)
        ]
        return jnp.concatenate(cuts, axis=1)

    three_grads = [absolute([three_columns(e, k) for e in late], 1) for k in range(3)]
    biases = sum(e[lines, : 2 * team_lines] for e in late).reshape(2, team_lines)
    biases = cut(biases, rank, lines, 1)
    spots = [biases[0], biases[1], six[2], six[0], six[1], inner_bias_grad[0], six[5], six[3], six[4]]

    return (
        layer_out,
        input_grad,
        three_grads[0],
        spots[0],
        three_grads[1],
        three_grads[2],
        spots[1],
        out_weight_grad,
        spots[2],
        spots[3],
        spots[4],
        inner_weight_grad,
        spots[5],
        outer_weight_grad,
        spots[6],
        spots[7],
        spots[8],
    )


def solution(mesh):
    split = P("dp", "blk", None)
    row = P("dp")
    both = P(BOTH)
    in_specs = (split, row, row, row, row) + (P(),) * 15
    out_specs = (split, split) + (both,) * 15
    return jax.shard_map(
        per_device, mesh=mesh, in_specs=in_specs, out_specs=out_specs, check_vma=False
    )
```
